32 devices in a mesh: fsdp: 4 (over y, x), context: 2 (over core), tensor: 4 (over z).
Axes of the slice: x: 2, y: 2, z: 4, core: 2. Of those that a mesh axis runs over, the one named last changes fastest.
Arguments:
- inputs: bfloat16 [4, 1024, 2048], P('fsdp', 'context'), may hold values from -6 to 6
- lengths: int32 [4], P('fsdp'), may hold values from 256 to 1024, as said below
- norm_attn: bfloat16 [2048], P('fsdp'), may hold values from 0.099609375 to 1.8984375
- w_query: bfloat16 [2048, 2048], P('fsdp', 'tensor'), may hold values from -0.125 to 0.125
- w_key: bfloat16 [2048, 2048], P('fsdp', 'tensor'), may hold values from -0.125 to 0.125
- w_value: bfloat16 [2048, 4096], P('fsdp', 'tensor'), may hold values from -0.125 to 0.125
- w_decay: bfloat16 [2048, 16], P('fsdp', 'tensor'), may hold values from -0.25 to 0.25
- w_strength: bfloat16 [2048, 16], P('fsdp', 'tensor'), may hold values from -0.125 to 0.125
- decay_log: bfloat16 [16], P('tensor'), may hold values from -1.5 to 1
- decay_bias: bfloat16 [16], P('tensor'), may hold values from -9 to -2
- conv_query: bfloat16 [16, 4, 128], P('tensor', None, 'fsdp'), may hold values from -3 to 3
- conv_key: bfloat16 [16, 4, 128], P('tensor', None, 'fsdp'), may hold values from -3 to 3
- conv_value: bfloat16 [16, 4, 256], P('tensor', None, 'fsdp'), may hold values from -3 to 3
- w_outgate: bfloat16 [2048, 4096], P('fsdp', 'tensor'), may hold values from -0.125 to 0.125
- norm_head: bfloat16 [256], P('fsdp'), may hold values from 0.099609375 to 1.8984375
- w_out: bfloat16 [4096, 2048], P('tensor', 'fsdp'), may hold values from -0.125 to 0.125
- norm_mlp: bfloat16 [2048], P('fsdp'), may hold values from 0.099609375 to 1.8984375
- w_gate: bfloat16 [2048, 5632], P('fsdp', 'tensor'), may hold values from -0.125 to 0.125
- w_up: bfloat16 [2048, 5632], P('fsdp', 'tensor'), may hold values from -0.125 to 0.125
- w_down: bfloat16 [5632, 2048], P('tensor', 'fsdp'), may hold values from -0.109375 to 0.109375
- cotangent: bfloat16 [4, 1024, 2048], P('fsdp', 'context'), may hold values from -6 to 6
Outputs:
- output: bfloat16 [4, 1024, 2048], P('fsdp', 'context')
- input_grad: bfloat16 [4, 1024, 2048], P('fsdp', 'context')
- grad_norm_attn: float32 [2048], P('fsdp')
- grad_w_query: float32 [2048, 2048], P('fsdp', 'tensor')
- grad_w_key: float32 [2048, 2048], P('fsdp', 'tensor')
- grad_w_value: float32 [2048, 4096], P('fsdp', 'tensor')
- grad_w_decay: float32 [2048, 16], P('fsdp', 'tensor')
- grad_w_strength: float32 [2048, 16], P('fsdp', 'tensor')
- grad_decay_log: float32 [16], P('tensor')
- grad_decay_bias: float32 [16], P('tensor')
- grad_conv_query: float32 [16, 4, 128], P('tensor', None, 'fsdp')
- grad_conv_key: float32 [16, 4, 128], P('tensor', None, 'fsdp')
- grad_conv_value: float32 [16, 4, 256], P('tensor', None, 'fsdp')
- grad_w_outgate: float32 [2048, 4096], P('fsdp', 'tensor')
- grad_norm_head: float32 [256], P('fsdp')
- grad_w_out: float32 [4096, 2048], P('tensor', 'fsdp')
- grad_norm_mlp: float32 [2048], P('fsdp')
- grad_w_gate: float32 [2048, 5632], P('fsdp', 'tensor')
- grad_w_up: float32 [2048, 5632], P('fsdp', 'tensor')
- grad_w_down: float32 [5632, 2048], P('tensor', 'fsdp')
The draws below stay inside these ranges and needn't reach their ends.
Inputs may be any that keep to these rules, and one draw needn't show every extreme that they name: Slot s holds one sequence that fills its first lengths[s] positions; the rest of the slot is padding. In every draw at least one slot is full (1024 positions).
All inputs are finite; a program needn't handle non-finite values.
Results may differ from the reference program's by a relative error of at most 0.033.
Values may be sent and summed in bfloat16 or wider, within the bound.
No kernel may reach another device: no remote copies, remote signals or barrier semaphores. Data moves between devices by JAX's collectives and lax.ppermute only.
A program may use at most 256 MiB of HBM per device.

```python
import jax
import jax.numpy as jnp
from jax import lax

D = 2048
FF = 5632
H = 16
DK = 128
DV = 256
KERNEL = 4
BLOCK = 64
SLOT = 1024
SLOTS = 4
MIN_LEN = 256


def draw_lengths(key, part):
    first_key = jax.random.fold_in(key, 11)
    second_key = jax.random.fold_in(key, 23)
    drawn = jax.random.randint(first_key, (SLOTS,), MIN_LEN, SLOT + 1)
    chosen = jax.random.randint(second_key, (), 0, SLOTS)
    slot_ids = jnp.arange(SLOTS, dtype=jnp.int32)
    return jnp.where(slot_ids == chosen, SLOT, drawn).astype(jnp.int32)


def shard_levels(rng, extent, cuts, least, high):
    level = 1.0
    for position, shards_of in cuts:
        draws = jax.random.uniform(jax.random.fold_in(jax.random.fold_in(rng, 6), position), (shards_of,), jnp.float32, least / len(cuts), high / len(cuts))
        level = level * jnp.repeat(jnp.exp(draws), extent[position] // shards_of).reshape((-1,) + (1,) * (len(extent) - 1 - position))
    return level


def bell_draw(own_key, shape, width, most, split=(), kind=jnp.bfloat16):
    level = shard_levels(own_key, shape, split, -0.22, 0.18) if split else 1.0
    values = jax.random.normal(own_key, shape, jnp.float32) * width * level
    return jnp.minimum(jnp.maximum(values, -most), most).astype(kind)


def setup_inputs(seed: int = 0) -> dict:
    streams_of = jax.random.split(jax.random.key(seed), 22)
    return {
        "inputs": bell_draw(streams_of[0], (SLOTS, SLOT, D), 1.0, 6.0, ((0, 4), (1, 2))),
        "lengths": draw_lengths(jax.random.fold_in(streams_of[21], 71), 0),
        "norm_attn": jnp.clip(1.0 + 0.18 * jax.random.normal(streams_of[2], (D,), jnp.float32), 0.099609375, 1.8984375).astype(jnp.bfloat16),
        "w_query": bell_draw(streams_of[3], (D, H * DK), D ** -0.5, 0.125, ((0, 4), (1, 4))),
        "w_key": bell_draw(streams_of[4], (D, H * DK), D ** -0.5, 0.125, ((0, 4), (1, 4))),
        "w_value": bell_draw(streams_of[5], (D, H * DV), D ** -0.5, 0.125, ((0, 4), (1, 4))),
        "w_decay": bell_draw(streams_of[6], (D, H), (D // 4) ** -0.5, 0.25, ((0, 4), (1, 4))),
        "w_strength": bell_draw(streams_of[7], (D, H), D ** -0.5, 0.125, ((0, 4), (1, 4))),
        "decay_log": jnp.clip(-1.5 + 2.5 * jax.random.uniform(streams_of[8], (H,), jnp.float32) ** shard_levels(streams_of[8], (H,), ((0, 4),), -0.2, 0.2), -1.5, 1.0).astype(jnp.bfloat16),
        "decay_bias": jnp.clip(-9.0 + 7.0 * jax.random.uniform(streams_of[9], (H,), jnp.float32) ** shard_levels(streams_of[9], (H,), ((0, 4),), -0.2, 0.2), -9.0, -2.0).astype(jnp.bfloat16),
        "conv_query": bell_draw(streams_of[10], (H, KERNEL, DK), 0.5, 3.0, ((0, 4), (2, 4))),
        "conv_key": bell_draw(streams_of[11], (H, KERNEL, DK), 0.5, 3.0, ((0, 4), (2, 4))),
        "conv_value": bell_draw(streams_of[12], (H, KERNEL, DV), 0.5, 3.0, ((0, 4), (2, 4))),
        "w_outgate": bell_draw(streams_of[13], (D, H * DV), D ** -0.5, 0.125, ((0, 4), (1, 4))),
        "norm_head": jnp.clip(1.0 + 0.18 * jax.random.normal(streams_of[14], (DV,), jnp.float32), 0.099609375, 1.8984375).astype(jnp.bfloat16),
        "w_out": bell_draw(streams_of[15], (H * DV, D), (H * DV // 2) ** -0.5, 0.125, ((0, 4), (1, 4))),
        "norm_mlp": jnp.clip(1.0 + 0.18 * jax.random.normal(streams_of[16], (D,), jnp.float32), 0.099609375, 1.8984375).astype(jnp.bfloat16),
        "w_gate": bell_draw(streams_of[17], (D, FF), D ** -0.5, 0.125, ((0, 4), (1, 4))),
        "w_up": bell_draw(streams_of[18], (D, FF), D ** -0.5, 0.125, ((0, 4), (1, 4))),
        "w_down": bell_draw(streams_of[19], (FF, D), (FF // 2) ** -0.5, 0.109375, ((0, 4), (1, 4))),
        "cotangent": bell_draw(streams_of[20], (SLOTS, SLOT, D), 1.0, 6.0, ((0, 4), (1, 2))),
    }


exact = lax.Precision.HIGHEST

@jax.custom_vjp
def low(v):
    return lax.optimization_barrier(v.astype(jnp.bfloat16)).astype(jnp.float32)

@jax.custom_vjp
def low_back(v):
    return v

def low_keep(v):
    return (low(v), None)

def low_pass(kept, grad):
    return (grad,)

def back_keep(v):
    return (v, None)

def back_low(kept, grad):
    return (low(grad),)
low.defvjp(low_keep, low_pass)
low_back.defvjp(back_keep, back_low)

def rms_scale(values, gain, epsilon):
    return values * lax.rsqrt(lax.optimization_barrier(jnp.mean(values * values, -1, keepdims=True)) + epsilon) * gain

def unit_rows(values):
    return values * lax.rsqrt(lax.optimization_barrier(jnp.sum(values * values, -1, keepdims=True)) + 1e-06)

def block_step(carried, query, keys, values, strength, logdecay):
    length = query.shape[-2]
    key_dim = query.shape[-1]
    row_ids = lax.broadcasted_iota(jnp.int32, (length, length), 0)
    col_ids = lax.broadcasted_iota(jnp.int32, (length, length), 1)
    causal = row_ids >= col_ids
    strict = row_ids > col_ids
    triangle = causal.astype(jnp.float32)
    running = jnp.einsum('ij,...j->...i', triangle, logdecay, precision=exact)
    decays = jnp.exp(running)
    spread = running[..., :, None] - running[..., None, :]
    ratios = jnp.where(causal, jnp.exp(jnp.where(causal, spread, 0.0)), 0.0)
    key_dots = jnp.einsum('...id,...jd->...ij', keys, keys, precision=exact)
    system = jnp.where(strict, strength[..., :, None] * key_dots * ratios, 0.0) + jnp.eye(length, dtype=jnp.float32)
    targets = jnp.concatenate([(strength * decays)[..., None] * keys, strength[..., None] * values], -1)
    solved = lax.linalg.triangular_solve(system, targets, left_side=True, lower=True, unit_diagonal=True)
    updates = solved[..., key_dim:] - jnp.einsum('...cd,...dw->...cw', solved[..., :key_dim], carried, precision=exact)
    remains = jnp.exp(running[..., -1:] - running)
    new_state = decays[..., -1:, None] * carried + jnp.einsum('...cd,...cw->...dw', keys * remains[..., None], updates, precision=exact)
    scores = jnp.einsum('...id,...jd->...ij', query, keys, precision=exact) * ratios
    result = jnp.einsum('...cd,...dw->...cw', query * decays[..., None], carried, precision=exact)
    result = result + jnp.einsum('...ij,...jw->...iw', scores, updates, precision=exact)
    return (new_state, result)

def delta_rule(query, keys, values, strength, logdecay):
    head_count, length = (query.shape[0], query.shape[1])
    block_count = length // BLOCK

    def split_up(array):
        return jnp.moveaxis(array.reshape((head_count, block_count, BLOCK) + array.shape[2:]), 1, 0)

    def advance(carried, pieces):
        return block_step(carried, *pieces)
    start = jnp.zeros((head_count, query.shape[-1], values.shape[-1]), jnp.float32)
    last_state, results = lax.scan(jax.checkpoint(advance), start, (split_up(query), split_up(keys), split_up(values), split_up(strength), split_up(logdecay)))
    return jnp.moveaxis(results, 0, 1).reshape(head_count, length, values.shape[-1])

def convolve(pre_mix, taps_w):
    taps = jnp.transpose(taps_w, (1, 0, 2)).reshape(KERNEL, -1)
    length = pre_mix.shape[0]
    padded = jnp.pad(pre_mix, ((KERNEL - 1, 0), (0, 0)))
    summed = jnp.zeros_like(pre_mix)
    for shift_at in range(KERNEL):
        summed = summed + taps[shift_at] * padded[shift_at:shift_at + length]
    return jax.nn.silu(summed)

def layer(tokens, live_mask, params):
    norm_attn, w_query, w_key, w_value, w_decay, w_strength, decay_log, decay_bias, conv_query, conv_key, conv_value, w_outgate, norm_head, w_out, norm_mlp, w_gate, w_up, w_down = params
    length = tokens.shape[0]
    normed = low(rms_scale(tokens, norm_attn, 1e-06))

    def project(matrix):
        return jnp.dot(normed, matrix, precision=exact)
    pre_query = low_back(low(project(w_query)))
    pre_key = low_back(low(project(w_key)))
    pre_value = low_back(low(project(w_value)))
    gate_pre = low_back(project(w_outgate))
    decay_pre = project(w_decay)
    strength_pre = project(w_strength)
    act_query = convolve(pre_query, conv_query).reshape(length, H, DK)
    act_key = convolve(pre_key, conv_key).reshape(length, H, DK)
    act_value = convolve(pre_value, conv_value).reshape(length, H, DV)
    query = unit_rows(act_query) * DK ** (-0.5)
    keys = unit_rows(act_key)
    strength = jax.nn.sigmoid(strength_pre)
    logdecay = -jnp.exp(decay_log) * jax.nn.softplus(decay_pre + decay_bias)
    mixed = delta_rule(jnp.transpose(query, (1, 0, 2)), jnp.transpose(keys, (1, 0, 2)), jnp.transpose(act_value, (1, 0, 2)), strength.T, logdecay.T)
    mixed = jnp.transpose(mixed, (1, 0, 2))
    gated = rms_scale(mixed, norm_head, 1e-05) * jax.nn.silu(gate_pre.reshape(length, H, DV))
    heads_out = low(gated.reshape(length, H * DV))
    attn = low_back(jnp.dot(heads_out, w_out, precision=exact))
    middle = tokens + live_mask[:, None] * attn
    hidden_in = low(rms_scale(middle, norm_mlp, 1e-06))
    gate_mlp = low_back(jnp.dot(hidden_in, w_gate, precision=exact))
    up_mlp = low_back(jnp.dot(hidden_in, w_up, precision=exact))
    act_mlp = low(jax.nn.silu(gate_mlp) * up_mlp)
    branch = low_back(jnp.dot(act_mlp, w_down, precision=exact))
    return middle + live_mask[:, None] * branch

def reference(inputs, lengths, norm_attn, w_query, w_key, w_value, w_decay, w_strength, decay_log, decay_bias, conv_query, conv_key, conv_value, w_outgate, norm_head, w_out, norm_mlp, w_gate, w_up, w_down, cotangent):
    params = tuple((weight.astype(jnp.float32) for weight in (norm_attn, w_query, w_key, w_value, w_decay, w_strength, decay_log, decay_bias, conv_query, conv_key, conv_value, w_outgate, norm_head, w_out, norm_mlp, w_gate, w_up, w_down)))
    places = lax.broadcasted_iota(jnp.int32, (SLOTS, SLOT), 1)
    masks = (places < lengths[:, None]).astype(jnp.float32)

    def whole(tokens, weights):

        def one_slot(slot_pair):
            return jax.checkpoint(layer)(slot_pair[0], slot_pair[1], weights)
        return lax.map(one_slot, (tokens, masks))
    output, pullback = jax.vjp(whole, inputs.astype(jnp.float32), params)
    input_grad, grads = pullback(cotangent.astype(jnp.float32))
    return (output.astype(jnp.bfloat16), input_grad.astype(jnp.bfloat16), grads[0], grads[1], grads[2], grads[3], grads[4], grads[5], grads[6], grads[7], grads[8], grads[9], grads[10], grads[11], grads[12], grads[13], grads[14], grads[15], grads[16], grads[17])
```

```python
import functools
import jax
import jax.numpy as jnp
from jax import lax
from jax.experimental import pallas as pl
from jax.experimental.pallas import tpu as pltpu
from jax.sharding import PartitionSpec as P

F32 = jnp.float32
BF16 = jnp.bfloat16
CHUNK = 128
exact = lax.Precision.HIGHEST
NN = ((1,), (0,))
NT = ((1,), (1,))
TN = ((0,), (0,))


def mm(a, b, dims=NN):
    return lax.dot_general(
        a.astype(BF16), b.astype(BF16), (dims, ((), ())), preferred_element_type=F32
    )


def mm_exact(a, b, dims=NN):
    return lax.dot_general(a, b, (dims, ((), ())), precision=exact, preferred_element_type=F32)


def grid_ids(size):
    rows = lax.broadcasted_iota(jnp.int32, (size, size), 0)
    cols = lax.broadcasted_iota(jnp.int32, (size, size), 1)
    return rows, cols


def softplus(v):
    return jnp.maximum(v, 0.0) + jnp.log1p(jnp.exp(-jnp.abs(v)))


def rates_of(rates, params, heads, triangle):
    lanes = lax.broadcasted_iota(jnp.int32, rates.shape, 1)
    shifted = rates + params[1:2, :]
    scale = jnp.exp(params[0:1, :])
    logdecay = jnp.where(lanes < heads, -scale * softplus(shifted), 0.0)
    running = mm_exact(triangle, logdecay)
    last = running[CHUNK - 1 : CHUNK, :]
    return (
        jax.nn.sigmoid(rates),
        shifted,
        scale,
        logdecay,
        running,
        jnp.transpose(running),
        jnp.exp(running),
        jnp.exp(last - running),
        jnp.exp(last),
    )


def inverse_of(system, rows, cols):
    eye = (rows == cols).astype(F32)
    size = 8
    near = jnp.where(rows // size == cols // size, system, 0.0)
    second = mm(near, near)
    third = mm(second, near)
    fourth = mm(second, second)
    partial = eye - near + second - third
    result = partial + mm(partial, fourth)
    while size < CHUNK:
        off = jnp.where(
            (rows // (2 * size) == cols // (2 * size)) & (rows // size > cols // size), system, 0.0
        )
        result = result - mm(mm(result, off), result)
        size *= 2
    return result


def refined(system, first, rows, cols):
    eye = (rows == cols).astype(F32)
    high = system.astype(BF16)
    low = system - high.astype(F32)
    first_high = first.astype(BF16)
    first_low = first - first_high.astype(F32)
    product = first + mm(high, first_high) + mm(low, first_high) + mm(high, first_low)
    return first + mm(first, eye - product)


def convolved(window, taps, rows):
    total = taps[0:1, :] * window[5 : 5 + rows, :]
    for j in range(1, 4):
        total = total + taps[j : j + 1, :] * window[5 + j : 5 + j + rows, :]
    return total


def forward_kernel(
    heads, key_dim, val_dim, order_ref, pre_ref, taps_ref, params_ref,
    mixed_ref, states_ref, inverse_ref, new_ref, state, window,
):
    step = pl.program_id(0)
    wide = heads * key_dim

    @pl.when(step == 0)
    def _():
        state[...] = jnp.zeros_like(state)
        window[0:8, :] = jnp.zeros((8, window.shape[1]), F32)

    width = window.shape[1]
    current = pre_ref[:, :width].astype(BF16).astype(F32)
    window[8 : 8 + CHUNK, :] = current
    summed = convolved(window, taps_ref, CHUNK)
    window[0:8, :] = current[CHUNK - 8 :, :]
    active = summed * jax.nn.sigmoid(summed)
    rows, cols = grid_ids(CHUNK)
    causal = rows >= cols
    strict = rows > cols
    strengths, _, _, _, running, running_t, decays, remains, whole = rates_of(
        pre_ref[:, width:], params_ref, heads, causal.astype(F32)
    )
    for h in range(heads):
        q_act = active[:, h * key_dim : (h + 1) * key_dim]
        k_act = active[:, wide + h * key_dim : wide + (h + 1) * key_dim]
        values = active[:, 2 * wide + h * val_dim : 2 * wide + (h + 1) * val_dim]
        query = q_act * (
            lax.rsqrt(jnp.sum(q_act * q_act, -1, keepdims=True) + 1e-6) * key_dim ** -0.5
        )
        keys = k_act * lax.rsqrt(jnp.sum(k_act * k_act, -1, keepdims=True) + 1e-6)
        beta = strengths[:, heads + h : heads + h + 1]
        spread = running[:, h : h + 1] - running_t[h : h + 1, :]
        ratios = jnp.where(causal, jnp.exp(jnp.where(causal, spread, 0.0)), 0.0)
        decay = decays[:, h : h + 1]
        dots = mm(jnp.concatenate([keys, query], 0), keys, NT)
        system = jnp.where(strict, beta * dots[:CHUNK] * ratios, 0.0)
        scores = dots[CHUNK:] * ratios
        inverse = refined(system, inverse_of(system, rows, cols), rows, cols)
        solved = mm(inverse, jnp.concatenate([(beta * decay) * keys, beta * values], 1))
        begin = state[h * key_dim : (h + 1) * key_dim, :]
        begin_low = begin.astype(BF16)
        through = mm(jnp.concatenate([solved[:, :key_dim], query * decay], 0), begin_low)
        new = (solved[:, key_dim:] - through[:CHUNK]).astype(BF16)
        mixed_ref[:, h * val_dim : (h + 1) * val_dim] = through[CHUNK:] + mm(scores, new)
        state[h * key_dim : (h + 1) * key_dim, :] = whole[:, h : h + 1] * begin + mm(
            keys * remains[:, h : h + 1], new, TN
        )
        states_ref[h * key_dim : (h + 1) * key_dim, :] = begin_low
        inverse_ref[h * CHUNK : (h + 1) * CHUNK, :] = inverse.astype(BF16)
        new_ref[:, h * val_dim : (h + 1) * val_dim] = new


def backward_kernel(
    heads, key_dim, val_dim, order_ref, pre_ref, before_ref, taps_ref, params_ref,
    states_ref, inverse_ref, new_ref, mixed_ref, gates_ref, d_own_ref, d_other_ref, side_ref,
    gain_ref,
    d_pre_ref, d_taps_ref, d_params_ref, d_gain_ref,
    d_state, window, after,
):
    step = pl.program_id(0)
    chunks = pl.num_programs(0)
    wide = heads * key_dim

    @pl.when(step == 0)
    def _():
        d_state[...] = jnp.zeros_like(d_state)
        after[CHUNK : CHUNK + 8, :] = jnp.zeros((8, after.shape[1]), F32)
        d_taps_ref[...] = jnp.zeros_like(d_taps_ref)
        d_params_ref[...] = jnp.zeros_like(d_params_ref)
        d_gain_ref[...] = jnp.zeros_like(d_gain_ref)

    width = window.shape[1]
    window[8 : 8 + CHUNK, :] = pre_ref[:, :width].astype(BF16).astype(F32)
    before = before_ref[:, :width].astype(BF16).astype(F32)
    window[0:8, :] = jnp.where(step == chunks - 1, 0.0, before)
    summed = convolved(window, taps_ref, CHUNK)
    sigma = jax.nn.sigmoid(summed)
    active = summed * sigma
    slope = sigma * (1.0 + summed * (1.0 - sigma))
    rows, cols = grid_ids(CHUNK)
    causal = rows >= cols
    strict = rows > cols
    strengths, shifted, scale, logdecay, running, running_t, decays, remains, whole = rates_of(
        pre_ref[:, width:], params_ref, heads, causal.astype(F32)
    )
    lanes = lax.broadcasted_iota(jnp.int32, (CHUNK, 128), 1)
    row_ids = lax.broadcasted_iota(jnp.int32, (CHUNK, 1), 0)
    d_attn = jnp.where(
        order_ref[chunks - 1 - step] < chunks // 2, d_own_ref[...], d_other_ref[...]
    )
    depth = side_ref.shape[2]
    d_heads = mm(d_attn[:, :depth], side_ref[0, 1])
    for f in range(1, side_ref.shape[0]):
        d_heads = d_heads + mm(d_attn[:, f * depth : (f + 1) * depth], side_ref[f, 1])
    d_running = jnp.zeros((CHUNK, 128), F32)
    d_strengths = jnp.zeros((CHUNK, 128), F32)
    for h in range(heads):
        q_at = slice(h * key_dim, (h + 1) * key_dim)
        k_at = slice(wide + h * key_dim, wide + (h + 1) * key_dim)
        v_at = slice(2 * wide + h * val_dim, 2 * wide + (h + 1) * val_dim)
        o_at = slice(h * val_dim, (h + 1) * val_dim)
        s_at = slice(h * key_dim, (h + 1) * key_dim)
        q_act = active[:, q_at]
        k_act = active[:, k_at]
        values = active[:, v_at]
        q_scale = lax.rsqrt(jnp.sum(q_act * q_act, -1, keepdims=True) + 1e-6)
        k_scale = lax.rsqrt(jnp.sum(k_act * k_act, -1, keepdims=True) + 1e-6)
        q_unit = q_act * q_scale
        keys = k_act * k_scale
        query = q_unit * key_dim ** -0.5
        mixed = mixed_ref[:, o_at]
        gates = gates_ref[:, o_at]
        d_out = d_heads[:, o_at]
        gain = gain_ref[...]
        m_scale = lax.rsqrt(jnp.mean(mixed * mixed, -1, keepdims=True) + 1e-5)
        unit = mixed * m_scale
        g_sigma = jax.nn.sigmoid(gates)
        gated = gates * g_sigma
        weighted = d_out * unit
        d_pre_ref[:, width + 128 + h * val_dim : width + 128 + (h + 1) * val_dim] = (
            weighted * gain * (g_sigma * (1.0 + gates * (1.0 - g_sigma)))
        ).astype(BF16)
        d_gain_ref[0:1, :] += jnp.sum(weighted * gated, 0, keepdims=True)
        d_unit = d_out * gated * gain
        d_mixed = (m_scale * (d_unit - unit * jnp.mean(d_unit * unit, -1, keepdims=True))).astype(
            BF16
        )
        beta = strengths[:, heads + h : heads + h + 1]
        spread = running[:, h : h + 1] - running_t[h : h + 1, :]
        ratios = jnp.where(causal, jnp.exp(jnp.where(causal, spread, 0.0)), 0.0)
        decay = decays[:, h : h + 1]
        remain = remains[:, h : h + 1]
        keys_low = keys.astype(BF16)
        query_low = query.astype(BF16)
        dots = mm(jnp.concatenate([keys_low, query_low], 0), keys_low, NT)
        weights = jnp.where(strict, dots[:CHUNK] * ratios, 0.0)
        scores = dots[CHUNK:] * ratios
        begin = states_ref[s_at, :]
        inverse = inverse_ref[h * CHUNK : (h + 1) * CHUNK, :]
        new = new_ref[:, o_at]
        d_end = d_state[s_at, :]
        d_end_low = d_end.astype(BF16)
        kept = (keys * remain).astype(BF16)
        d_new = mm(scores, d_mixed, TN) + mm(kept, d_end_low)
        solved = mm(inverse, d_new, TN)
        solved_low = solved.astype(BF16)
        pair = jnp.concatenate([d_mixed, solved_low], 0)
        outer = mm(pair, jnp.concatenate([begin, new], 0), NT)
        d_query_state = outer[:CHUNK, :key_dim]
        d_keys_state = outer[CHUNK:, :key_dim]
        d_scores = jnp.where(causal, outer[:CHUNK, key_dim:], 0.0)
        d_system = jnp.where(strict, -outer[CHUNK:, key_dim:], 0.0)
        d_kept = mm(new, d_end_low, NT)
        lead = beta * decay
        d_begin = whole[:, h : h + 1] * d_end + mm(
            jnp.concatenate([query * decay, -lead * keys], 0), pair, TN
        )
        d_state[s_at, :] = d_begin
        d_dots_k = d_system * (beta * ratios)
        d_dots_q = d_scores * ratios
        near = mm(
            jnp.concatenate([d_dots_q, d_dots_k + jnp.transpose(d_dots_k)], 0), keys_low
        )
        d_query = decay * d_query_state + near[:CHUNK]
        d_keys = (
            near[CHUNK:] + mm(d_dots_q, query_low, TN) - lead * d_keys_state + remain * d_kept
        )
        along = decay * jnp.sum(keys * d_keys_state, -1, keepdims=True)
        weighed = d_system * weights
        d_beta = (
            jnp.sum(solved * values, -1, keepdims=True)
            - along
            + jnp.sum(weighed, -1, keepdims=True)
        )
        joint = weighed * beta + d_scores * scores
        left = remain * jnp.sum(keys * d_kept, -1, keepdims=True)
        total = jnp.sum(left, 0, keepdims=True) + whole[:, h : h + 1] * jnp.sum(
            jnp.sum(d_end * begin.astype(F32), -1, keepdims=True), 0, keepdims=True
        )
        d_run = (
            jnp.sum(joint, -1, keepdims=True)
            - jnp.sum(jnp.transpose(joint), -1, keepdims=True)
            + decay * jnp.sum(query * d_query_state, -1, keepdims=True)
            - beta * along
            - left
            + jnp.where(row_ids == CHUNK - 1, total, 0.0)
        )
        d_running = jnp.where(lanes == h, d_run, d_running)
        d_strengths = jnp.where(lanes == heads + h, d_beta, d_strengths)
        d_q = d_query * key_dim ** -0.5
        d_q = q_scale * (d_q - q_unit * jnp.sum(q_unit * d_q, -1, keepdims=True))
        d_k = k_scale * (d_keys - keys * jnp.sum(keys * d_keys, -1, keepdims=True))
        after[0:CHUNK, q_at] = d_q * slope[:, q_at]
        after[0:CHUNK, k_at] = d_k * slope[:, k_at]
        after[0:CHUNK, v_at] = (beta * solved) * slope[:, v_at]
    d_logdecay = mm_exact((rows <= cols).astype(F32), d_running)
    d_shifted = jnp.where(lanes < heads, d_logdecay * (-scale) * jax.nn.sigmoid(shifted), 0.0)
    d_params_ref[0:1, :] += jnp.sum(d_logdecay * logdecay, 0, keepdims=True)
    d_params_ref[1:2, :] += jnp.sum(d_shifted, 0, keepdims=True)
    d_pre_ref[:, width : width + 128] = (d_shifted + d_strengths * strengths * (1.0 - strengths)).astype(BF16)
    d_summed = after[0:CHUNK, :]
    total = taps_ref[3:4, :] * d_summed
    for j in range(3):
        total = total + taps_ref[j : j + 1, :] * after[3 - j : 3 - j + CHUNK, :]
    d_pre_ref[:, :width] = total.astype(BF16)
    for j in range(4):
        d_taps_ref[j : j + 1, :] += jnp.sum(
            d_summed * window[5 + j : 5 + j + CHUNK, :], 0, keepdims=True
        )
    after[CHUNK : CHUNK + 8, :] = after[0:8, :]


def mixer_forward(order, pre, taps, params, heads, key_dim, val_dim):
    chunks = pre.shape[0] // CHUNK
    width = taps.shape[1]
    here = lambda n, order: (order[n], 0)
    plain = lambda n, order: (n, 0)
    fixed = lambda n, order: (0, 0)
    return pl.pallas_call(
        functools.partial(forward_kernel, heads, key_dim, val_dim),
        grid_spec=pltpu.PrefetchScalarGridSpec(
            num_scalar_prefetch=1,
            grid=(chunks,),
            in_specs=[
                pl.BlockSpec((CHUNK, pre.shape[1]), here),
                pl.BlockSpec(taps.shape, fixed),
                pl.BlockSpec(params.shape, fixed),
            ],
            out_specs=[
                pl.BlockSpec((CHUNK, heads * val_dim), here),
                pl.BlockSpec((heads * key_dim, val_dim), plain),
                pl.BlockSpec((heads * CHUNK, CHUNK), plain),
                pl.BlockSpec((CHUNK, heads * val_dim), plain),
            ],
            scratch_shapes=[
                pltpu.VMEM((heads * key_dim, val_dim), F32),
                pltpu.VMEM((CHUNK + 8, width), F32),
            ],
        ),
        out_shape=[
            jax.ShapeDtypeStruct((pre.shape[0], heads * val_dim), F32),
            jax.ShapeDtypeStruct((chunks * heads * key_dim, val_dim), BF16),
            jax.ShapeDtypeStruct((chunks * heads * CHUNK, CHUNK), BF16),
            jax.ShapeDtypeStruct((pre.shape[0], heads * val_dim), BF16),
        ],
        compiler_params=pltpu.CompilerParams(vmem_limit_bytes=48 * 2**20),
        cost_estimate=pl.CostEstimate(
            flops=2 * 10**9, bytes_accessed=2**20, transcendentals=0
        ),
        name="mixer_forward",
    )(order, pre, taps, params)


def mixer_backward(
    order, pre, taps, params, states, inverses, news, mixed, gates, d_own, d_other, side, gain,
    heads, key_dim, val_dim,
):
    chunks = pre.shape[0] // CHUNK
    width = taps.shape[1]
    out_width = heads * val_dim
    per = CHUNK // 8
    here = lambda n, order: (order[chunks - 1 - n], 0)
    half = chunks // 2
    first = lambda n, order: (jnp.minimum(order[chunks - 1 - n], half - 1), 0)
    second = lambda n, order: (jnp.maximum(order[chunks - 1 - n] - half, 0), 0)
    before = lambda n, order: (order[jnp.maximum(chunks - 2 - n, 0)] * per + per - 1, 0)
    plain = lambda n, order: (chunks - 1 - n, 0)
    fixed = lambda n, order: (0, 0)
    return pl.pallas_call(
        functools.partial(backward_kernel, heads, key_dim, val_dim),
        grid_spec=pltpu.PrefetchScalarGridSpec(
            num_scalar_prefetch=1,
            grid=(chunks,),
            in_specs=[
                pl.BlockSpec((CHUNK, pre.shape[1]), here),
                pl.BlockSpec((8, pre.shape[1]), before),
                pl.BlockSpec(taps.shape, fixed),
                pl.BlockSpec(params.shape, fixed),
                pl.BlockSpec((heads * key_dim, val_dim), plain),
                pl.BlockSpec((heads * CHUNK, CHUNK), plain),
                pl.BlockSpec((CHUNK, out_width), plain),
                pl.BlockSpec((CHUNK, out_width), here),
                pl.BlockSpec((CHUNK, out_width), here),
                pl.BlockSpec((CHUNK, d_own.shape[1]), first),
                pl.BlockSpec((CHUNK, d_own.shape[1]), second),
                pl.BlockSpec(side.shape, lambda n, order: (0, 0, 0, 0)),
                pl.BlockSpec((1, val_dim), fixed),
            ],
            out_specs=[
                pl.BlockSpec((CHUNK, pre.shape[1] + out_width), here),
                pl.BlockSpec((8, width), fixed),
                pl.BlockSpec((8, 128), fixed),
                pl.BlockSpec((8, val_dim), fixed),
            ],
            scratch_shapes=[
                pltpu.VMEM((heads * key_dim, val_dim), F32),
                pltpu.VMEM((CHUNK + 8, width), F32),
                pltpu.VMEM((CHUNK + 8, width), F32),
            ],
        ),
        out_shape=[
            jax.ShapeDtypeStruct((pre.shape[0], pre.shape[1] + out_width), BF16),
            jax.ShapeDtypeStruct((8, width), F32),
            jax.ShapeDtypeStruct((8, 128), F32),
            jax.ShapeDtypeStruct((8, val_dim), F32),
        ],
        compiler_params=pltpu.CompilerParams(vmem_limit_bytes=48 * 2**20),
        cost_estimate=pl.CostEstimate(
            flops=2 * 10**9, bytes_accessed=2 * 2**20, transcendentals=0
        ),
        name="mixer_backward",
    )(order, pre, pre, taps, params, states, inverses, news, mixed, gates, d_own, d_other, side, gain)


def roomy(**cost):
    return dict(
        compiler_params=pltpu.CompilerParams(vmem_limit_bytes=56 * 2**20),
        cost_estimate=pl.CostEstimate(
            flops=cost["flops"] // 8, bytes_accessed=cost["bytes"] // 8, transcendentals=0
        ),
    )


def pack_mix_kernel(heads, core_ref, q_ref, k_ref, v_ref, decay_ref, strength_ref, out_ref):
    first = core_ref[0] == 0
    wide, tall = q_ref.shape[1], v_ref.shape[1]
    out_ref[:, :wide] = q_ref[...]
    out_ref[:, wide : 2 * wide] = k_ref[...]
    out_ref[:, 2 * wide : 2 * wide + tall] = v_ref[...]

    def part(ref):
        values = ref[...].astype(F32)
        return jnp.where(first, values[:, :heads], values[:, heads:])

    rows = out_ref.shape[0]
    out_ref[:, 2 * wide + tall :] = jnp.concatenate(
        [part(decay_ref), part(strength_ref), jnp.zeros((rows, 128 - 2 * heads), F32)], 1
    ).astype(BF16)


def pack_mix(core, heads, w_query, w_key, w_value, w_decay, w_strength):
    depth = w_query.shape[0]
    wide, tall = w_query.shape[1] // 2, w_value.shape[1] // 2
    here = lambda i, core: (0, core[0])
    fixed = lambda i, core: (0, 0)
    return pl.pallas_call(
        functools.partial(pack_mix_kernel, heads),
        grid_spec=pltpu.PrefetchScalarGridSpec(
            num_scalar_prefetch=1,
            grid=(1,),
            in_specs=[
                pl.BlockSpec((depth, wide), here),
                pl.BlockSpec((depth, wide), here),
                pl.BlockSpec((depth, tall), here),
                pl.BlockSpec(w_decay.shape, fixed),
                pl.BlockSpec(w_strength.shape, fixed),
            ],
            out_specs=pl.BlockSpec((depth, 2 * wide + tall + 128), fixed),
        ),
        out_shape=jax.ShapeDtypeStruct((depth, 2 * wide + tall + 128), BF16),
        name="pack_mix",
        **roomy(flops=10**6, bytes=2**21),
    )(core, w_query, w_key, w_value, w_decay, w_strength)


def pack_rest_kernel(core_ref, outgate_ref, out_ref, gate_ref, up_ref, down_ref, side_ref, wide_ref):
    first = core_ref[0] == 0
    depth = outgate_ref.shape[0]
    units = gate_ref.shape[1] // 2
    side_ref[:depth, :] = outgate_ref[...]
    side_ref[depth:, :] = jnp.transpose(out_ref[...].astype(F32)).astype(BF16)
    for at, ref in ((0, gate_ref), (1, up_ref)):
        values = ref[...]
        wide_ref[at * depth : (at + 1) * depth, :] = jnp.where(
            first, values[:, :units], values[:, units:]
        )
    wide_ref[2 * depth :, :] = jnp.transpose(down_ref[...].astype(F32)).astype(BF16)


def pack_rest(core, w_outgate, w_out, w_gate, w_up, w_down):
    depth = w_outgate.shape[0]
    tall, units = w_outgate.shape[1] // 2, w_gate.shape[1] // 2
    fixed = lambda i, core: (0, 0)
    return pl.pallas_call(
        pack_rest_kernel,
        grid_spec=pltpu.PrefetchScalarGridSpec(
            num_scalar_prefetch=1,
            grid=(1,),
            in_specs=[
                pl.BlockSpec((depth, tall), lambda i, core: (0, core[0])),
                pl.BlockSpec((tall, depth), lambda i, core: (core[0], 0)),
                pl.BlockSpec(w_gate.shape, fixed),
                pl.BlockSpec(w_up.shape, fixed),
                pl.BlockSpec((units, depth), lambda i, core: (core[0], 0)),
            ],
            out_specs=[
                pl.BlockSpec((2 * depth, tall), fixed),
                pl.BlockSpec((3 * depth, units), fixed),
            ],
        ),
        out_shape=[
            jax.ShapeDtypeStruct((2 * depth, tall), BF16),
            jax.ShapeDtypeStruct((3 * depth, units), BF16),
        ],
        name="pack_rest",
        **roomy(flops=10**6, bytes=10 * 2**20),
    )(core, w_outgate, w_out, w_gate, w_up, w_down)


def arrange_kernel(scalars_ref, tokens_ref, cotangent_ref, gain_ref, normed_ref, branch_ref):
    step = pl.program_id(0)
    rows = tokens_ref.shape[0]
    tokens = tokens_ref[...].astype(F32)
    scale = lax.rsqrt(jnp.mean(tokens * tokens, -1, keepdims=True) + 1e-6)
    normed_ref[...] = (tokens * scale * gain_ref[...]).astype(BF16)
    place = scalars_ref[0] + scalars_ref[2 + step] * rows + lax.broadcasted_iota(
        jnp.int32, (rows, 1), 0
    )
    branch_ref[...] = jnp.where(place < scalars_ref[1], cotangent_ref[...], 0).astype(BF16)


def arrange(scalars, tokens, cotangent, gain, layers):
    rows, model = tokens.shape[0] // layers, tokens.shape[1]
    there = pl.BlockSpec((rows, model), lambda p, scalars: (scalars[2 + p], 0))
    plain = pl.BlockSpec((rows, model), lambda p, scalars: (p, 0))
    return pl.pallas_call(
        arrange_kernel,
        grid_spec=pltpu.PrefetchScalarGridSpec(
            num_scalar_prefetch=1,
            grid=(layers,),
            in_specs=[there, there, pl.BlockSpec((1, model), lambda p, scalars: (0, 0))],
            out_specs=[plain, plain],
        ),
        out_shape=[jax.ShapeDtypeStruct(tokens.shape, BF16)] * 2,
        name="arrange",
        **roomy(flops=10**7, bytes=8 * 2**20),
    )(scalars, tokens, cotangent, gain)


TILE = 256


def heads_kernel(
    heads, normed_ref, mixed_ref, side_ref, gain_ref, gates_ref, heads_ref, other_ref, own_ref
):
    step = pl.program_id(0)
    half = pl.num_programs(0) // 2
    shards, _, depth, tall = side_ref.shape
    val_dim = tall // heads
    gates = mm(normed_ref[:, :depth], side_ref[0, 0])
    for f in range(1, shards):
        gates = gates + mm(normed_ref[:, f * depth : (f + 1) * depth], side_ref[f, 0])
    gates_ref[...] = gates
    for h in range(heads):
        at = slice(h * val_dim, (h + 1) * val_dim)
        mixed = mixed_ref[:, at]
        gate = gates[:, at]
        scale = lax.rsqrt(jnp.mean(mixed * mixed, -1, keepdims=True) + 1e-5)
        heads_ref[:, at] = (
            mixed * scale * gain_ref[...] * (gate * jax.nn.sigmoid(gate))
        ).astype(BF16)
    low = heads_ref[...]

    def write(ref):
        for f in range(shards):
            ref[:, f * depth : (f + 1) * depth] = mm(low, side_ref[f, 1], NT).astype(BF16)

    @pl.when(step < half)
    def _():
        write(other_ref)

    @pl.when(step >= half)
    def _():
        write(own_ref)


def turned_specs(tiles):
    half = tiles // 2
    here = lambda i: (jnp.where(i < half, i + half, i - half), 0)
    other = lambda i: (jnp.minimum(i, half - 1), 0)
    own = lambda i: (jnp.maximum(i - half, 0), 0)
    return here, other, own


def head_outputs(normed, mixed, side, gain, heads):
    count, model = normed.shape
    tall = mixed.shape[1]
    here, other, own = turned_specs(count // TILE)
    return pl.pallas_call(
        functools.partial(heads_kernel, heads),
        grid=(count // TILE,),
        in_specs=[
            pl.BlockSpec((TILE, model), here),
            pl.BlockSpec((TILE, tall), here),
            pl.BlockSpec(side.shape, lambda i: (0, 0, 0, 0)),
            pl.BlockSpec(gain.shape, lambda i: (0, 0)),
        ],
        out_specs=[
            pl.BlockSpec((TILE, tall), here),
            pl.BlockSpec((TILE, tall), here),
            pl.BlockSpec((TILE, model), other),
            pl.BlockSpec((TILE, model), own),
        ],
        out_shape=[
            jax.ShapeDtypeStruct((count, tall), F32),
            jax.ShapeDtypeStruct((count, tall), BF16),
            jax.ShapeDtypeStruct((count // 2, model), BF16),
            jax.ShapeDtypeStruct((count // 2, model), BF16),
        ],
        name="head_outputs",
        **roomy(flops=4 * count * model * tall, bytes=16 * 2**20),
    )(normed, mixed, side, gain)


def feed_kernel(hidden_ref, branch_ref, wide_ref, stack_ref, d_hidden_ref, branch_out_ref):
    shards, _, depth, units = wide_ref.shape

    def forward(ref, at):
        total = mm(ref[:, :depth], wide_ref[0, at])
        for f in range(1, shards):
            total = total + mm(ref[:, f * depth : (f + 1) * depth], wide_ref[f, at])
        return total

    gate = forward(hidden_ref, 0)
    up = forward(hidden_ref, 1)
    d_act = forward(branch_ref, 2)
    sigma = jax.nn.sigmoid(gate)
    silu = gate * sigma
    act = (silu * up).astype(BF16)
    d_gate = (d_act * up * (sigma + silu * (1.0 - sigma))).astype(BF16)
    d_up = (d_act * silu).astype(BF16)
    stack_ref[0] = d_gate
    stack_ref[1] = d_up
    stack_ref[2] = act
    for f in range(shards):
        at = slice(f * depth, (f + 1) * depth)
        d_hidden_ref[:, at] = (
            mm(d_gate, wide_ref[f, 0], NT) + mm(d_up, wide_ref[f, 1], NT)
        ).astype(BF16)
        branch_out_ref[:, at] = mm(act, wide_ref[f, 2], NT).astype(BF16)


def feed_forward(hidden, branch, wide):
    count, model = hidden.shape
    units = wide.shape[3]
    row = pl.BlockSpec((TILE, model), lambda i: (i, 0))
    return pl.pallas_call(
        feed_kernel,
        grid=(count // TILE,),
        in_specs=[row, row, pl.BlockSpec(wide.shape, lambda i: (0, 0, 0, 0))],
        out_specs=[pl.BlockSpec((3, TILE, units), lambda i: (0, i, 0)), row, row],
        out_shape=[
            jax.ShapeDtypeStruct((3, count, units), BF16),
            jax.ShapeDtypeStruct((count, model), BF16),
            jax.ShapeDtypeStruct((count, model), BF16),
        ],
        name="feed_forward",
        **roomy(flops=12 * count * model * units, bytes=20 * 2**20),
    )(hidden, branch, wide)


def feed_grads_kernel(h_own, h_other, b_own, b_other, s_own, s_other, out_ref):
    units = s_own.shape[2]
    for at, own, other in ((0, h_own, h_other), (1, h_own, h_other), (2, b_own, b_other)):
        out_ref[:, at * units : (at + 1) * units] = (
            mm(own[...], s_own[at], TN) + mm(other[...], s_other[at], TN)
        ).astype(BF16)
    rest = out_ref.shape[1] - 3 * units
    if rest:
        out_ref[:, 3 * units :] = jnp.zeros((out_ref.shape[0], rest), BF16)


def feed_grads(hidden, branch, stacks, shards):
    count, model = hidden[0].shape
    units = stacks[0].shape[2]
    depth = model // shards
    width = -(-3 * units // 128) * 128
    part = pl.BlockSpec((count, depth), lambda f: (0, f))
    use_s = pl.BlockSpec((3, count, units), lambda f: (0, 0, 0))
    return pl.pallas_call(
        feed_grads_kernel,
        grid=(shards,),
        in_specs=[part, part, part, part, use_s, use_s],
        out_specs=pl.BlockSpec((depth, width), lambda f: (f, 0)),
        out_shape=jax.ShapeDtypeStruct((model, width), BF16),
        name="feed_grads",
        **roomy(flops=12 * count * model * units, bytes=20 * 2**20),
    )(*hidden, *branch, *stacks)


def d_normed_kernel(side_at, mix_ref, normed_ref, weights_ref, side_ref, other_ref, own_ref, sum_ref):
    step = pl.program_id(0)
    half = pl.num_programs(0) // 2
    shards, _, depth, _ = side_ref.shape

    @pl.when(step == 0)
    def _():
        sum_ref[...] = jnp.zeros_like(sum_ref)

    def write(ref):
        for f in range(shards):
            at = slice(f * depth, (f + 1) * depth)
            part = mm(mix_ref[:, :side_at], weights_ref[at, :], NT) + mm(
                mix_ref[:, side_at:], side_ref[f, 0], NT
            )
            ref[:, at] = part.astype(BF16)
            sum_ref[0:1, at] += jnp.sum(part * normed_ref[:, at].astype(F32), 0, keepdims=True)

    @pl.when(step < half)
    def _():
        write(other_ref)

    @pl.when(step >= half)
    def _():
        write(own_ref)


def d_normed_rows(d_mix, normed, weights, side):
    count, model = normed.shape
    here, other, own = turned_specs(count // TILE)
    fixed = lambda i: (0, 0)
    return pl.pallas_call(
        functools.partial(d_normed_kernel, weights.shape[1]),
        grid=(count // TILE,),
        in_specs=[
            pl.BlockSpec((TILE, d_mix.shape[1]), here),
            pl.BlockSpec((TILE, model), here),
            pl.BlockSpec(weights.shape, fixed),
            pl.BlockSpec(side.shape, lambda i: (0, 0, 0, 0)),
        ],
        out_specs=[
            pl.BlockSpec((TILE, model), other),
            pl.BlockSpec((TILE, model), own),
            pl.BlockSpec((8, model), fixed),
        ],
        out_shape=[
            jax.ShapeDtypeStruct((count // 2, model), BF16),
            jax.ShapeDtypeStruct((count // 2, model), BF16),
            jax.ShapeDtypeStruct((8, model), F32),
        ],
        name="d_normed_rows",
        **roomy(flops=2 * count * model * d_mix.shape[1], bytes=16 * 2**20),
    )(d_mix, normed, weights, side)


def mix_grads_kernel(at, normed_ref, mix_ref, d_own_ref, d_other_ref, heads_ref, extra_ref, out_ref):
    width = mix_ref.shape[1]
    half = d_own_ref.shape[0]
    out_ref[:, :width] = mm(normed_ref[...], mix_ref[...], TN).astype(BF16)
    out_ref[:, width:] = (
        mm(d_own_ref[...], heads_ref[:half, :], TN) + mm(d_other_ref[...], heads_ref[half:, :], TN)
    ).astype(BF16)
    out_ref[:, at : at + extra_ref.shape[1]] = extra_ref[...]


def mix_grads(normed, d_mix, d_own, d_other, heads_out, extra, at, shards):
    count, model = normed.shape
    depth = model // shards
    width = d_mix.shape[1] + heads_out.shape[1]
    fixed = lambda f: (0, 0)
    return pl.pallas_call(
        functools.partial(mix_grads_kernel, at),
        grid=(shards,),
        in_specs=[
            pl.BlockSpec((count, depth), lambda f: (0, f)),
            pl.BlockSpec(d_mix.shape, fixed),
            pl.BlockSpec((count // 2, depth), lambda f: (0, f)),
            pl.BlockSpec((count // 2, depth), lambda f: (0, f)),
            pl.BlockSpec(heads_out.shape, fixed),
            pl.BlockSpec((depth, extra.shape[1]), lambda f: (f, 0)),
        ],
        out_specs=pl.BlockSpec((depth, width), lambda f: (f, 0)),
        out_shape=jax.ShapeDtypeStruct((model, width), BF16),
        name="mix_grads",
        **roomy(flops=2 * count * model * width, bytes=20 * 2**20),
    )(normed, d_mix, d_own, d_other, heads_out, extra)


def finish_wide_kernel(units, core_ref, own_ref, other_ref, gate_ref, up_ref, down_ref):
    first = core_ref[0] == 0
    own, other = own_ref[...].astype(F32), other_ref[...].astype(F32)
    low, high = jnp.where(first, own, other), jnp.where(first, other, own)
    for at, ref in ((0, gate_ref), (1, up_ref)):
        ref[:, :units] = low[:, at * units : (at + 1) * units]
        ref[:, units:] = high[:, at * units : (at + 1) * units]
    down_ref[:units, :] = jnp.transpose(low[:, 2 * units : 3 * units])
    down_ref[units:, :] = jnp.transpose(high[:, 2 * units : 3 * units])


def finish_wide(core, own, other, units):
    depth, width = own.shape
    row = lambda size: pl.BlockSpec((128, size), lambda i, core: (i, 0))
    return pl.pallas_call(
        functools.partial(finish_wide_kernel, units),
        grid_spec=pltpu.PrefetchScalarGridSpec(
            num_scalar_prefetch=1,
            grid=(depth // 128,),
            in_specs=[row(width), row(width)],
            out_specs=[
                row(2 * units),
                row(2 * units),
                pl.BlockSpec((2 * units, 128), lambda i, core: (0, i)),
            ],
        ),
        out_shape=[
            jax.ShapeDtypeStruct((depth, 2 * units), F32),
            jax.ShapeDtypeStruct((depth, 2 * units), F32),
            jax.ShapeDtypeStruct((2 * units, depth), F32),
        ],
        name="finish_wide",
        **roomy(flops=10**6, bytes=14 * 2**20),
    )(core, own, other)


def finish_mix_kernel(cuts, core_ref, a_ref, b_ref, *refs):
    first = core_ref[0] == 0
    own, other = a_ref[...].astype(F32), b_ref[...].astype(F32)
    low, high = jnp.where(first, own, other), jnp.where(first, other, own)
    for (begin, size), ref in zip(cuts[:-1], refs):
        ref[:, :size] = low[:, begin : begin + size]
        ref[:, size:] = high[:, begin : begin + size]
    begin, size = cuts[-1]
    refs[-1][:size, :] = jnp.transpose(low[:, begin : begin + size])
    refs[-1][size:, :] = jnp.transpose(high[:, begin : begin + size])


def finish_mix(core, own, other, cuts):
    depth, width = own.shape
    tall = cuts[-1][1]
    row = lambda size: pl.BlockSpec((128, size), lambda i, core: (i, 0))
    return pl.pallas_call(
        functools.partial(finish_mix_kernel, cuts),
        grid_spec=pltpu.PrefetchScalarGridSpec(
            num_scalar_prefetch=1,
            grid=(depth // 128,),
            in_specs=[row(width), row(width)],
            out_specs=[row(2 * size) for _, size in cuts[:-1]]
            + [pl.BlockSpec((2 * tall, 128), lambda i, core: (0, i))],
        ),
        out_shape=[jax.ShapeDtypeStruct((depth, 2 * size), F32) for _, size in cuts[:-1]]
        + [jax.ShapeDtypeStruct((2 * tall, depth), F32)],
        name="finish_mix",
        **roomy(flops=10**6, bytes=14 * 2**20),
    )(core, own, other)


def after(value, *others):
    return lax.optimization_barrier((value,) + others)[0]


def is_square(axis):
    return lax.axis_size(axis) == 4


def across(value, flip):
    return lax.ppermute(value, "fsdp", [(i, i ^ flip) for i in range(4)])


def swapped(value):
    return lax.ppermute(value, "context", [(0, 1), (1, 0)])


def gathered_rows(own, beside):
    if not is_square("fsdp"):
        return lax.all_gather(own, "fsdp", axis=0, tiled=True), beside
    rows = own.shape[0]
    half = rows // 2
    along_x = across(own, 1)
    along_y = across(own, 2)
    along_x, along_y, beside = lax.optimization_barrier((along_x, along_y, beside))
    low = across(along_x[:half], 2)
    high = across(along_y[half:], 1)
    shard = lax.axis_index("fsdp")
    whole = jnp.zeros((4 * rows,) + own.shape[1:], own.dtype)
    for place, part in ((0, own), (1, along_x), (2, along_y)):
        whole = lax.dynamic_update_slice_in_dim(whole, part, (shard ^ place) * rows, 0)
    whole = lax.dynamic_update_slice_in_dim(whole, low, (shard ^ 3) * rows, 0)
    return lax.dynamic_update_slice_in_dim(whole, high, (shard ^ 3) * rows + half, 0), beside


def scattered(blocks):
    return lax.psum_scatter(blocks, "fsdp", scatter_dimension=0, tiled=True)


def line_sum(value, beside=(), axis="tensor"):
    size = lax.axis_size(axis)
    rows = value.shape[0] // size
    parts = [
        lax.ppermute(
            value[p * rows : (p + 1) * rows], axis, [(i, (i - p) % size) for i in range(size)]
        )
        for p in range(1, size)
    ]
    if beside:
        parts, beside = lax.optimization_barrier((parts, tuple(beside)))
    total = value[:rows].astype(F32)
    for part in parts:
        total = total + part.astype(F32)
    return (total, *beside) if beside else total


def line_sum_hops(value, axis="tensor"):
    size = lax.axis_size(axis)
    rows = value.shape[0] // size
    block = lambda p: value[p * rows : (p + 1) * rows].astype(F32)
    right = left = None
    for step in range(1, size):
        send_r, send_l = block(step), block(size - step)
        if right is not None:
            send_r = send_r + right.astype(F32)
            send_l = send_l + left.astype(F32)
        right = lax.ppermute(send_r.astype(BF16), axis, [(i, i + 1) for i in range(step)])
        left = lax.ppermute(
            send_l.astype(BF16), axis, [(i, i - 1) for i in range(size - step, size)]
        )
    return block(0) + right.astype(F32) + left.astype(F32)


def line_gather(own, beside=(), axis="tensor"):
    size = lax.axis_size(axis)
    rights, lefts = [own], [own]
    for step in range(1, size):
        rights.append(
            lax.ppermute(rights[-1], axis, [(i, i + 1) for i in range(step - 1, size - 1)])
        )
        lefts.append(lax.ppermute(lefts[-1], axis, [(i, i - 1) for i in range(1, size - step + 1)]))
    if beside:
        (rights, lefts), beside = lax.optimization_barrier(((rights, lefts), tuple(beside)))
    parts = [own] + [rights[k] + lefts[size - k] for k in range(1, size)]
    return (parts, *beside) if beside else parts


def line_gather_direct(own, axis="tensor"):
    size = lax.axis_size(axis)
    return [own] + [
        lax.ppermute(own, axis, [(i, (i + p) % size) for i in range(size)]) for p in range(1, size)
    ]


def line_total(value, axis="tensor"):
    size = lax.axis_size(axis)
    step = 1
    while step < size:
        value = value + lax.ppermute(value, axis, [(i, i ^ step) for i in range(size)])
        step *= 2
    return value


def core_sum(other_rows, own_rows):
    return (own_rows.astype(F32) + swapped(other_rows).astype(F32)).astype(BF16)


def dot(a, b, dims=NN):
    return lax.dot_general(a, b, (dims, ((), ())), preferred_element_type=F32)


def norm_parts(values, epsilon):
    return lax.rsqrt(jnp.mean(values * values, -1, keepdims=True) + epsilon)


def norm_back(d_scaled, values, scale, gain):
    raised = d_scaled * gain
    return scale * raised - values * (
        scale * scale * scale * jnp.mean(raised * values, -1, keepdims=True)
    )


def on_device(
    inputs, lengths, norm_attn, w_query, w_key, w_value, w_decay, w_strength, decay_log,
    decay_bias, conv_query, conv_key, conv_value, w_outgate, norm_head, w_out, norm_mlp, w_gate,
    w_up, w_down, cotangent,
):
    shard, core, layer = (lax.axis_index(name) for name in ("fsdp", "context", "tensor"))
    shards, layers = lax.axis_size("fsdp"), lax.axis_size("tensor")
    seg, model = inputs.shape[1:]
    rows = seg // layers
    depth = norm_attn.shape[0]
    all_heads, taps_count, key_part = conv_query.shape
    val_part = conv_value.shape[2]
    heads = all_heads // 2
    key_dim, val_dim = key_part * shards, val_part * shards
    wide, tall = heads * key_dim, heads * val_dim
    width = 2 * wide + tall
    units = w_gate.shape[1] // 2

    def mine(array, dim):
        size = array.shape[dim] // 2
        first = lax.slice_in_dim(array, 0, size, axis=dim)
        second = lax.slice_in_dim(array, size, 2 * size, axis=dim)
        return jnp.where(core == 0, first, second)

    core_id = core.reshape(1).astype(jnp.int32)
    own_mix = pack_mix(core_id, heads, w_query, w_key, w_value, w_decay, w_strength)

    pieces = (
        norm_attn, norm_mlp, norm_head,
        mine(conv_query, 0).reshape(-1), mine(conv_key, 0).reshape(-1),
        mine(conv_value, 0).reshape(-1),
    )
    small = after(jnp.concatenate(pieces), own_mix)
    if is_square("fsdp"):
        stack = jnp.stack([small, across(small, 1), across(small, 2), across(small, 3)])
        stack = jnp.stack([lax.dynamic_index_in_dim(stack, shard ^ i, 0, False) for i in range(4)])
    else:
        stack = lax.all_gather(small, "fsdp")
    cuts = [0]
    for piece in pieces:
        cuts.append(cuts[-1] + piece.shape[0])
    gain_attn = stack[:, cuts[0] : cuts[1]].reshape(1, model).astype(F32)
    gain_mlp = stack[:, cuts[1] : cuts[2]].reshape(1, model).astype(F32)
    gain_head = stack[:, cuts[2] : cuts[3]].reshape(1, val_dim).astype(F32)

    def taps_of(at, part):
        array = stack[:, cuts[at] : cuts[at + 1]].reshape(shards, heads, taps_count, part)
        return jnp.transpose(array, (2, 1, 0, 3)).reshape(taps_count, -1)

    taps = jnp.concatenate([taps_of(3, key_part), taps_of(4, key_part), taps_of(5, val_part)], 1)
    taps = jnp.pad(taps.astype(F32), ((0, 8 - taps_count), (0, 0)))
    params = jnp.pad(
        jnp.stack([mine(decay_log, 0), mine(decay_bias, 0)]).astype(F32),
        ((0, 6), (0, 128 - heads)),
    )

    turns = (layer - jnp.arange(layers, dtype=jnp.int32)) % layers
    scalars = jnp.concatenate([(core * seg).reshape(1), lengths[:1], turns]).astype(jnp.int32)
    per_core, per_block = seg // CHUNK, rows // CHUNK
    ids = jnp.arange(2 * per_core, dtype=jnp.int32)
    within = ids % per_core
    order = (
        jnp.where(ids // per_core == core, 0, per_core)
        + ((layer - within // per_block) % layers) * per_block
        + within % per_block
    ).astype(jnp.int32)
    live_own = (
        core * seg + layer * rows + jnp.arange(rows, dtype=jnp.int32) < lengths[0]
    ).astype(F32)[:, None]
    tokens_own = lax.dynamic_slice_in_dim(inputs[0], layer * rows, rows, 0).astype(F32)
    d_out_own = lax.dynamic_slice_in_dim(cotangent[0], layer * rows, rows, 0).astype(F32)
    normed_own, d_branch_own = arrange(scalars, inputs[0], cotangent[0], gain_attn, layers)
    normed_other = swapped(normed_own)
    own_side, own_feed = pack_rest(core_id, w_outgate, w_out, w_gate, w_up, w_down)
    full_mix, (normed_other, own_side, own_feed) = gathered_rows(
        own_mix, (normed_other, own_side, own_feed)
    )
    normed = jnp.concatenate([normed_own, normed_other], 0)
    d_branch = (d_branch_own, swapped(after(d_branch_own, full_mix)))
    side = lax.all_gather(after(own_side, full_mix), "fsdp", axis=0, tiled=True)

    projected = dot(normed, full_mix)
    feed = lax.all_gather(after(own_feed, projected), "fsdp", axis=0, tiled=True)
    side = side.reshape(shards, 2, depth, tall)
    feed = feed.reshape(shards, 3, depth, units)
    mixed, states, inverses, news = mixer_forward(
        order, projected, taps, params, heads, key_dim, val_dim
    )
    gates, heads_out, attn_other, attn_own = head_outputs(normed, mixed, side, gain_head, heads)
    attn = line_sum_hops(core_sum(attn_other, attn_own))
    middle = tokens_own + live_own * attn
    mlp_scale = norm_parts(middle, 1e-6)
    hidden_own = (middle * mlp_scale * gain_mlp).astype(BF16)
    hidden_mine = jnp.concatenate(line_gather(hidden_own), 0)
    hidden = (hidden_mine, swapped(hidden_mine))

    stack_own, d_hidden_mine, branch_mine = feed_forward(hidden[0], d_branch[0], feed)
    stack_other, d_hidden_other, branch_other = feed_forward(hidden[1], d_branch[1], feed)
    d_hidden_core = core_sum(d_hidden_other, d_hidden_mine)
    held = lax.optimization_barrier((stack_own, stack_other, branch_other, d_hidden_core))
    grad_feed = feed_grads(hidden, d_branch, held[:2], shards)
    branch_core = core_sum(held[2], branch_mine)
    d_hidden, grad_feed, branch_core = line_sum(d_hidden_core, (grad_feed, branch_core))
    sum_feed = scattered(grad_feed)

    grad_mlp = jnp.sum(d_hidden * middle * mlp_scale, 0)
    d_middle = d_out_own + norm_back(d_hidden, middle, mlp_scale, gain_mlp)
    d_attn_mine = jnp.concatenate(line_gather((live_own * d_middle).astype(BF16)), 0)
    d_attn = (d_attn_mine, swapped(d_attn_mine))

    branch_core, *d_attn = lax.optimization_barrier((branch_core, *d_attn))

    def placed(parts):
        whole = jnp.zeros((seg, model), BF16)
        for p, part in enumerate(parts):
            whole = lax.dynamic_update_slice(whole, part, (((layer - p) % layers) * rows, 0))
        return whole[None]

    d_mix, d_taps, d_params, d_gain = mixer_backward(
        order, projected, taps, params, states, inverses, news, mixed, gates, *d_attn, side,
        gain_head, heads, key_dim, val_dim,
    )
    branch, d_mix = line_sum(branch_core, (d_mix,))
    out_own = (middle + live_own * branch).astype(BF16)
    out_own, sum_feed, d_mix = lax.optimization_barrier((out_own, sum_feed, d_mix))
    out_parts = line_gather_direct(out_own)
    side_at = width + 128
    d_normed_other, d_normed_mine, weighted = d_normed_rows(d_mix, normed, full_mix, side)
    d_normed_core = core_sum(d_normed_other, d_normed_mine)

    grad_attn = weighted[0] / gain_attn[0]
    vector = after(jnp.concatenate([grad_mlp, grad_attn, d_gain[0]]), d_normed_core)
    vector = line_total(vector + swapped(vector))

    def tap_rows(begin, size):
        array = d_taps[:taps_count, begin : begin + heads * size]
        array = array.reshape(taps_count, heads, shards, size // shards)
        return jnp.transpose(array, (2, 0, 1, 3)).reshape(shards, -1)

    tap_list = jnp.concatenate(
        [tap_rows(0, key_dim), tap_rows(wide, key_dim), tap_rows(2 * wide, val_dim)], 1
    )
    tap_size = tap_list.shape[1]
    tap_lines = -(-tap_size // depth)
    tap_list = jnp.pad(tap_list, ((0, 0), (0, tap_lines * depth - tap_size)))
    tap_list = jnp.transpose(tap_list.reshape(shards, tap_lines, depth), (1, 0, 2))
    decays = jnp.concatenate([d_params[0, :heads], d_params[1, :heads]])
    mixed_line = jnp.concatenate(
        [
            vector[2 * model :].reshape(shards, val_part),
            jnp.broadcast_to(decays, (shards, 2 * heads)),
            jnp.zeros((shards, depth - val_part - 2 * heads), F32),
        ],
        1,
    )
    lines = jnp.concatenate(
        [
            vector[: 2 * model].reshape(2, model), mixed_line.reshape(1, model),
            tap_list.reshape(tap_lines, model),
        ],
        0,
    )
    extra = jnp.transpose(jnp.pad(lines, ((0, 64 - lines.shape[0]), (0, 0)))).astype(BF16)
    grad_mix = mix_grads(normed, d_mix, *d_attn, heads_out, extra, width + 64, shards)
    d_normed, grad_mix = line_sum(d_normed_core, (grad_mix,))
    low_mix = scattered(grad_mix)
    other_mix = swapped(low_mix)

    d_tokens = norm_back(d_normed, tokens_own, norm_parts(tokens_own, 1e-6), gain_attn)
    feed_done = finish_wide(core_id, sum_feed, swapped(sum_feed), units)
    parts, (g_gate, g_up, g_down) = line_gather((d_middle + d_tokens).astype(BF16), (feed_done,))
    input_grad = placed(parts)
    output = placed(out_parts)
    g_query, g_key, g_value, g_outgate, g_out = finish_mix(
        core_id, low_mix, other_mix,
        ((0, wide), (wide, wide), (2 * wide, tall), (side_at, tall), (side_at + tall, tall)),
    )

    def column(table, at):
        return table[:, width + 64 + at].astype(F32)

    def of_heads(table):
        flat = jnp.concatenate([column(table, 3 + i) for i in range(tap_lines)])
        q_count, v_count = taps_count * heads * key_part, taps_count * heads * val_part

        def cut_taps(begin, count):
            array = flat[begin : begin + count].reshape(taps_count, heads, -1)
            return jnp.transpose(array, (1, 0, 2))

        line = column(table, 2)
        return (
            line[val_part : val_part + heads],
            line[val_part + heads : val_part + 2 * heads],
            cut_taps(0, q_count),
            cut_taps(q_count, q_count),
            cut_taps(2 * q_count, v_count),
        )

    def ordered(own, other, dim):
        return jnp.where(
            core == 0, jnp.concatenate([own, other], dim), jnp.concatenate([other, own], dim)
        )

    d_log, d_bias, d_conv_q, d_conv_k, d_conv_v = (
        ordered(a, b, 0) for a, b in zip(of_heads(low_mix), of_heads(other_mix))
    )

    def narrow(begin):
        return ordered(
            low_mix[:, begin : begin + heads], other_mix[:, begin : begin + heads], 1
        ).astype(F32)

    return (
        output,
        input_grad,
        column(low_mix, 1),
        g_query,
        g_key,
        g_value,
        narrow(width),
        narrow(width + heads),
        d_log,
        d_bias,
        d_conv_q,
        d_conv_k,
        d_conv_v,
        g_outgate,
        column(low_mix, 2)[:val_part],
        g_out,
        column(low_mix, 0),
        g_gate,
        g_up,
        g_down,
    )


def solution(mesh):
    placed = (
        P("fsdp", "context", None),
        P("fsdp"),
        P("fsdp"),
        P("fsdp", "tensor"),
        P("fsdp", "tensor"),
        P("fsdp", "tensor"),
        P("fsdp", "tensor"),
        P("fsdp", "tensor"),
        P("tensor"),
        P("tensor"),
        P("tensor", None, "fsdp"),
        P("tensor", None, "fsdp"),
        P("tensor", None, "fsdp"),
        P("fsdp", "tensor"),
        P("fsdp"),
        P("tensor", "fsdp"),
        P("fsdp"),
        P("fsdp", "tensor"),
        P("fsdp", "tensor"),
        P("tensor", "fsdp"),
        P("fsdp", "context", None),
    )
    return jax.shard_map(
        on_device,
        mesh=mesh,
        in_specs=placed,
        out_specs=(placed[0], placed[0]) + placed[2:20],
        check_vma=False,
    )
```

```python
import functools
import jax
import jax.numpy as jnp
from jax import lax
from jax.experimental import pallas as pl
from jax.experimental.pallas import tpu as pltpu
from jax.sharding import PartitionSpec as P

F32 = jnp.float32
BF16 = jnp.bfloat16
CHUNK = 128
exact = lax.Precision.HIGHEST
NN = ((1,), (0,))
NT = ((1,), (1,))
TN = ((0,), (0,))


def mm(a, b, dims=NN):
    return lax.dot_general(
        a.astype(BF16), b.astype(BF16), (dims, ((), ())), preferred_element_type=F32
    )


def mm_exact(a, b, dims=NN):
    return lax.dot_general(a, b, (dims, ((), ())), precision=exact, preferred_element_type=F32)


def small_cost():
    return pl.CostEstimate(flops=1, bytes_accessed=1, transcendentals=0)


def grid_ids(size):
    rows = lax.broadcasted_iota(jnp.int32, (size, size), 0)
    cols = lax.broadcasted_iota(jnp.int32, (size, size), 1)
    return rows, cols


def softplus(v):
    return jnp.maximum(v, 0.0) + jnp.log1p(jnp.exp(-jnp.abs(v)))


def rates_of(rates, params, heads, triangle):
    lanes = lax.broadcasted_iota(jnp.int32, rates.shape, 1)
    shifted = rates + params[1:2, :]
    scale = jnp.exp(params[0:1, :])
    logdecay = jnp.where(lanes < heads, -scale * softplus(shifted), 0.0)
    running = mm_exact(triangle, logdecay)
    last = running[CHUNK - 1 : CHUNK, :]
    return (
        jax.nn.sigmoid(rates),
        shifted,
        scale,
        logdecay,
        running,
        jnp.transpose(running),
        jnp.exp(running),
        jnp.exp(last - running),
        jnp.exp(last),
    )


def convolved(window, taps, rows):
    total = taps[0:1, :] * window[5 : 5 + rows, :]
    for j in range(1, 4):
        total = total + taps[j : j + 1, :] * window[5 + j : 5 + j + rows, :]
    return total


PER = 2


def inverses_of(systems, rows, cols):
    eye = (rows == cols).astype(F32)
    near = [jnp.where(rows // 8 == cols // 8, s, 0.0).astype(BF16) for s in systems]
    second = [mm(n, n) for n in near]
    low = [s.astype(BF16) for s in second]
    third = [mm(s, n) for s, n in zip(low, near)]
    fourth = [mm(s, s) for s in low]
    partial = [eye - n.astype(F32) + s - t for n, s, t in zip(near, second, third)]
    result = [p + mm(p, f) for p, f in zip(partial, fourth)]
    size = 8
    while size < CHUNK:
        step = min(4, CHUNK // size)
        inside = (rows // (step * size) == cols // (step * size)) & (rows // size > cols // size)
        off = [jnp.where(inside, s, 0.0).astype(BF16) for s in systems]
        low = [r.astype(BF16) for r in result]
        reach = [mm(o, r).astype(BF16) for o, r in zip(off, low)]
        twice = [mm(r, r) for r in reach]
        once = [r - mm(x, y) for r, x, y in zip(result, low, reach)]
        result = [o + mm(o, t) for o, t in zip(once, twice)]
        size *= step
    high = [s.astype(BF16) for s in systems]
    rest = [s - h.astype(F32) for s, h in zip(systems, high)]
    low = [r.astype(BF16) for r in result]
    tail = [r - x.astype(F32) for r, x in zip(result, low)]
    left = [
        eye - (r + mm(h, x) + mm(e, x) + mm(h, t))
        for r, h, x, e, t in zip(result, high, low, rest, tail)
    ]
    return [r + mm(x, d) for r, x, d in zip(result, low, left)]


def forward_kernel(heads, key_dim, val_dim, order_ref, *refs):
    pre_refs, refs = refs[:PER], refs[PER:]
    (
        taps_ref, params_ref, mixed_ref, states_ref, inverse_ref, new_ref, active_ref, sigma_ref,
        state, window,
    ) = refs
    step = pl.program_id(0)
    wide = heads * key_dim
    width = window.shape[1]
    span = PER * CHUNK

    @pl.when(step == 0)
    def _():
        state[...] = jnp.zeros_like(state)
        window[0:8, :] = jnp.zeros((8, width), F32)

    for c in range(PER):
        window[8 + c * CHUNK : 8 + (c + 1) * CHUNK, :] = (
            pre_refs[c][:, :width].astype(BF16).astype(F32)
        )
    summed = convolved(window, taps_ref, span)
    window[0:8, :] = window[span : span + 8, :]
    sigma = jax.nn.sigmoid(summed)
    active = summed * sigma
    active_ref[...] = active
    sigma_ref[...] = sigma
    rows, cols = grid_ids(CHUNK)
    causal = rows >= cols
    strict = rows > cols
    triangle = causal.astype(F32)
    rates = [rates_of(pre_refs[c][:, width:], params_ref, heads, triangle) for c in range(PER)]
    chains = [(c, h) for c in range(PER) for h in range(heads)]

    def piece(at, c, h, size):
        return active[c * CHUNK : (c + 1) * CHUNK, at + h * size : at + (h + 1) * size]

    def unit(values, factor):
        return values * (lax.rsqrt(jnp.sum(values * values, -1, keepdims=True) + 1e-6) * factor)

    query = [unit(piece(0, c, h, key_dim), key_dim ** -0.5) for c, h in chains]
    keys = [unit(piece(wide, c, h, key_dim), 1.0) for c, h in chains]
    values = [piece(2 * wide, c, h, val_dim) for c, h in chains]
    beta = [rates[c][0][:, heads + h : heads + h + 1] for c, h in chains]
    decay = [rates[c][6][:, h : h + 1] for c, h in chains]
    ratios = [
        jnp.where(
            causal,
            jnp.exp(jnp.where(causal, rates[c][4][:, h : h + 1] - rates[c][5][h : h + 1, :], 0.0)),
            0.0,
        )
        for c, h in chains
    ]
    dots = [mm(jnp.concatenate([k, q], 0), k, NT) for k, q in zip(keys, query)]
    systems = [
        jnp.where(strict, b * d[:CHUNK] * r, 0.0) for b, d, r in zip(beta, dots, ratios)
    ]
    scores = [(d[CHUNK:] * r).astype(BF16) for d, r in zip(dots, ratios)]
    inverse = [x.astype(BF16) for x in inverses_of(systems, rows, cols)]
    solved = [
        mm(x, jnp.concatenate([(b * e) * k, b * v], 1))
        for x, b, e, k, v in zip(inverse, beta, decay, keys, values)
    ]
    for i, (c, h) in enumerate(chains):
        inverse_ref[(c * heads + h) * CHUNK : (c * heads + h + 1) * CHUNK, :] = inverse[i]
    for c in range(PER):
        place = pl.multiple_of(order_ref[step * PER + c] * CHUNK, CHUNK)
        for h in range(heads):
            i = c * heads + h
            begin = state[h * key_dim : (h + 1) * key_dim, :]
            begin_low = begin.astype(BF16)
            states_ref[(c * heads + h) * key_dim : (c * heads + h + 1) * key_dim, :] = begin_low
            through = mm(
                jnp.concatenate([solved[i][:, :key_dim], query[i] * decay[i]], 0), begin_low
            )
            new = (solved[i][:, key_dim:] - through[:CHUNK]).astype(BF16)
            mixed_ref[pl.ds(place, CHUNK), h * val_dim : (h + 1) * val_dim] = through[
                CHUNK:
            ] + mm(scores[i], new)
            state[h * key_dim : (h + 1) * key_dim, :] = rates[c][8][:, h : h + 1] * begin + mm(
                keys[i] * rates[c][7][:, h : h + 1], new, TN
            )
            new_ref[c * CHUNK : (c + 1) * CHUNK, h * val_dim : (h + 1) * val_dim] = new


def backward_kernel(heads, key_dim, val_dim, order_ref, *refs):
    pre_refs, refs = refs[:PER], refs[PER:]
    active_ref, sigma_ref, taps_ref, params_ref, states_ref, inverse_ref, new_ref = refs[:7]
    mixed_refs, refs = refs[7 : 7 + PER], refs[7 + PER :]
    gates_refs, refs = refs[:PER], refs[PER:]
    own_refs, refs = refs[:PER], refs[PER:]
    other_refs, refs = refs[:PER], refs[PER:]
    (side_ref, gain_ref, d_pre_ref, d_taps_ref, d_params_ref, d_gain_ref, d_state, after) = (
        refs
    )
    step = pl.program_id(0)
    steps = pl.num_programs(0)
    wide = heads * key_dim
    width = after.shape[1]
    span = PER * CHUNK
    first = (steps - 1 - step) * PER

    @pl.when(step == 0)
    def _():
        d_state[...] = jnp.zeros_like(d_state)
        after[span : span + 8, :] = jnp.zeros((8, width), F32)
        d_taps_ref[...] = jnp.zeros_like(d_taps_ref)
        d_params_ref[...] = jnp.zeros_like(d_params_ref)
        d_gain_ref[...] = jnp.zeros_like(d_gain_ref)

    active = active_ref[...]
    sigma = sigma_ref[...]
    slope = sigma + active * (1.0 - sigma)
    rows, cols = grid_ids(CHUNK)
    causal = rows >= cols
    strict = rows > cols
    triangle = causal.astype(F32)
    rates = [rates_of(pre_refs[c][:, width:], params_ref, heads, triangle) for c in range(PER)]
    chains = [(c, h) for c in range(PER) for h in range(heads)]
    places = [pl.multiple_of(order_ref[first + c] * CHUNK, CHUNK) for c in range(PER)]
    d_attn = jnp.concatenate(
        [
            jnp.where(order_ref[first + c] < steps * PER // 2, own_refs[c][...], other_refs[c][...])
            for c in range(PER)
        ],
        0,
    )
    depth = side_ref.shape[2]
    d_heads = mm(d_attn[:, :depth], side_ref[0, 1])
    for f in range(1, side_ref.shape[0]):
        d_heads = d_heads + mm(d_attn[:, f * depth : (f + 1) * depth], side_ref[f, 1])
    gain = gain_ref[...]

    def piece(array, at, c, h, size):
        return array[c * CHUNK : (c + 1) * CHUNK, at + h * size : at + (h + 1) * size]

    def scale_of(values):
        return lax.rsqrt(jnp.sum(values * values, -1, keepdims=True) + 1e-6)

    q_act = [piece(active, 0, c, h, key_dim) for c, h in chains]
    k_act = [piece(active, wide, c, h, key_dim) for c, h in chains]
    values = [piece(active, 2 * wide, c, h, val_dim) for c, h in chains]
    q_scale = [scale_of(x) for x in q_act]
    k_scale = [scale_of(x) for x in k_act]
    q_unit = [x * s for x, s in zip(q_act, q_scale)]
    keys = [x * s for x, s in zip(k_act, k_scale)]
    query = [x * key_dim ** -0.5 for x in q_unit]
    keys_low = [x.astype(BF16) for x in keys]
    query_low = [x.astype(BF16) for x in query]
    beta = [rates[c][0][:, heads + h : heads + h + 1] for c, h in chains]
    decay = [rates[c][6][:, h : h + 1] for c, h in chains]
    remain = [rates[c][7][:, h : h + 1] for c, h in chains]
    whole = [rates[c][8][:, h : h + 1] for c, h in chains]
    lead = [b * e for b, e in zip(beta, decay)]
    ratios = [
        jnp.where(
            causal,
            jnp.exp(jnp.where(causal, rates[c][4][:, h : h + 1] - rates[c][5][h : h + 1, :], 0.0)),
            0.0,
        )
        for c, h in chains
    ]
    d_mixed = []
    for c, h in chains:
        at = slice(h * val_dim, (h + 1) * val_dim)
        mixed = mixed_refs[c][:, at]
        gates = gates_refs[c][:, at]
        d_out = piece(d_heads, 0, c, h, val_dim)
        m_scale = lax.rsqrt(jnp.mean(mixed * mixed, -1, keepdims=True) + 1e-5)
        unit = mixed * m_scale
        g_sigma = jax.nn.sigmoid(gates)
        gated = gates * g_sigma
        weighted = d_out * unit
        d_pre_ref[
            pl.ds(places[c], CHUNK), width + 128 + h * val_dim : width + 128 + (h + 1) * val_dim
        ] = (weighted * gain * (g_sigma * (1.0 + gates * (1.0 - g_sigma)))).astype(BF16)
        d_gain_ref[0:1, :] += jnp.sum(weighted * gated, 0, keepdims=True)
        d_unit = d_out * gated * gain
        d_mixed.append(
            (m_scale * (d_unit - unit * jnp.mean(d_unit * unit, -1, keepdims=True))).astype(BF16)
        )
    dots = [mm(jnp.concatenate([k, q], 0), k, NT) for k, q in zip(keys_low, query_low)]
    weights = [jnp.where(strict, d[:CHUNK] * r, 0.0) for d, r in zip(dots, ratios)]
    scores = [d[CHUNK:] * r for d, r in zip(dots, ratios)]
    begin = [
        states_ref[(c * heads + h) * key_dim : (c * heads + h + 1) * key_dim, :] for c, h in chains
    ]
    inverse = [
        inverse_ref[(c * heads + h) * CHUNK : (c * heads + h + 1) * CHUNK, :] for c, h in chains
    ]
    new = [
        new_ref[c * CHUNK : (c + 1) * CHUNK, h * val_dim : (h + 1) * val_dim] for c, h in chains
    ]
    straight = [mm(s, d, TN) for s, d in zip(scores, d_mixed)]
    kept = [(k * r).astype(BF16) for k, r in zip(keys, remain)]
    both = [mm(x, jnp.concatenate([s.astype(BF16), k], 1), TN) for x, s, k in zip(inverse, straight, kept)]
    fixed = [mm(q * e, d, TN) for q, e, d in zip(query, decay, d_mixed)]
    pull = [(l * k).astype(BF16) for l, k in zip(lead, keys)]
    d_end = [None] * len(chains)
    solved = [None] * len(chains)
    for c in reversed(range(PER)):
        for h in range(heads):
            i = c * heads + h
            at = slice(h * key_dim, (h + 1) * key_dim)
            d_end[i] = d_state[at, :]
            solved[i] = both[i][:, :val_dim] + mm(both[i][:, val_dim:], d_end[i])
            d_state[at, :] = whole[i] * d_end[i] + fixed[i] - mm(pull[i], solved[i], TN)
    end_low = [d.astype(BF16) for d in d_end]
    outer = [
        mm(jnp.concatenate([d, s.astype(BF16)], 0), jnp.concatenate([b, n], 0), NT)
        for d, s, b, n in zip(d_mixed, solved, begin, new)
    ]
    d_kept = [mm(n, d, NT) for n, d in zip(new, end_low)]
    d_scores = [jnp.where(causal, o[:CHUNK, key_dim:], 0.0) for o in outer]
    d_system = [jnp.where(strict, -o[CHUNK:, key_dim:], 0.0) for o in outer]
    d_dots_k = [d * (b * r) for d, b, r in zip(d_system, beta, ratios)]
    d_dots_q = [(d * r).astype(BF16) for d, r in zip(d_scores, ratios)]
    near = [
        mm(jnp.concatenate([q, (k + jnp.transpose(k)).astype(BF16)], 0), low)
        for q, k, low in zip(d_dots_q, d_dots_k, keys_low)
    ]
    far = [mm(q, low, TN) for q, low in zip(d_dots_q, query_low)]
    lanes = lax.broadcasted_iota(jnp.int32, (CHUNK, 128), 1)
    row_ids = lax.broadcasted_iota(jnp.int32, (CHUNK, 1), 0)
    d_running = [jnp.zeros((CHUNK, 128), F32) for _ in range(PER)]
    d_strengths = [jnp.zeros((CHUNK, 128), F32) for _ in range(PER)]
    for i, (c, h) in enumerate(chains):
        d_query_state = outer[i][:CHUNK, :key_dim]
        d_keys_state = outer[i][CHUNK:, :key_dim]
        d_query = decay[i] * d_query_state + near[i][:CHUNK]
        d_keys = near[i][CHUNK:] + far[i] - lead[i] * d_keys_state + remain[i] * d_kept[i]
        along = decay[i] * jnp.sum(keys[i] * d_keys_state, -1, keepdims=True)
        weighed = d_system[i] * weights[i]
        d_beta = (
            jnp.sum(solved[i] * values[i], -1, keepdims=True)
            - along
            + jnp.sum(weighed, -1, keepdims=True)
        )
        joint = weighed * beta[i] + d_scores[i] * scores[i]
        left = remain[i] * jnp.sum(keys[i] * d_kept[i], -1, keepdims=True)
        total = jnp.sum(left, 0, keepdims=True) + whole[i] * jnp.sum(
            jnp.sum(d_end[i] * begin[i].astype(F32), -1, keepdims=True), 0, keepdims=True
        )
        d_run = (
            jnp.sum(joint, -1, keepdims=True)
            - jnp.sum(jnp.transpose(joint), -1, keepdims=True)
            + decay[i] * jnp.sum(query[i] * d_query_state, -1, keepdims=True)
            - beta[i] * along
            - left
            + jnp.where(row_ids == CHUNK - 1, total, 0.0)
        )
        d_running[c] = jnp.where(lanes == h, d_run, d_running[c])
        d_strengths[c] = jnp.where(lanes == heads + h, d_beta, d_strengths[c])
        d_q = d_query * key_dim ** -0.5
        d_q = q_scale[i] * (d_q - q_unit[i] * jnp.sum(q_unit[i] * d_q, -1, keepdims=True))
        d_k = k_scale[i] * (d_keys - keys[i] * jnp.sum(keys[i] * d_keys, -1, keepdims=True))
        here = slice(c * CHUNK, (c + 1) * CHUNK)
        after[here, h * key_dim : (h + 1) * key_dim] = d_q * piece(slope, 0, c, h, key_dim)
        after[here, wide + h * key_dim : wide + (h + 1) * key_dim] = d_k * piece(
            slope, wide, c, h, key_dim
        )
        after[here, 2 * wide + h * val_dim : 2 * wide + (h + 1) * val_dim] = (
            beta[i] * solved[i]
        ) * piece(slope, 2 * wide, c, h, val_dim)
    upper = (rows <= cols).astype(F32)
    for c in range(PER):
        strengths, shifted, scale, logdecay = rates[c][:4]
        d_logdecay = mm_exact(upper, d_running[c])
        d_shifted = jnp.where(lanes < heads, d_logdecay * (-scale) * jax.nn.sigmoid(shifted), 0.0)
        d_params_ref[0:1, :] += jnp.sum(d_logdecay * logdecay, 0, keepdims=True)
        d_params_ref[1:2, :] += jnp.sum(d_shifted, 0, keepdims=True)
        d_pre_ref[pl.ds(places[c], CHUNK), width : width + 128] = (
            d_shifted + d_strengths[c] * strengths * (1.0 - strengths)
        ).astype(BF16)
    total = None
    pre = jnp.concatenate([ref[:, :width].astype(BF16).astype(F32) for ref in pre_refs], 0)
    for j in range(4):
        shifted = after[3 - j : 3 - j + span, :]
        term = taps_ref[j : j + 1, :] * shifted
        total = term if total is None else total + term
        d_taps_ref[j : j + 1, :] += jnp.sum(pre * shifted, 0, keepdims=True)
    for c in range(PER):
        d_pre_ref[pl.ds(places[c], CHUNK), :width] = total[c * CHUNK : (c + 1) * CHUNK].astype(BF16)
    after[span : span + 8, :] = after[0:8, :]


def mixer_forward(order, pre, taps, params, heads, key_dim, val_dim):
    chunks = pre.shape[0] // CHUNK
    width = taps.shape[1]
    here = lambda c: lambda n, order: (order[n * PER + c], 0)
    plain = lambda n, order: (n, 0)
    fixed = lambda n, order: (0, 0)
    return pl.pallas_call(
        functools.partial(forward_kernel, heads, key_dim, val_dim),
        grid_spec=pltpu.PrefetchScalarGridSpec(
            num_scalar_prefetch=1,
            grid=(chunks // PER,),
            in_specs=[pl.BlockSpec((CHUNK, pre.shape[1]), here(c)) for c in range(PER)]
            + [pl.BlockSpec(taps.shape, fixed), pl.BlockSpec(params.shape, fixed)],
            out_specs=[
                pl.BlockSpec((pre.shape[0], heads * val_dim), fixed),
                pl.BlockSpec((PER * heads * key_dim, val_dim), plain),
                pl.BlockSpec((PER * heads * CHUNK, CHUNK), plain),
                pl.BlockSpec((PER * CHUNK, heads * val_dim), plain),
                pl.BlockSpec((PER * CHUNK, width), plain),
                pl.BlockSpec((PER * CHUNK, width), plain),
            ],
            scratch_shapes=[
                pltpu.VMEM((heads * key_dim, val_dim), F32),
                pltpu.VMEM((PER * CHUNK + 8, width), F32),
            ],
        ),
        out_shape=[
            jax.ShapeDtypeStruct((pre.shape[0], heads * val_dim), F32),
            jax.ShapeDtypeStruct((chunks * heads * key_dim, val_dim), BF16),
            jax.ShapeDtypeStruct((chunks * heads * CHUNK, CHUNK), BF16),
            jax.ShapeDtypeStruct((pre.shape[0], heads * val_dim), BF16),
            jax.ShapeDtypeStruct((pre.shape[0], width), F32),
            jax.ShapeDtypeStruct((pre.shape[0], width), F32),
        ],
        compiler_params=pltpu.CompilerParams(vmem_limit_bytes=48 * 2**20),
        cost_estimate=small_cost(),
        name="mixer_forward",
    )(order, *[pre] * PER, taps, params)


def mixer_backward(
    order, pre, active, sigma, taps, params, states, inverses, news, mixed, gates, d_own, d_other,
    side, gain, heads, key_dim, val_dim,
):
    chunks = pre.shape[0] // CHUNK
    width = taps.shape[1]
    out_width = heads * val_dim
    steps = chunks // PER
    half = chunks // 2
    at = lambda n, c, order: order[(steps - 1 - n) * PER + c]
    here = lambda c: lambda n, order: (at(n, c, order), 0)
    first = lambda c: lambda n, order: (jnp.minimum(at(n, c, order), half - 1), 0)
    second = lambda c: lambda n, order: (jnp.maximum(at(n, c, order) - half, 0), 0)
    plain = lambda n, order: (steps - 1 - n, 0)
    fixed = lambda n, order: (0, 0)
    each = lambda shape, place: [pl.BlockSpec(shape, place(c)) for c in range(PER)]
    return pl.pallas_call(
        functools.partial(backward_kernel, heads, key_dim, val_dim),
        grid_spec=pltpu.PrefetchScalarGridSpec(
            num_scalar_prefetch=1,
            grid=(steps,),
            in_specs=each((CHUNK, pre.shape[1]), here)
            + [
                pl.BlockSpec((PER * CHUNK, width), plain),
                pl.BlockSpec((PER * CHUNK, width), plain),
                pl.BlockSpec(taps.shape, fixed),
                pl.BlockSpec(params.shape, fixed),
                pl.BlockSpec((PER * heads * key_dim, val_dim), plain),
                pl.BlockSpec((PER * heads * CHUNK, CHUNK), plain),
                pl.BlockSpec((PER * CHUNK, out_width), plain),
            ]
            + each((CHUNK, out_width), here)
            + each((CHUNK, out_width), here)
            + each((CHUNK, d_own.shape[1]), first)
            + each((CHUNK, d_own.shape[1]), second)
            + [
                pl.BlockSpec(side.shape, lambda n, order: (0, 0, 0, 0)),
                pl.BlockSpec((1, val_dim), fixed),
            ],
            out_specs=[
                pl.BlockSpec((pre.shape[0], pre.shape[1] + out_width), fixed),
                pl.BlockSpec((8, width), fixed),
                pl.BlockSpec((8, 128), fixed),
                pl.BlockSpec((8, val_dim), fixed),
            ],
            scratch_shapes=[
                pltpu.VMEM((heads * key_dim, val_dim), F32),
                pltpu.VMEM((PER * CHUNK + 8, width), F32),
            ],
        ),
        out_shape=[
            jax.ShapeDtypeStruct((pre.shape[0], pre.shape[1] + out_width), BF16),
            jax.ShapeDtypeStruct((8, width), F32),
            jax.ShapeDtypeStruct((8, 128), F32),
            jax.ShapeDtypeStruct((8, val_dim), F32),
        ],
        compiler_params=pltpu.CompilerParams(vmem_limit_bytes=56 * 2**20),
        cost_estimate=small_cost(),
        name="mixer_backward",
    )(
        order, *[pre] * PER, active, sigma, taps, params, states, inverses, news, *[mixed] * PER,
        *[gates] * PER, *[d_own] * PER, *[d_other] * PER, side, gain,
    )


def roomy():
    return dict(
        compiler_params=pltpu.CompilerParams(vmem_limit_bytes=56 * 2**20),
        cost_estimate=small_cost(),
    )


def pack_mix_kernel(heads, core_ref, q_ref, k_ref, v_ref, decay_ref, strength_ref, out_ref):
    first = core_ref[0] == 0
    wide, tall = q_ref.shape[1], v_ref.shape[1]
    out_ref[:, :wide] = q_ref[...]
    out_ref[:, wide : 2 * wide] = k_ref[...]
    out_ref[:, 2 * wide : 2 * wide + tall] = v_ref[...]

    rates = jnp.transpose(
        jnp.concatenate([decay_ref[...].astype(F32), strength_ref[...].astype(F32)], 0)
    )
    pick = lambda at: jnp.where(
        first, rates[:, at : at + heads], rates[:, at + heads : at + 2 * heads]
    )
    rows = out_ref.shape[0]
    out_ref[:, 2 * wide + tall :] = jnp.concatenate(
        [pick(0), pick(2 * heads), jnp.zeros((rows, 128 - 2 * heads), F32)], 1
    ).astype(BF16)


def pack_mix(core, heads, w_query, w_key, w_value, w_decay, w_strength):
    depth = w_query.shape[0]
    wide, tall = w_query.shape[1] // 2, w_value.shape[1] // 2
    here = lambda i, core: (0, core[0])
    fixed = lambda i, core: (0, 0)
    return pl.pallas_call(
        functools.partial(pack_mix_kernel, heads),
        grid_spec=pltpu.PrefetchScalarGridSpec(
            num_scalar_prefetch=1,
            grid=(1,),
            in_specs=[
                pl.BlockSpec((depth, wide), here),
                pl.BlockSpec((depth, wide), here),
                pl.BlockSpec((depth, tall), here),
                pl.BlockSpec(w_decay.shape[::-1], fixed),
                pl.BlockSpec(w_strength.shape[::-1], fixed),
            ],
            out_specs=pl.BlockSpec((depth, 2 * wide + tall + 128), fixed),
        ),
        out_shape=jax.ShapeDtypeStruct((depth, 2 * wide + tall + 128), BF16),
        name="pack_mix",
        **roomy(),
    )(core, w_query, w_key, w_value, w_decay.T, w_strength.T)


def pack_rest_kernel(core_ref, outgate_ref, out_ref, gate_ref, up_ref, down_ref, side_ref, wide_ref):
    first = core_ref[0] == 0
    depth = outgate_ref.shape[0]
    units = gate_ref.shape[1] // 2
    side_ref[:depth, :] = outgate_ref[...]
    side_ref[depth:, :] = jnp.transpose(out_ref[...].astype(F32)).astype(BF16)
    for at, ref in ((0, gate_ref), (1, up_ref)):
        values = ref[...]
        wide_ref[at * depth : (at + 1) * depth, :] = jnp.where(
            first, values[:, :units], values[:, units:]
        )
    wide_ref[2 * depth :, :] = jnp.transpose(down_ref[...].astype(F32)).astype(BF16)


def pack_rest(core, w_outgate, w_out, w_gate, w_up, w_down):
    depth = w_outgate.shape[0]
    tall, units = w_outgate.shape[1] // 2, w_gate.shape[1] // 2
    fixed = lambda i, core: (0, 0)
    return pl.pallas_call(
        pack_rest_kernel,
        grid_spec=pltpu.PrefetchScalarGridSpec(
            num_scalar_prefetch=1,
            grid=(1,),
            in_specs=[
                pl.BlockSpec((depth, tall), lambda i, core: (0, core[0])),
                pl.BlockSpec((tall, depth), lambda i, core: (core[0], 0)),
                pl.BlockSpec(w_gate.shape, fixed),
                pl.BlockSpec(w_up.shape, fixed),
                pl.BlockSpec((units, depth), lambda i, core: (core[0], 0)),
            ],
            out_specs=[
                pl.BlockSpec((2 * depth, tall), fixed),
                pl.BlockSpec((3 * depth, units), fixed),
            ],
        ),
        out_shape=[
            jax.ShapeDtypeStruct((2 * depth, tall), BF16),
            jax.ShapeDtypeStruct((3 * depth, units), BF16),
        ],
        name="pack_rest",
        **roomy(),
    )(core, w_outgate, w_out, w_gate, w_up, w_down)


def arrange_kernel(scalars_ref, tokens_ref, cotangent_ref, gain_ref, normed_ref, branch_ref):
    step = pl.program_id(0)
    rows = tokens_ref.shape[0]
    tokens = tokens_ref[...].astype(F32)
    scale = lax.rsqrt(jnp.mean(tokens * tokens, -1, keepdims=True) + 1e-6)
    normed_ref[...] = (tokens * scale * gain_ref[...]).astype(BF16)
    place = scalars_ref[0] + scalars_ref[2 + step] * rows + lax.broadcasted_iota(
        jnp.int32, (rows, 1), 0
    )
    branch_ref[...] = jnp.where(place < scalars_ref[1], cotangent_ref[...], 0).astype(BF16)


def arrange(scalars, tokens, cotangent, gain, layers):
    rows, model = tokens.shape[0] // layers, tokens.shape[1]
    there = pl.BlockSpec((rows, model), lambda p, scalars: (scalars[2 + p], 0))
    plain = pl.BlockSpec((rows, model), lambda p, scalars: (p, 0))
    return pl.pallas_call(
        arrange_kernel,
        grid_spec=pltpu.PrefetchScalarGridSpec(
            num_scalar_prefetch=1,
            grid=(layers,),
            in_specs=[there, there, pl.BlockSpec((1, model), lambda p, scalars: (0, 0))],
            out_specs=[plain, plain],
        ),
        out_shape=[jax.ShapeDtypeStruct(tokens.shape, BF16)] * 2,
        name="arrange",
        **roomy(),
    )(scalars, tokens, cotangent, gain)


TILE = 256


def heads_kernel(
    heads, normed_ref, mixed_ref, side_ref, gain_ref, gates_ref, heads_ref, other_ref, own_ref
):
    step = pl.program_id(0)
    half = pl.num_programs(0) // 2
    shards, _, depth, tall = side_ref.shape
    val_dim = tall // heads
    gates = mm(normed_ref[:, :depth], side_ref[0, 0])
    for f in range(1, shards):
        gates = gates + mm(normed_ref[:, f * depth : (f + 1) * depth], side_ref[f, 0])
    gates_ref[...] = gates
    for h in range(heads):
        at = slice(h * val_dim, (h + 1) * val_dim)
        mixed = mixed_ref[:, at]
        gate = gates[:, at]
        scale = lax.rsqrt(jnp.mean(mixed * mixed, -1, keepdims=True) + 1e-5)
        heads_ref[:, at] = (
            mixed * scale * gain_ref[...] * (gate * jax.nn.sigmoid(gate))
        ).astype(BF16)
    low = heads_ref[...]

    def write(ref):
        for f in range(shards):
            ref[:, f * depth : (f + 1) * depth] = mm(low, side_ref[f, 1], NT).astype(BF16)

    @pl.when(step < half)
    def _():
        write(other_ref)

    @pl.when(step >= half)
    def _():
        write(own_ref)


def turned_specs(tiles):
    half = tiles // 2
    here = lambda i: (jnp.where(i < half, i + half, i - half), 0)
    other = lambda i: (jnp.minimum(i, half - 1), 0)
    own = lambda i: (jnp.maximum(i - half, 0), 0)
    return here, other, own


def head_outputs(normed, mixed, side, gain, heads):
    count, model = normed.shape
    tall = mixed.shape[1]
    here, other, own = turned_specs(count // TILE)
    return pl.pallas_call(
        functools.partial(heads_kernel, heads),
        grid=(count // TILE,),
        in_specs=[
            pl.BlockSpec((TILE, model), here),
            pl.BlockSpec((TILE, tall), here),
            pl.BlockSpec(side.shape, lambda i: (0, 0, 0, 0)),
            pl.BlockSpec(gain.shape, lambda i: (0, 0)),
        ],
        out_specs=[
            pl.BlockSpec((TILE, tall), here),
            pl.BlockSpec((TILE, tall), here),
            pl.BlockSpec((TILE, model), other),
            pl.BlockSpec((TILE, model), own),
        ],
        out_shape=[
            jax.ShapeDtypeStruct((count, tall), F32),
            jax.ShapeDtypeStruct((count, tall), BF16),
            jax.ShapeDtypeStruct((count // 2, model), BF16),
            jax.ShapeDtypeStruct((count // 2, model), BF16),
        ],
        name="head_outputs",
        **roomy(),
    )(normed, mixed, side, gain)


def feed_kernel(hidden_ref, branch_ref, wide_ref, stack_ref, d_hidden_ref, branch_out_ref):
    shards, _, depth, units = wide_ref.shape

    def forward(ref, at):
        total = mm(ref[:, :depth], wide_ref[0, at])
        for f in range(1, shards):
            total = total + mm(ref[:, f * depth : (f + 1) * depth], wide_ref[f, at])
        return total

    gate = forward(hidden_ref, 0)
    up = forward(hidden_ref, 1)
    d_act = forward(branch_ref, 2)
    sigma = jax.nn.sigmoid(gate)
    silu = gate * sigma
    act = (silu * up).astype(BF16)
    d_gate = (d_act * up * (sigma + silu * (1.0 - sigma))).astype(BF16)
    d_up = (d_act * silu).astype(BF16)
    stack_ref[0] = d_gate
    stack_ref[1] = d_up
    stack_ref[2] = act
    for f in range(shards):
        at = slice(f * depth, (f + 1) * depth)
        d_hidden_ref[:, at] = (
            mm(d_gate, wide_ref[f, 0], NT) + mm(d_up, wide_ref[f, 1], NT)
        ).astype(BF16)
        branch_out_ref[:, at] = mm(act, wide_ref[f, 2], NT).astype(BF16)


def feed_forward(hidden, branch, wide):
    count, model = hidden.shape
    units = wide.shape[3]
    row = pl.BlockSpec((TILE, model), lambda i: (i, 0))
    return pl.pallas_call(
        feed_kernel,
        grid=(count // TILE,),
        in_specs=[row, row, pl.BlockSpec(wide.shape, lambda i: (0, 0, 0, 0))],
        out_specs=[pl.BlockSpec((3, TILE, units), lambda i: (0, i, 0)), row, row],
        out_shape=[
            jax.ShapeDtypeStruct((3, count, units), BF16),
            jax.ShapeDtypeStruct((count, model), BF16),
            jax.ShapeDtypeStruct((count, model), BF16),
        ],
        name="feed_forward",
        **roomy(),
    )(hidden, branch, wide)


def feed_grads_kernel(h_own, h_other, b_own, b_other, s_own, s_other, out_ref):
    units = s_own.shape[2]
    for at, own, other in ((0, h_own, h_other), (1, h_own, h_other), (2, b_own, b_other)):
        out_ref[:, at * units : (at + 1) * units] = (
            mm(own[...], s_own[at], TN) + mm(other[...], s_other[at], TN)
        ).astype(BF16)
    rest = out_ref.shape[1] - 3 * units
    if rest:
        out_ref[:, 3 * units :] = jnp.zeros((out_ref.shape[0], rest), BF16)


def feed_grads(hidden, branch, stacks, shards):
    count, model = hidden[0].shape
    units = stacks[0].shape[2]
    depth = model // shards
    width = -(-3 * units // 128) * 128
    part = pl.BlockSpec((count, depth), lambda f: (0, f))
    use_s = pl.BlockSpec((3, count, units), lambda f: (0, 0, 0))
    return pl.pallas_call(
        feed_grads_kernel,
        grid=(shards,),
        in_specs=[part, part, part, part, use_s, use_s],
        out_specs=pl.BlockSpec((depth, width), lambda f: (f, 0)),
        out_shape=jax.ShapeDtypeStruct((model, width), BF16),
        name="feed_grads",
        **roomy(),
    )(*hidden, *branch, *stacks)


def d_normed_kernel(side_at, mix_ref, normed_ref, weights_ref, side_ref, other_ref, own_ref, sum_ref):
    step = pl.program_id(0)
    half = pl.num_programs(0) // 2
    shards, _, depth, _ = side_ref.shape

    @pl.when(step == 0)
    def _():
        sum_ref[...] = jnp.zeros_like(sum_ref)

    def write(ref):
        for f in range(shards):
            at = slice(f * depth, (f + 1) * depth)
            part = mm(mix_ref[:, :side_at], weights_ref[at, :], NT) + mm(
                mix_ref[:, side_at:], side_ref[f, 0], NT
            )
            ref[:, at] = part.astype(BF16)
            sum_ref[0:1, at] += jnp.sum(part * normed_ref[:, at].astype(F32), 0, keepdims=True)

    @pl.when(step < half)
    def _():
        write(other_ref)

    @pl.when(step >= half)
    def _():
        write(own_ref)


def d_normed_rows(d_mix, normed, weights, side):
    count, model = normed.shape
    here, other, own = turned_specs(count // TILE)
    fixed = lambda i: (0, 0)
    return pl.pallas_call(
        functools.partial(d_normed_kernel, weights.shape[1]),
        grid=(count // TILE,),
        in_specs=[
            pl.BlockSpec((TILE, d_mix.shape[1]), here),
            pl.BlockSpec((TILE, model), here),
            pl.BlockSpec(weights.shape, fixed),
            pl.BlockSpec(side.shape, lambda i: (0, 0, 0, 0)),
        ],
        out_specs=[
            pl.BlockSpec((TILE, model), other),
            pl.BlockSpec((TILE, model), own),
            pl.BlockSpec((8, model), fixed),
        ],
        out_shape=[
            jax.ShapeDtypeStruct((count // 2, model), BF16),
            jax.ShapeDtypeStruct((count // 2, model), BF16),
            jax.ShapeDtypeStruct((8, model), F32),
        ],
        name="d_normed_rows",
        **roomy(),
    )(d_mix, normed, weights, side)


def mix_grads_kernel(normed_ref, mix_ref, out_ref):
    out_ref[...] = mm(normed_ref[...], mix_ref[...], TN).astype(BF16)


def mix_grads(normed, d_mix, shards):
    count, model = normed.shape
    depth, width = model // shards, d_mix.shape[1]
    return pl.pallas_call(
        mix_grads_kernel,
        grid=(shards,),
        in_specs=[
            pl.BlockSpec((count, depth), lambda f: (0, f)),
            pl.BlockSpec(d_mix.shape, lambda f: (0, 0)),
        ],
        out_specs=pl.BlockSpec((depth, width), lambda f: (f, 0)),
        out_shape=jax.ShapeDtypeStruct((model, width), BF16),
        name="mix_grads",
        **roomy(),
    )(normed, d_mix)


def out_grads_kernel(d_own_ref, d_other_ref, heads_ref, out_ref):
    half = d_own_ref.shape[0]
    out_ref[...] = (
        mm(d_own_ref[...], heads_ref[:half, :], TN) + mm(d_other_ref[...], heads_ref[half:, :], TN)
    ).astype(BF16)


def out_grads(d_own, d_other, heads_out, shards):
    count, model = d_own.shape
    depth, width = model // shards, heads_out.shape[1]
    column = pl.BlockSpec((count, depth), lambda f: (0, f))
    return pl.pallas_call(
        out_grads_kernel,
        grid=(shards,),
        in_specs=[column, column, pl.BlockSpec(heads_out.shape, lambda f: (0, 0))],
        out_specs=pl.BlockSpec((depth, width), lambda f: (f, 0)),
        out_shape=jax.ShapeDtypeStruct((model, width), BF16),
        name="out_grads",
        **roomy(),
    )(d_own, d_other, heads_out)


def place_kernel(turns_ref, *refs):
    parts, out_ref = refs[:-1], refs[-1]
    size = turns_ref.shape[0]
    rows = parts[0].shape[0]
    for p in range(size):
        at = pl.multiple_of(turns_ref[p] * rows, rows)
        if len(parts) == size:
            part = parts[p][...]
        elif p == 0:
            part = parts[0][...]
        else:
            part = parts[p][...] + parts[2 * size - 1 - p][...]
        out_ref[pl.ds(at, rows), :] = part


def place(turns, parts):
    size = turns.shape[0]
    rows, model = parts[0].shape
    whole = lambda i, turns: (0, 0)
    return pl.pallas_call(
        place_kernel,
        grid_spec=pltpu.PrefetchScalarGridSpec(
            num_scalar_prefetch=1,
            grid=(1,),
            in_specs=[pl.BlockSpec((rows, model), whole)] * len(parts),
            out_specs=pl.BlockSpec((size * rows, model), whole),
        ),
        out_shape=jax.ShapeDtypeStruct((size * rows, model), BF16),
        name="place",
        **roomy(),
    )(turns, *parts)


def finish_wide_kernel(
    units, core_ref, own_ref, other_ref, out_own_ref, out_other_ref, gate_ref, up_ref, down_ref,
    out_ref,
):
    first = core_ref[0] == 0

    def pair(a, b):
        own, other = a[...].astype(F32), b[...].astype(F32)
        return jnp.where(first, own, other), jnp.where(first, other, own)

    low, high = pair(own_ref, other_ref)
    for at, ref in ((0, gate_ref), (1, up_ref)):
        ref[:, :units] = low[:, at * units : (at + 1) * units]
        ref[:, units:] = high[:, at * units : (at + 1) * units]
    down_ref[:units, :] = jnp.transpose(low[:, 2 * units : 3 * units])
    down_ref[units:, :] = jnp.transpose(high[:, 2 * units : 3 * units])
    low, high = pair(out_own_ref, out_other_ref)
    tall = low.shape[1]
    out_ref[:tall, :] = jnp.transpose(low)
    out_ref[tall:, :] = jnp.transpose(high)


def finish_wide(core, own, other, out_own, out_other, units):
    depth, width = own.shape
    tall = out_own.shape[1]
    row = lambda size: pl.BlockSpec((128, size), lambda i, core: (i, 0))
    column = lambda size: pl.BlockSpec((size, 128), lambda i, core: (0, i))
    return pl.pallas_call(
        functools.partial(finish_wide_kernel, units),
        grid_spec=pltpu.PrefetchScalarGridSpec(
            num_scalar_prefetch=1,
            grid=(depth // 128,),
            in_specs=[row(width), row(width), row(tall), row(tall)],
            out_specs=[row(2 * units), row(2 * units), column(2 * units), column(2 * tall)],
        ),
        out_shape=[
            jax.ShapeDtypeStruct((depth, 2 * units), F32),
            jax.ShapeDtypeStruct((depth, 2 * units), F32),
            jax.ShapeDtypeStruct((2 * units, depth), F32),
            jax.ShapeDtypeStruct((2 * tall, depth), F32),
        ],
        name="finish_wide",
        **roomy(),
    )(core, own, other, out_own, out_other)


def finish_mix_kernel(cuts, core_ref, a_ref, b_ref, *refs):
    first = core_ref[0] == 0
    own, other = a_ref[...].astype(F32), b_ref[...].astype(F32)
    low, high = jnp.where(first, own, other), jnp.where(first, other, own)
    for (begin, size), ref in zip(cuts, refs):
        ref[:, :size] = low[:, begin : begin + size]
        ref[:, size:] = high[:, begin : begin + size]


def finish_mix(core, own, other, cuts):
    depth, width = own.shape
    row = lambda size: pl.BlockSpec((128, size), lambda i, core: (i, 0))
    return pl.pallas_call(
        functools.partial(finish_mix_kernel, cuts),
        grid_spec=pltpu.PrefetchScalarGridSpec(
            num_scalar_prefetch=1,
            grid=(depth // 128,),
            in_specs=[row(width), row(width)],
            out_specs=[row(2 * size) for _, size in cuts],
        ),
        out_shape=[jax.ShapeDtypeStruct((depth, 2 * size), F32) for _, size in cuts],
        name="finish_mix",
        **roomy(),
    )(core, own, other)


def after(value, *others):
    return lax.optimization_barrier((value,) + others)[0]


def is_square(axis):
    return lax.axis_size(axis) == 4


def across(value, flip):
    return lax.ppermute(value, "fsdp", [(i, i ^ flip) for i in range(4)])


def swapped(value):
    return lax.ppermute(value, "context", [(0, 1), (1, 0)])


def gathered_rows(own, beside):
    if not is_square("fsdp"):
        return lax.all_gather(own, "fsdp", axis=0, tiled=True), beside
    rows = own.shape[0]
    half = rows // 2
    along_x = across(own, 1)
    along_y = across(own, 2)
    along_x, along_y, beside = lax.optimization_barrier((along_x, along_y, beside))
    low = across(along_x[:half], 2)
    high = across(along_y[half:], 1)
    shard = lax.axis_index("fsdp")
    whole = jnp.zeros((4 * rows,) + own.shape[1:], own.dtype)
    for place, part in ((0, own), (1, along_x), (2, along_y)):
        whole = lax.dynamic_update_slice_in_dim(whole, part, (shard ^ place) * rows, 0)
    whole = lax.dynamic_update_slice_in_dim(whole, low, (shard ^ 3) * rows, 0)
    return lax.dynamic_update_slice_in_dim(whole, high, (shard ^ 3) * rows + half, 0), beside


def scattered(blocks):
    return lax.psum_scatter(blocks, "fsdp", scatter_dimension=0, tiled=True)


def line_sum(value, beside=(), axis="tensor"):
    size = lax.axis_size(axis)
    rows = value.shape[0] // size
    parts = [
        lax.ppermute(
            value[p * rows : (p + 1) * rows], axis, [(i, (i - p) % size) for i in range(size)]
        )
        for p in range(1, size)
    ]
    if beside:
        parts, beside = lax.optimization_barrier((parts, tuple(beside)))
    total = value[:rows].astype(F32)
    for part in parts:
        total = total + part.astype(F32)
    return (total, *beside) if beside else total


def line_sum_hops(value, axis="tensor"):
    size = lax.axis_size(axis)
    rows = value.shape[0] // size
    block = lambda p: value[p * rows : (p + 1) * rows].astype(F32)
    right = left = None
    for step in range(1, size):
        send_r, send_l = block(step), block(size - step)
        if right is not None:
            send_r = send_r + right.astype(F32)
            send_l = send_l + left.astype(F32)
        right = lax.ppermute(send_r.astype(BF16), axis, [(i, i + 1) for i in range(step)])
        left = lax.ppermute(
            send_l.astype(BF16), axis, [(i, i - 1) for i in range(size - step, size)]
        )
    return block(0) + right.astype(F32) + left.astype(F32)


def line_gather(own, axis="tensor"):
    size = lax.axis_size(axis)
    rights, lefts = [own], [own]
    for step in range(1, size):
        rights.append(
            lax.ppermute(rights[-1], axis, [(i, i + 1) for i in range(step - 1, size - 1)])
        )
        lefts.append(lax.ppermute(lefts[-1], axis, [(i, i - 1) for i in range(1, size - step + 1)]))
    return [own] + [rights[k] + lefts[size - k] for k in range(1, size)]


def line_hop(right, left, step, axis="tensor"):
    size = lax.axis_size(axis)
    return (
        lax.ppermute(right, axis, [(i, i + 1) for i in range(step - 1, size - 1)]),
        lax.ppermute(left, axis, [(i, i - 1) for i in range(1, size - step + 1)]),
    )


def flat(hops):
    return [hops[0][0]] + [hop[0] for hop in hops[1:]] + [hop[1] for hop in hops[1:]]


def line_total(value, axis="tensor"):
    size = lax.axis_size(axis)
    step = 1
    while step < size:
        value = value + lax.ppermute(value, axis, [(i, i ^ step) for i in range(size)])
        step *= 2
    return value


def core_sum(other_rows, own_rows):
    return (own_rows.astype(F32) + swapped(other_rows).astype(F32)).astype(BF16)


def dot(a, b, dims=NN):
    return lax.dot_general(a, b, (dims, ((), ())), preferred_element_type=F32)


def norm_parts(values, epsilon):
    return lax.rsqrt(jnp.mean(values * values, -1, keepdims=True) + epsilon)


def norm_back(d_scaled, values, scale, gain):
    raised = d_scaled * gain
    return scale * raised - values * (
        scale * scale * scale * jnp.mean(raised * values, -1, keepdims=True)
    )


def on_device(
    inputs, lengths, norm_attn, w_query, w_key, w_value, w_decay, w_strength, decay_log,
    decay_bias, conv_query, conv_key, conv_value, w_outgate, norm_head, w_out, norm_mlp, w_gate,
    w_up, w_down, cotangent,
):
    shard, core, layer = (lax.axis_index(name) for name in ("fsdp", "context", "tensor"))
    shards, layers = lax.axis_size("fsdp"), lax.axis_size("tensor")
    seg, model = inputs.shape[1:]
    rows = seg // layers
    depth = norm_attn.shape[0]
    all_heads, taps_count, key_part = conv_query.shape
    val_part = conv_value.shape[2]
    heads = all_heads // 2
    key_dim, val_dim = key_part * shards, val_part * shards
    wide, tall = heads * key_dim, heads * val_dim
    width = 2 * wide + tall
    units = w_gate.shape[1] // 2

    def mine(array, dim):
        size = array.shape[dim] // 2
        first = lax.slice_in_dim(array, 0, size, axis=dim)
        second = lax.slice_in_dim(array, size, 2 * size, axis=dim)
        return jnp.where(core == 0, first, second)

    core_id = core.reshape(1).astype(jnp.int32)
    own_mix = pack_mix(core_id, heads, w_query, w_key, w_value, w_decay, w_strength)

    pieces = (
        norm_attn, norm_mlp, norm_head,
        mine(conv_query, 0).reshape(-1), mine(conv_key, 0).reshape(-1),
        mine(conv_value, 0).reshape(-1),
    )
    small = after(jnp.concatenate(pieces), own_mix)
    if is_square("fsdp"):
        stack = jnp.stack([small, across(small, 1), across(small, 2), across(small, 3)])
        stack = jnp.stack([lax.dynamic_index_in_dim(stack, shard ^ i, 0, False) for i in range(4)])
    else:
        stack = lax.all_gather(small, "fsdp")
    cuts = [0]
    for piece in pieces:
        cuts.append(cuts[-1] + piece.shape[0])
    gain_attn = stack[:, cuts[0] : cuts[1]].reshape(1, model).astype(F32)
    gain_mlp = stack[:, cuts[1] : cuts[2]].reshape(1, model).astype(F32)
    gain_head = stack[:, cuts[2] : cuts[3]].reshape(1, val_dim).astype(F32)

    def taps_of(at, part):
        array = stack[:, cuts[at] : cuts[at + 1]].reshape(shards, heads, taps_count, part)
        return jnp.transpose(array, (2, 1, 0, 3)).reshape(taps_count, -1)

    taps = jnp.concatenate([taps_of(3, key_part), taps_of(4, key_part), taps_of(5, val_part)], 1)
    taps = jnp.pad(taps.astype(F32), ((0, 8 - taps_count), (0, 0)))
    params = jnp.pad(
        jnp.stack([mine(decay_log, 0), mine(decay_bias, 0)]).astype(F32),
        ((0, 6), (0, 128 - heads)),
    )

    turns = (layer - jnp.arange(layers, dtype=jnp.int32)) % layers
    scalars = jnp.concatenate([(core * seg).reshape(1), lengths[:1], turns]).astype(jnp.int32)
    per_core, per_block = seg // CHUNK, rows // CHUNK
    ids = jnp.arange(2 * per_core, dtype=jnp.int32)
    within = ids % per_core
    order = (
        jnp.where(ids // per_core == core, 0, per_core)
        + ((layer - within // per_block) % layers) * per_block
        + within % per_block
    ).astype(jnp.int32)
    live_own = (
        core * seg + layer * rows + jnp.arange(rows, dtype=jnp.int32) < lengths[0]
    ).astype(F32)[:, None]
    tokens_own = lax.dynamic_slice_in_dim(inputs[0], layer * rows, rows, 0).astype(F32)
    d_out_own = lax.dynamic_slice_in_dim(cotangent[0], layer * rows, rows, 0).astype(F32)
    normed_own, d_branch_own = arrange(scalars, inputs[0], cotangent[0], gain_attn, layers)
    own_side, own_feed = pack_rest(core_id, w_outgate, w_out, w_gate, w_up, w_down)
    full_mix, (normed_own, own_side, own_feed) = gathered_rows(
        own_mix, (normed_own, own_side, own_feed)
    )
    side = lax.all_gather(own_side, "fsdp", axis=0, tiled=True)
    normed = jnp.concatenate([normed_own, swapped(normed_own)], 0)
    d_branch = (d_branch_own, swapped(after(d_branch_own, full_mix)))

    projected = dot(normed, full_mix)
    feed = lax.all_gather(after(own_feed, projected), "fsdp", axis=0, tiled=True)
    side = side.reshape(shards, 2, depth, tall)
    feed = feed.reshape(shards, 3, depth, units)
    mixed, states, inverses, news, active, sigma = mixer_forward(
        order, projected, taps, params, heads, key_dim, val_dim
    )
    gates, heads_out, attn_other, attn_own = head_outputs(normed, mixed, side, gain_head, heads)
    attn = line_sum_hops(core_sum(attn_other, attn_own))
    middle = tokens_own + live_own * attn
    mlp_scale = norm_parts(middle, 1e-6)
    hidden_own = (middle * mlp_scale * gain_mlp).astype(BF16)
    hidden_mine = jnp.concatenate(line_gather(hidden_own), 0)
    hidden = (hidden_mine, swapped(hidden_mine))

    stack_own, d_hidden_mine, branch_mine = feed_forward(hidden[0], d_branch[0], feed)
    stack_other, d_hidden_other, branch_other = feed_forward(hidden[1], d_branch[1], feed)
    d_hidden_core = core_sum(d_hidden_other, d_hidden_mine)
    held = lax.optimization_barrier((stack_own, stack_other, branch_other, d_hidden_core))
    grad_feed = feed_grads(hidden, d_branch, held[:2], shards)
    branch_core = core_sum(held[2], branch_mine)
    d_hidden, grad_feed, branch_core = line_sum(d_hidden_core, (grad_feed, branch_core))
    sum_feed = scattered(grad_feed)

    grad_mlp = jnp.sum(d_hidden * middle * mlp_scale, 0)
    d_middle = d_out_own + norm_back(d_hidden, middle, mlp_scale, gain_mlp)
    d_attn_mine = jnp.concatenate(line_gather((live_own * d_middle).astype(BF16)), 0)
    branch_core, d_attn_mine = lax.optimization_barrier((branch_core, d_attn_mine))
    d_attn = (d_attn_mine, swapped(d_attn_mine))


    d_mix, d_taps, d_params, d_gain = mixer_backward(
        order, projected, active, sigma, taps, params, states, inverses, news, mixed, gates,
        *d_attn, side, gain_head, heads, key_dim, val_dim,
    )
    branch, d_mix = line_sum(branch_core, (d_mix,))
    out_own = (middle + live_own * branch).astype(BF16)
    out_own, sum_feed, d_mix = lax.optimization_barrier((out_own, sum_feed, d_mix))
    side_at = width + 128

    hops = [(out_own, out_own)]
    hops.append(line_hop(*hops[-1], 1))
    d_normed_other, d_normed_mine, weighted = d_normed_rows(d_mix, normed, full_mix, side)
    hops[1], d_normed_other, d_normed_mine = lax.optimization_barrier(
        (hops[1], d_normed_other, d_normed_mine)
    )
    hops.append(line_hop(*hops[-1], 2))
    grad_out = out_grads(*d_attn, heads_out, shards)
    d_normed_other, grad_out = lax.optimization_barrier((swapped(d_normed_other), grad_out))
    d_normed_core = (d_normed_mine.astype(F32) + d_normed_other.astype(F32)).astype(BF16)
    sum_out = scattered(grad_out)
    hops[2], d_normed_core = lax.optimization_barrier((hops[2], d_normed_core))
    for step in range(3, layers):
        hops.append(line_hop(*hops[-1], step))

    grad_mix = mix_grads(normed, after(d_mix, d_normed_core), shards)
    d_normed, grad_mix, hops = line_sum(d_normed_core, (grad_mix, hops))
    low_mix = scattered(grad_mix)

    vector = after(jnp.concatenate([weighted[0] / gain_attn[0], grad_mlp, d_gain[0]]), grad_mix)
    vector = line_total(line_total(vector, "context"), "tensor")
    vector = jnp.concatenate([vector, d_taps[:taps_count].reshape(-1), d_params[:2].reshape(-1)])
    vector = line_total(vector, "fsdp")
    g_attn = lax.dynamic_slice_in_dim(vector, shard * depth, depth, 0)
    g_mlp = lax.dynamic_slice_in_dim(vector, model + shard * depth, depth, 0)
    g_head = lax.dynamic_slice_in_dim(vector, 2 * model + shard * val_part, val_part, 0)
    mine_taps = vector[2 * model + val_dim :]
    local = jnp.stack([mine_taps, swapped(mine_taps)])
    table = jnp.where(core == 0, local, local[::-1])
    tap_table = table[:, : taps_count * width].reshape(2, taps_count, width)
    param_table = table[:, taps_count * width :].reshape(2, 2, 128)
    d_log, d_bias = param_table[:, 0, :heads].reshape(-1), param_table[:, 1, :heads].reshape(-1)

    def tap_grad(begin, size):
        array = tap_table[:, :, begin : begin + heads * size].reshape(2, taps_count, heads, size)
        part = lax.dynamic_slice_in_dim(array, shard * (size // shards), size // shards, 3)
        return jnp.transpose(part, (0, 2, 1, 3)).reshape(all_heads, taps_count, size // shards)

    d_conv_q, d_conv_k, d_conv_v = (
        tap_grad(0, key_dim), tap_grad(wide, key_dim), tap_grad(2 * wide, val_dim)
    )

    d_tokens = norm_back(d_normed, tokens_own, norm_parts(tokens_own, 1e-6), gain_attn)
    grad_own = (d_middle + d_tokens).astype(BF16)
    back = [(grad_own, grad_own)]
    for step in range(1, layers):
        back.append(line_hop(*back[-1], step))
        if step == 1:
            output = place(turns, flat(hops))
            done = finish_wide(
                core_id, sum_feed, swapped(sum_feed), sum_out, swapped(sum_out), units
            )
            back[1], output, done = lax.optimization_barrier((back[1], output, done))
    g_gate, g_up, g_down, g_out = done
    input_grad = place(turns, flat(back))[None]
    low_mix, input_grad = lax.optimization_barrier((low_mix, input_grad))
    other_mix = swapped(low_mix)
    g_query, g_key, g_value, g_outgate = finish_mix(
        core_id, low_mix, other_mix,
        ((0, wide), (wide, wide), (2 * wide, tall), (side_at, tall)),
    )

    def narrow(begin):
        own, other = low_mix[:, begin : begin + heads], other_mix[:, begin : begin + heads]
        return jnp.where(
            core == 0, jnp.concatenate([own, other], 1), jnp.concatenate([other, own], 1)
        ).astype(F32)

    return (
        output[None],
        input_grad,
        g_attn,
        g_query,
        g_key,
        g_value,
        narrow(width),
        narrow(width + heads),
        d_log,
        d_bias,
        d_conv_q,
        d_conv_k,
        d_conv_v,
        g_outgate,
        g_head,
        g_out,
        g_mlp,
        g_gate,
        g_up,
        g_down,
    )


def solution(mesh):
    placed = (
        P("fsdp", "context", None),
        P("fsdp"),
        P("fsdp"),
        P("fsdp", "tensor"),
        P("fsdp", "tensor"),
        P("fsdp", "tensor"),
        P("fsdp", "tensor"),
        P("fsdp", "tensor"),
        P("tensor"),
        P("tensor"),
        P("tensor", None, "fsdp"),
        P("tensor", None, "fsdp"),
        P("tensor", None, "fsdp"),
        P("fsdp", "tensor"),
        P("fsdp"),
        P("tensor", "fsdp"),
        P("fsdp"),
        P("fsdp", "tensor"),
        P("fsdp", "tensor"),
        P("tensor", "fsdp"),
        P("fsdp", "context", None),
    )
    return jax.shard_map(
        on_device,
        mesh=mesh,
        in_specs=placed,
        out_specs=(placed[0], placed[0]) + placed[2:20],
        check_vma=False,
    )
```

```python
import functools
import jax
import jax.numpy as jnp
from jax import lax
from jax.experimental import pallas as pl
from jax.experimental.pallas import tpu as pltpu
from jax.sharding import PartitionSpec as P

F32 = jnp.float32
BF16 = jnp.bfloat16
CHUNK = 128
exact = lax.Precision.HIGHEST
NN = ((1,), (0,))
NT = ((1,), (1,))
TN = ((0,), (0,))


def mm(a, b, dims=NN):
    return lax.dot_general(
        a.astype(BF16), b.astype(BF16), (dims, ((), ())), preferred_element_type=F32
    )


def mm_exact(a, b, dims=NN):
    return lax.dot_general(a, b, (dims, ((), ())), precision=exact, preferred_element_type=F32)


def small_cost():
    return pl.CostEstimate(flops=1, bytes_accessed=1, transcendentals=0)


def grid_ids(size):
    rows = lax.broadcasted_iota(jnp.int32, (size, size), 0)
    cols = lax.broadcasted_iota(jnp.int32, (size, size), 1)
    return rows, cols


def softplus(v):
    return jnp.maximum(v, 0.0) + jnp.log1p(jnp.exp(-jnp.abs(v)))


def rates_of(rates, params, heads, triangle):
    lanes = lax.broadcasted_iota(jnp.int32, rates.shape, 1)
    shifted = rates + params[1:2, :]
    scale = jnp.exp(params[0:1, :])
    logdecay = jnp.where(lanes < heads, -scale * softplus(shifted), 0.0)
    running = mm_exact(triangle, logdecay)
    last = running[CHUNK - 1 : CHUNK, :]
    return (
        jax.nn.sigmoid(rates),
        shifted,
        scale,
        logdecay,
        running,
        jnp.transpose(running),
        jnp.exp(running),
        jnp.exp(last - running),
        jnp.exp(last),
    )


def convolved(window, taps, rows):
    total = taps[0:1, :] * window[5 : 5 + rows, :]
    for j in range(1, 4):
        total = total + taps[j : j + 1, :] * window[5 + j : 5 + j + rows, :]
    return total


PER = 2


def inverses_of(systems, rows, cols):
    eye = (rows == cols).astype(F32)
    near = [jnp.where(rows // 8 == cols // 8, s, 0.0).astype(BF16) for s in systems]
    second = [mm(n, n) for n in near]
    low = [s.astype(BF16) for s in second]
    third = [mm(s, n) for s, n in zip(low, near)]
    fourth = [mm(s, s) for s in low]
    partial = [eye - n.astype(F32) + s - t for n, s, t in zip(near, second, third)]
    result = [p + mm(p, f) for p, f in zip(partial, fourth)]
    size = 8
    while size < CHUNK:
        step = min(4, CHUNK // size)
        inside = (rows // (step * size) == cols // (step * size)) & (rows // size > cols // size)
        off = [jnp.where(inside, s, 0.0).astype(BF16) for s in systems]
        low = [r.astype(BF16) for r in result]
        reach = [mm(o, r).astype(BF16) for o, r in zip(off, low)]
        twice = [mm(r, r) for r in reach]
        once = [r - mm(x, y) for r, x, y in zip(result, low, reach)]
        result = [o + mm(o, t) for o, t in zip(once, twice)]
        size *= step
    high = [s.astype(BF16) for s in systems]
    rest = [s - h.astype(F32) for s, h in zip(systems, high)]
    low = [r.astype(BF16) for r in result]
    tail = [r - x.astype(F32) for r, x in zip(result, low)]
    left = [
        eye - (r + mm(h, x) + mm(e, x) + mm(h, t))
        for r, h, x, e, t in zip(result, high, low, rest, tail)
    ]
    return [r + mm(x, d) for r, x, d in zip(result, low, left)]


def forward_kernel(heads, key_dim, val_dim, order_ref, *refs):
    pre_refs, refs = refs[:PER], refs[PER:]
    (
        taps_ref, params_ref, mixed_ref, states_ref, inverse_ref, new_ref, active_ref, sigma_ref,
        state, window,
    ) = refs
    step = pl.program_id(0)
    wide = heads * key_dim
    width = window.shape[1]
    span = PER * CHUNK

    @pl.when(step == 0)
    def _():
        state[...] = jnp.zeros_like(state)
        window[0:8, :] = jnp.zeros((8, width), F32)

    for c in range(PER):
        window[8 + c * CHUNK : 8 + (c + 1) * CHUNK, :] = (
            pre_refs[c][:, :width].astype(BF16).astype(F32)
        )
    summed = convolved(window, taps_ref, span)
    window[0:8, :] = window[span : span + 8, :]
    sigma = jax.nn.sigmoid(summed)
    active = summed * sigma
    active_ref[...] = active
    sigma_ref[...] = sigma
    rows, cols = grid_ids(CHUNK)
    causal = rows >= cols
    strict = rows > cols
    triangle = causal.astype(F32)
    rates = [rates_of(pre_refs[c][:, width:], params_ref, heads, triangle) for c in range(PER)]
    chains = [(c, h) for c in range(PER) for h in range(heads)]

    def piece(at, c, h, size):
        return active[c * CHUNK : (c + 1) * CHUNK, at + h * size : at + (h + 1) * size]

    def unit(values, factor):
        return values * (lax.rsqrt(jnp.sum(values * values, -1, keepdims=True) + 1e-6) * factor)

    query = [unit(piece(0, c, h, key_dim), key_dim ** -0.5) for c, h in chains]
    keys = [unit(piece(wide, c, h, key_dim), 1.0) for c, h in chains]
    values = [piece(2 * wide, c, h, val_dim) for c, h in chains]
    beta = [rates[c][0][:, heads + h : heads + h + 1] for c, h in chains]
    decay = [rates[c][6][:, h : h + 1] for c, h in chains]
    ratios = [
        jnp.where(
            causal,
            jnp.exp(jnp.where(causal, rates[c][4][:, h : h + 1] - rates[c][5][h : h + 1, :], 0.0)),
            0.0,
        )
        for c, h in chains
    ]
    dots = [mm(jnp.concatenate([k, q], 0), k, NT) for k, q in zip(keys, query)]
    systems = [
        jnp.where(strict, b * d[:CHUNK] * r, 0.0) for b, d, r in zip(beta, dots, ratios)
    ]
    scores = [(d[CHUNK:] * r).astype(BF16) for d, r in zip(dots, ratios)]
    inverse = [x.astype(BF16) for x in inverses_of(systems, rows, cols)]
    solved = [
        mm(x, jnp.concatenate([(b * e) * k, b * v], 1))
        for x, b, e, k, v in zip(inverse, beta, decay, keys, values)
    ]
    for i, (c, h) in enumerate(chains):
        inverse_ref[(c * heads + h) * CHUNK : (c * heads + h + 1) * CHUNK, :] = inverse[i]
    for c in range(PER):
        place = pl.multiple_of(order_ref[step * PER + c] * CHUNK, CHUNK)
        for h in range(heads):
            i = c * heads + h
            begin = state[h * key_dim : (h + 1) * key_dim, :]
            begin_low = begin.astype(BF16)
            states_ref[(c * heads + h) * key_dim : (c * heads + h + 1) * key_dim, :] = begin_low
            through = mm(
                jnp.concatenate([solved[i][:, :key_dim], query[i] * decay[i]], 0), begin_low
            )
            new = (solved[i][:, key_dim:] - through[:CHUNK]).astype(BF16)
            mixed_ref[pl.ds(place, CHUNK), h * val_dim : (h + 1) * val_dim] = through[
                CHUNK:
            ] + mm(scores[i], new)
            state[h * key_dim : (h + 1) * key_dim, :] = rates[c][8][:, h : h + 1] * begin + mm(
                keys[i] * rates[c][7][:, h : h + 1], new, TN
            )
            new_ref[c * CHUNK : (c + 1) * CHUNK, h * val_dim : (h + 1) * val_dim] = new


def backward_kernel(heads, key_dim, val_dim, order_ref, *refs):
    pre_refs, refs = refs[:PER], refs[PER:]
    active_ref, sigma_ref, taps_ref, params_ref, states_ref, inverse_ref, new_ref = refs[:7]
    mixed_refs, refs = refs[7 : 7 + PER], refs[7 + PER :]
    gates_refs, refs = refs[:PER], refs[PER:]
    own_refs, refs = refs[:PER], refs[PER:]
    other_refs, refs = refs[:PER], refs[PER:]
    (side_ref, gain_ref, d_pre_ref, d_taps_ref, d_params_ref, d_gain_ref, d_state, after) = (
        refs
    )
    step = pl.program_id(0)
    steps = pl.num_programs(0)
    wide = heads * key_dim
    width = after.shape[1]
    span = PER * CHUNK
    first = (steps - 1 - step) * PER

    @pl.when(step == 0)
    def _():
        d_state[...] = jnp.zeros_like(d_state)
        after[span : span + 8, :] = jnp.zeros((8, width), F32)
        d_taps_ref[...] = jnp.zeros_like(d_taps_ref)
        d_params_ref[...] = jnp.zeros_like(d_params_ref)
        d_gain_ref[...] = jnp.zeros_like(d_gain_ref)

    active = active_ref[...]
    sigma = sigma_ref[...]
    slope = sigma + active * (1.0 - sigma)
    rows, cols = grid_ids(CHUNK)
    causal = rows >= cols
    strict = rows > cols
    triangle = causal.astype(F32)
    rates = [rates_of(pre_refs[c][:, width:], params_ref, heads, triangle) for c in range(PER)]
    chains = [(c, h) for c in range(PER) for h in range(heads)]
    places = [pl.multiple_of(order_ref[first + c] * CHUNK, CHUNK) for c in range(PER)]
    d_attn = jnp.concatenate(
        [
            jnp.where(order_ref[first + c] < steps * PER // 2, own_refs[c][...], other_refs[c][...])
            for c in range(PER)
        ],
        0,
    )
    depth = side_ref.shape[2]
    d_heads = mm(d_attn[:, :depth], side_ref[0, 0])
    for f in range(1, side_ref.shape[0]):
        d_heads = d_heads + mm(d_attn[:, f * depth : (f + 1) * depth], side_ref[f, 0])
    gain = gain_ref[...]

    def piece(array, at, c, h, size):
        return array[c * CHUNK : (c + 1) * CHUNK, at + h * size : at + (h + 1) * size]

    def scale_of(values):
        return lax.rsqrt(jnp.sum(values * values, -1, keepdims=True) + 1e-6)

    q_act = [piece(active, 0, c, h, key_dim) for c, h in chains]
    k_act = [piece(active, wide, c, h, key_dim) for c, h in chains]
    values = [piece(active, 2 * wide, c, h, val_dim) for c, h in chains]
    q_scale = [scale_of(x) for x in q_act]
    k_scale = [scale_of(x) for x in k_act]
    q_unit = [x * s for x, s in zip(q_act, q_scale)]
    keys = [x * s for x, s in zip(k_act, k_scale)]
    query = [x * key_dim ** -0.5 for x in q_unit]
    keys_low = [x.astype(BF16) for x in keys]
    query_low = [x.astype(BF16) for x in query]
    beta = [rates[c][0][:, heads + h : heads + h + 1] for c, h in chains]
    decay = [rates[c][6][:, h : h + 1] for c, h in chains]
    remain = [rates[c][7][:, h : h + 1] for c, h in chains]
    whole = [rates[c][8][:, h : h + 1] for c, h in chains]
    lead = [b * e for b, e in zip(beta, decay)]
    ratios = [
        jnp.where(
            causal,
            jnp.exp(jnp.where(causal, rates[c][4][:, h : h + 1] - rates[c][5][h : h + 1, :], 0.0)),
            0.0,
        )
        for c, h in chains
    ]
    d_mixed = []
    for c, h in chains:
        at = slice(h * val_dim, (h + 1) * val_dim)
        mixed = mixed_refs[c][:, at]
        gates = gates_refs[c][:, at]
        d_out = piece(d_heads, 0, c, h, val_dim)
        m_scale = lax.rsqrt(jnp.mean(mixed * mixed, -1, keepdims=True) + 1e-5)
        unit = mixed * m_scale
        g_sigma = jax.nn.sigmoid(gates)
        gated = gates * g_sigma
        weighted = d_out * unit
        d_pre_ref[
            pl.ds(places[c], CHUNK), width + 128 + h * val_dim : width + 128 + (h + 1) * val_dim
        ] = (weighted * gain * (g_sigma * (1.0 + gates * (1.0 - g_sigma)))).astype(BF16)
        d_gain_ref[0:1, :] += jnp.sum(weighted * gated, 0, keepdims=True)
        d_unit = d_out * gated * gain
        d_mixed.append(
            (m_scale * (d_unit - unit * jnp.mean(d_unit * unit, -1, keepdims=True))).astype(BF16)
        )
    dots = [mm(jnp.concatenate([k, q], 0), k, NT) for k, q in zip(keys_low, query_low)]
    weights = [jnp.where(strict, d[:CHUNK] * r, 0.0) for d, r in zip(dots, ratios)]
    scores = [d[CHUNK:] * r for d, r in zip(dots, ratios)]
    begin = [
        states_ref[(c * heads + h) * key_dim : (c * heads + h + 1) * key_dim, :] for c, h in chains
    ]
    inverse = [
        inverse_ref[(c * heads + h) * CHUNK : (c * heads + h + 1) * CHUNK, :] for c, h in chains
    ]
    new = [
        new_ref[c * CHUNK : (c + 1) * CHUNK, h * val_dim : (h + 1) * val_dim] for c, h in chains
    ]
    straight = [mm(s, d, TN) for s, d in zip(scores, d_mixed)]
    kept = [(k * r).astype(BF16) for k, r in zip(keys, remain)]
    both = [mm(x, jnp.concatenate([s.astype(BF16), k], 1), TN) for x, s, k in zip(inverse, straight, kept)]
    fixed = [mm(q * e, d, TN) for q, e, d in zip(query, decay, d_mixed)]
    pull = [(l * k).astype(BF16) for l, k in zip(lead, keys)]
    d_end = [None] * len(chains)
    solved = [None] * len(chains)
    for c in reversed(range(PER)):
        for h in range(heads):
            i = c * heads + h
            at = slice(h * key_dim, (h + 1) * key_dim)
            d_end[i] = d_state[at, :]
            solved[i] = both[i][:, :val_dim] + mm(both[i][:, val_dim:], d_end[i])
            d_state[at, :] = whole[i] * d_end[i] + fixed[i] - mm(pull[i], solved[i], TN)
    end_low = [d.astype(BF16) for d in d_end]
    outer = [
        mm(jnp.concatenate([d, s.astype(BF16)], 0), jnp.concatenate([b, n], 0), NT)
        for d, s, b, n in zip(d_mixed, solved, begin, new)
    ]
    d_kept = [mm(n, d, NT) for n, d in zip(new, end_low)]
    d_scores = [jnp.where(causal, o[:CHUNK, key_dim:], 0.0) for o in outer]
    d_system = [jnp.where(strict, -o[CHUNK:, key_dim:], 0.0) for o in outer]
    d_dots = [
        jnp.concatenate([(d * r).astype(BF16), (e * (b * r)).astype(BF16)], 0)
        for d, e, b, r in zip(d_scores, d_system, beta, ratios)
    ]
    near = [mm(d, low) for d, low in zip(d_dots, keys_low)]
    far = [
        mm(d, jnp.concatenate([q, k], 0), TN) for d, q, k in zip(d_dots, query_low, keys_low)
    ]
    lanes = lax.broadcasted_iota(jnp.int32, (CHUNK, 128), 1)
    row_ids = lax.broadcasted_iota(jnp.int32, (CHUNK, 1), 0)
    d_running = [jnp.zeros((CHUNK, 128), F32) for _ in range(PER)]
    d_strengths = [jnp.zeros((CHUNK, 128), F32) for _ in range(PER)]
    columns = [[] for _ in range(PER)]
    for i, (c, h) in enumerate(chains):
        d_query_state = outer[i][:CHUNK, :key_dim]
        d_keys_state = outer[i][CHUNK:, :key_dim]
        d_query = decay[i] * d_query_state + near[i][:CHUNK]
        d_keys = near[i][CHUNK:] + far[i] - lead[i] * d_keys_state + remain[i] * d_kept[i]
        along = decay[i] * jnp.sum(keys[i] * d_keys_state, -1, keepdims=True)
        weighed = d_system[i] * weights[i]
        d_beta = (
            jnp.sum(solved[i] * values[i], -1, keepdims=True)
            - along
            + jnp.sum(weighed, -1, keepdims=True)
        )
        joint = weighed * beta[i] + d_scores[i] * scores[i]
        left = remain[i] * jnp.sum(keys[i] * d_kept[i], -1, keepdims=True)
        total = jnp.sum(left, 0, keepdims=True) + whole[i] * jnp.sum(
            jnp.sum(d_end[i] * begin[i].astype(F32), -1, keepdims=True), 0, keepdims=True
        )
        d_run = (
            jnp.sum(joint, -1, keepdims=True)
            + decay[i] * jnp.sum(query[i] * d_query_state, -1, keepdims=True)
            - beta[i] * along
            - left
            + jnp.where(row_ids == CHUNK - 1, total, 0.0)
        )
        d_running[c] = jnp.where(lanes == h, d_run, d_running[c])
        columns[c].append(jnp.sum(joint, 0, keepdims=True))
        d_strengths[c] = jnp.where(lanes == heads + h, d_beta, d_strengths[c])
        d_q = d_query * key_dim ** -0.5
        d_q = q_scale[i] * (d_q - q_unit[i] * jnp.sum(q_unit[i] * d_q, -1, keepdims=True))
        d_k = k_scale[i] * (d_keys - keys[i] * jnp.sum(keys[i] * d_keys, -1, keepdims=True))
        here = slice(c * CHUNK, (c + 1) * CHUNK)
        after[here, h * key_dim : (h + 1) * key_dim] = d_q * piece(slope, 0, c, h, key_dim)
        after[here, wide + h * key_dim : wide + (h + 1) * key_dim] = d_k * piece(
            slope, wide, c, h, key_dim
        )
        after[here, 2 * wide + h * val_dim : 2 * wide + (h + 1) * val_dim] = (
            beta[i] * solved[i]
        ) * piece(slope, 2 * wide, c, h, val_dim)
    upper = (rows <= cols).astype(F32)
    for c in range(PER):
        strengths, shifted, scale, logdecay = rates[c][:4]
        turned = jnp.transpose(
            jnp.concatenate(columns[c] + [jnp.zeros((CHUNK - heads, CHUNK), F32)], 0)
        )
        d_logdecay = mm_exact(upper, d_running[c] - turned)
        d_shifted = jnp.where(lanes < heads, d_logdecay * (-scale) * jax.nn.sigmoid(shifted), 0.0)
        d_params_ref[0:1, :] += jnp.sum(d_logdecay * logdecay, 0, keepdims=True)
        d_params_ref[1:2, :] += jnp.sum(d_shifted, 0, keepdims=True)
        d_pre_ref[pl.ds(places[c], CHUNK), width : width + 128] = (
            d_shifted + d_strengths[c] * strengths * (1.0 - strengths)
        ).astype(BF16)
    total = None
    pre = jnp.concatenate([ref[:, :width].astype(BF16).astype(F32) for ref in pre_refs], 0)
    for j in range(4):
        shifted = after[3 - j : 3 - j + span, :]
        term = taps_ref[j : j + 1, :] * shifted
        total = term if total is None else total + term
        d_taps_ref[j : j + 1, :] += jnp.sum(pre * shifted, 0, keepdims=True)
    for c in range(PER):
        d_pre_ref[pl.ds(places[c], CHUNK), :width] = total[c * CHUNK : (c + 1) * CHUNK].astype(BF16)
    after[span : span + 8, :] = after[0:8, :]


def mixer_forward(order, pre, taps, params, heads, key_dim, val_dim):
    chunks = pre.shape[0] // CHUNK
    width = taps.shape[1]
    here = lambda c: lambda n, order: (order[n * PER + c], 0)
    plain = lambda n, order: (n, 0)
    fixed = lambda n, order: (0, 0)
    return pl.pallas_call(
        functools.partial(forward_kernel, heads, key_dim, val_dim),
        grid_spec=pltpu.PrefetchScalarGridSpec(
            num_scalar_prefetch=1,
            grid=(chunks // PER,),
            in_specs=[pl.BlockSpec((CHUNK, pre.shape[1]), here(c)) for c in range(PER)]
            + [pl.BlockSpec(taps.shape, fixed), pl.BlockSpec(params.shape, fixed)],
            out_specs=[
                pl.BlockSpec((pre.shape[0], heads * val_dim), fixed),
                pl.BlockSpec((PER * heads * key_dim, val_dim), plain),
                pl.BlockSpec((PER * heads * CHUNK, CHUNK), plain),
                pl.BlockSpec((PER * CHUNK, heads * val_dim), plain),
                pl.BlockSpec((PER * CHUNK, width), plain),
                pl.BlockSpec((PER * CHUNK, width), plain),
            ],
            scratch_shapes=[
                pltpu.VMEM((heads * key_dim, val_dim), F32),
                pltpu.VMEM((PER * CHUNK + 8, width), F32),
            ],
        ),
        out_shape=[
            jax.ShapeDtypeStruct((pre.shape[0], heads * val_dim), F32),
            jax.ShapeDtypeStruct((chunks * heads * key_dim, val_dim), BF16),
            jax.ShapeDtypeStruct((chunks * heads * CHUNK, CHUNK), BF16),
            jax.ShapeDtypeStruct((pre.shape[0], heads * val_dim), BF16),
            jax.ShapeDtypeStruct((pre.shape[0], width), F32),
            jax.ShapeDtypeStruct((pre.shape[0], width), F32),
        ],
        compiler_params=pltpu.CompilerParams(vmem_limit_bytes=48 * 2**20),
        cost_estimate=small_cost(),
        name="mixer_forward",
    )(order, *[pre] * PER, taps, params)


def mixer_backward(
    order, pre, active, sigma, taps, params, states, inverses, news, mixed, gates, d_own, d_other,
    side, gain, heads, key_dim, val_dim,
):
    chunks = pre.shape[0] // CHUNK
    width = taps.shape[1]
    out_width = heads * val_dim
    steps = chunks // PER
    half = chunks // 2
    at = lambda n, c, order: order[(steps - 1 - n) * PER + c]
    here = lambda c: lambda n, order: (at(n, c, order), 0)
    first = lambda c: lambda n, order: (jnp.minimum(at(n, c, order), half - 1), 0)
    second = lambda c: lambda n, order: (jnp.maximum(at(n, c, order) - half, 0), 0)
    plain = lambda n, order: (steps - 1 - n, 0)
    fixed = lambda n, order: (0, 0)
    each = lambda shape, place: [pl.BlockSpec(shape, place(c)) for c in range(PER)]
    return pl.pallas_call(
        functools.partial(backward_kernel, heads, key_dim, val_dim),
        grid_spec=pltpu.PrefetchScalarGridSpec(
            num_scalar_prefetch=1,
            grid=(steps,),
            in_specs=each((CHUNK, pre.shape[1]), here)
            + [
                pl.BlockSpec((PER * CHUNK, width), plain),
                pl.BlockSpec((PER * CHUNK, width), plain),
                pl.BlockSpec(taps.shape, fixed),
                pl.BlockSpec(params.shape, fixed),
                pl.BlockSpec((PER * heads * key_dim, val_dim), plain),
                pl.BlockSpec((PER * heads * CHUNK, CHUNK), plain),
                pl.BlockSpec((PER * CHUNK, out_width), plain),
            ]
            + each((CHUNK, out_width), here)
            + each((CHUNK, out_width), here)
            + each((CHUNK, d_own.shape[1]), first)
            + each((CHUNK, d_own.shape[1]), second)
            + [
                pl.BlockSpec(
                    (side.shape[0], 1) + side.shape[2:], lambda n, order: (0, 1, 0, 0)
                ),
                pl.BlockSpec((1, val_dim), fixed),
            ],
            out_specs=[
                pl.BlockSpec((pre.shape[0], pre.shape[1] + out_width), fixed),
                pl.BlockSpec((8, width), fixed),
                pl.BlockSpec((8, 128), fixed),
                pl.BlockSpec((8, val_dim), fixed),
            ],
            scratch_shapes=[
                pltpu.VMEM((heads * key_dim, val_dim), F32),
                pltpu.VMEM((PER * CHUNK + 8, width), F32),
            ],
        ),
        out_shape=[
            jax.ShapeDtypeStruct((pre.shape[0], pre.shape[1] + out_width), BF16),
            jax.ShapeDtypeStruct((8, width), F32),
            jax.ShapeDtypeStruct((8, 128), F32),
            jax.ShapeDtypeStruct((8, val_dim), F32),
        ],
        compiler_params=pltpu.CompilerParams(vmem_limit_bytes=56 * 2**20),
        cost_estimate=small_cost(),
        name="mixer_backward",
    )(
        order, *[pre] * PER, active, sigma, taps, params, states, inverses, news, *[mixed] * PER,
        *[gates] * PER, *[d_own] * PER, *[d_other] * PER, side, gain,
    )


def roomy():
    return dict(
        compiler_params=pltpu.CompilerParams(vmem_limit_bytes=56 * 2**20),
        cost_estimate=small_cost(),
    )


def pack_mix_kernel(heads, core_ref, q_ref, k_ref, v_ref, decay_ref, strength_ref, out_ref):
    first = core_ref[0] == 0
    wide, tall = q_ref.shape[1], v_ref.shape[1]
    out_ref[:, :wide] = q_ref[...]
    out_ref[:, wide : 2 * wide] = k_ref[...]
    out_ref[:, 2 * wide : 2 * wide + tall] = v_ref[...]

    rates = jnp.transpose(
        jnp.concatenate([decay_ref[...].astype(F32), strength_ref[...].astype(F32)], 0)
    )
    pick = lambda at: jnp.where(
        first, rates[:, at : at + heads], rates[:, at + heads : at + 2 * heads]
    )
    rows = out_ref.shape[0]
    out_ref[:, 2 * wide + tall :] = jnp.concatenate(
        [pick(0), pick(2 * heads), jnp.zeros((rows, 128 - 2 * heads), F32)], 1
    ).astype(BF16)


def pack_mix(core, heads, w_query, w_key, w_value, w_decay, w_strength):
    depth = w_query.shape[0]
    wide, tall = w_query.shape[1] // 2, w_value.shape[1] // 2
    here = lambda i, core: (0, core[0])
    fixed = lambda i, core: (0, 0)
    return pl.pallas_call(
        functools.partial(pack_mix_kernel, heads),
        grid_spec=pltpu.PrefetchScalarGridSpec(
            num_scalar_prefetch=1,
            grid=(1,),
            in_specs=[
                pl.BlockSpec((depth, wide), here),
                pl.BlockSpec((depth, wide), here),
                pl.BlockSpec((depth, tall), here),
                pl.BlockSpec(w_decay.shape[::-1], fixed),
                pl.BlockSpec(w_strength.shape[::-1], fixed),
            ],
            out_specs=pl.BlockSpec((depth, 2 * wide + tall + 128), fixed),
        ),
        out_shape=jax.ShapeDtypeStruct((depth, 2 * wide + tall + 128), BF16),
        name="pack_mix",
        **roomy(),
    )(core, w_query, w_key, w_value, w_decay.T, w_strength.T)


def pack_rest_kernel(core_ref, outgate_ref, out_ref, gate_ref, up_ref, down_ref, side_ref, wide_ref):
    first = core_ref[0] == 0
    depth = outgate_ref.shape[0]
    units = gate_ref.shape[1] // 2
    side_ref[:depth, :] = outgate_ref[...]
    side_ref[depth:, :] = jnp.transpose(out_ref[...].astype(F32)).astype(BF16)
    for at, ref in ((0, gate_ref), (1, up_ref)):
        values = ref[...]
        wide_ref[at * depth : (at + 1) * depth, :] = jnp.where(
            first, values[:, :units], values[:, units:]
        )
    wide_ref[2 * depth :, :] = jnp.transpose(down_ref[...].astype(F32)).astype(BF16)


def pack_rest(core, w_outgate, w_out, w_gate, w_up, w_down):
    depth = w_outgate.shape[0]
    tall, units = w_outgate.shape[1] // 2, w_gate.shape[1] // 2
    fixed = lambda i, core: (0, 0)
    return pl.pallas_call(
        pack_rest_kernel,
        grid_spec=pltpu.PrefetchScalarGridSpec(
            num_scalar_prefetch=1,
            grid=(1,),
            in_specs=[
                pl.BlockSpec((depth, tall), lambda i, core: (0, core[0])),
                pl.BlockSpec((tall, depth), lambda i, core: (core[0], 0)),
                pl.BlockSpec(w_gate.shape, fixed),
                pl.BlockSpec(w_up.shape, fixed),
                pl.BlockSpec((units, depth), lambda i, core: (core[0], 0)),
            ],
            out_specs=[
                pl.BlockSpec((2 * depth, tall), fixed),
                pl.BlockSpec((3 * depth, units), fixed),
            ],
        ),
        out_shape=[
            jax.ShapeDtypeStruct((2 * depth, tall), BF16),
            jax.ShapeDtypeStruct((3 * depth, units), BF16),
        ],
        name="pack_rest",
        **roomy(),
    )(core, w_outgate, w_out, w_gate, w_up, w_down)


def arrange_kernel(scalars_ref, tokens_ref, cotangent_ref, gain_ref, normed_ref, branch_ref):
    step = pl.program_id(0)
    rows = tokens_ref.shape[0]
    tokens = tokens_ref[...].astype(F32)
    scale = lax.rsqrt(jnp.mean(tokens * tokens, -1, keepdims=True) + 1e-6)
    normed_ref[...] = (tokens * scale * gain_ref[...]).astype(BF16)
    place = scalars_ref[0] + scalars_ref[2 + step] * rows + lax.broadcasted_iota(
        jnp.int32, (rows, 1), 0
    )
    branch_ref[...] = jnp.where(place < scalars_ref[1], cotangent_ref[...], 0).astype(BF16)


def arrange(scalars, tokens, cotangent, gain, layers):
    rows, model = tokens.shape[0] // layers, tokens.shape[1]
    there = pl.BlockSpec((rows, model), lambda p, scalars: (scalars[2 + p], 0))
    plain = pl.BlockSpec((rows, model), lambda p, scalars: (p, 0))
    return pl.pallas_call(
        arrange_kernel,
        grid_spec=pltpu.PrefetchScalarGridSpec(
            num_scalar_prefetch=1,
            grid=(layers,),
            in_specs=[there, there, pl.BlockSpec((1, model), lambda p, scalars: (0, 0))],
            out_specs=[plain, plain],
        ),
        out_shape=[jax.ShapeDtypeStruct(tokens.shape, BF16)] * 2,
        name="arrange",
        **roomy(),
    )(scalars, tokens, cotangent, gain)


TILE = 256


def heads_kernel(
    heads, normed_ref, mixed_ref, side_ref, gain_ref, gates_ref, heads_ref, other_ref, own_ref
):
    step = pl.program_id(0)
    half = pl.num_programs(0) // 2
    shards, _, depth, tall = side_ref.shape
    val_dim = tall // heads
    gates = mm(normed_ref[:, :depth], side_ref[0, 0])
    for f in range(1, shards):
        gates = gates + mm(normed_ref[:, f * depth : (f + 1) * depth], side_ref[f, 0])
    gates_ref[...] = gates
    for h in range(heads):
        at = slice(h * val_dim, (h + 1) * val_dim)
        mixed = mixed_ref[:, at]
        gate = gates[:, at]
        scale = lax.rsqrt(jnp.mean(mixed * mixed, -1, keepdims=True) + 1e-5)
        heads_ref[:, at] = (
            mixed * scale * gain_ref[...] * (gate * jax.nn.sigmoid(gate))
        ).astype(BF16)
    low = heads_ref[...]

    def write(ref):
        for f in range(shards):
            ref[:, f * depth : (f + 1) * depth] = mm(low, side_ref[f, 1], NT).astype(BF16)

    @pl.when(step < half)
    def _():
        write(other_ref)

    @pl.when(step >= half)
    def _():
        write(own_ref)


def turned_specs(tiles):
    half = tiles // 2
    here = lambda i: (jnp.where(i < half, i + half, i - half), 0)
    other = lambda i: (jnp.minimum(i, half - 1), 0)
    own = lambda i: (jnp.maximum(i - half, 0), 0)
    return here, other, own


def head_outputs(normed, mixed, side, gain, heads):
    count, model = normed.shape
    tall = mixed.shape[1]
    here, other, own = turned_specs(count // TILE)
    return pl.pallas_call(
        functools.partial(heads_kernel, heads),
        grid=(count // TILE,),
        in_specs=[
            pl.BlockSpec((TILE, model), here),
            pl.BlockSpec((TILE, tall), here),
            pl.BlockSpec(side.shape, lambda i: (0, 0, 0, 0)),
            pl.BlockSpec(gain.shape, lambda i: (0, 0)),
        ],
        out_specs=[
            pl.BlockSpec((TILE, tall), here),
            pl.BlockSpec((TILE, tall), here),
            pl.BlockSpec((TILE, model), other),
            pl.BlockSpec((TILE, model), own),
        ],
        out_shape=[
            jax.ShapeDtypeStruct((count, tall), F32),
            jax.ShapeDtypeStruct((count, tall), BF16),
            jax.ShapeDtypeStruct((count // 2, model), BF16),
            jax.ShapeDtypeStruct((count // 2, model), BF16),
        ],
        name="head_outputs",
        **roomy(),
    )(normed, mixed, side, gain)


def feed_kernel(turns_ref, hidden_ref, branch_ref, wide_ref, stack_ref, d_hidden_ref, branch_out_ref):
    shards, _, depth, units = wide_ref.shape
    step = pl.program_id(0)
    rows = d_hidden_ref.shape[0] // turns_ref.shape[0]
    blocks = hidden_ref.shape[0] // rows

    def forward(ref, at):
        total = mm(ref[:, :depth], wide_ref[0, at])
        for f in range(1, shards):
            total = total + mm(ref[:, f * depth : (f + 1) * depth], wide_ref[f, at])
        return total

    gate = forward(hidden_ref, 0)
    up = forward(hidden_ref, 1)
    d_act = forward(branch_ref, 2)
    sigma = jax.nn.sigmoid(gate)
    silu = gate * sigma
    act = (silu * up).astype(BF16)
    d_gate = (d_act * up * (sigma + silu * (1.0 - sigma))).astype(BF16)
    d_up = (d_act * silu).astype(BF16)
    stack_ref[0] = d_gate
    stack_ref[1] = d_up
    stack_ref[2] = act
    for f in range(shards):
        at = slice(f * depth, (f + 1) * depth)
        d_hidden = (mm(d_gate, wide_ref[f, 0], NT) + mm(d_up, wide_ref[f, 1], NT)).astype(BF16)
        for k in range(blocks):
            place = pl.multiple_of(turns_ref[step * blocks + k] * rows, rows)
            d_hidden_ref[pl.ds(place, rows), at] = d_hidden[k * rows : (k + 1) * rows]
        branch_out_ref[:, at] = mm(act, wide_ref[f, 2], NT).astype(BF16)


def feed_forward(turns, hidden, branch, wide):
    count, model = hidden.shape
    units = wide.shape[3]
    tile = max(TILE, count // turns.shape[0])
    row = pl.BlockSpec((tile, model), lambda i, turns: (i, 0))
    return pl.pallas_call(
        feed_kernel,
        grid_spec=pltpu.PrefetchScalarGridSpec(
            num_scalar_prefetch=1,
            grid=(count // tile,),
            in_specs=[row, row, pl.BlockSpec(wide.shape, lambda i, turns: (0, 0, 0, 0))],
            out_specs=[
                pl.BlockSpec((3, tile, units), lambda i, turns: (0, i, 0)),
                pl.BlockSpec((count, model), lambda i, turns: (0, 0)),
                row,
            ],
        ),
        out_shape=[
            jax.ShapeDtypeStruct((3, count, units), BF16),
            jax.ShapeDtypeStruct((count, model), BF16),
            jax.ShapeDtypeStruct((count, model), BF16),
        ],
        name="feed_forward",
        **roomy(),
    )(turns, hidden, branch, wide)


def feed_grads_kernel(h_own, h_other, b_own, b_other, s_own, s_other, out_ref):
    units = s_own.shape[2]
    for at, own, other in ((0, h_own, h_other), (1, h_own, h_other), (2, b_own, b_other)):
        out_ref[:, at * units : (at + 1) * units] = (
            mm(own[...], s_own[at], TN) + mm(other[...], s_other[at], TN)
        ).astype(BF16)
    rest = out_ref.shape[1] - 3 * units
    if rest:
        out_ref[:, 3 * units :] = jnp.zeros((out_ref.shape[0], rest), BF16)


def feed_grads(hidden, branch, stacks, shards):
    count, model = hidden[0].shape
    units = stacks[0].shape[2]
    depth = model // shards
    width = -(-3 * units // 128) * 128
    part = pl.BlockSpec((count, depth), lambda f: (0, f))
    use_s = pl.BlockSpec((3, count, units), lambda f: (0, 0, 0))
    return pl.pallas_call(
        feed_grads_kernel,
        grid=(shards,),
        in_specs=[part, part, part, part, use_s, use_s],
        out_specs=pl.BlockSpec((depth, width), lambda f: (f, 0)),
        out_shape=jax.ShapeDtypeStruct((model, width), BF16),
        name="feed_grads",
        **roomy(),
    )(*hidden, *branch, *stacks)


def d_normed_kernel(side_at, mix_ref, normed_ref, weights_ref, side_ref, other_ref, own_ref, sum_ref):
    step = pl.program_id(0)
    half = pl.num_programs(0) // 2
    shards, _, depth, _ = side_ref.shape

    @pl.when(step == 0)
    def _():
        sum_ref[...] = jnp.zeros_like(sum_ref)

    def write(ref):
        for f in range(shards):
            at = slice(f * depth, (f + 1) * depth)
            part = mm(mix_ref[:, :side_at], weights_ref[at, :], NT) + mm(
                mix_ref[:, side_at:], side_ref[f, 0], NT
            )
            ref[:, at] = part.astype(BF16)
            sum_ref[0:1, at] += jnp.sum(part * normed_ref[:, at].astype(F32), 0, keepdims=True)

    @pl.when(step < half)
    def _():
        write(other_ref)

    @pl.when(step >= half)
    def _():
        write(own_ref)


def d_normed_rows(d_mix, normed, weights, side):
    count, model = normed.shape
    here, other, own = turned_specs(count // TILE)
    fixed = lambda i: (0, 0)
    return pl.pallas_call(
        functools.partial(d_normed_kernel, weights.shape[1]),
        grid=(count // TILE,),
        in_specs=[
            pl.BlockSpec((TILE, d_mix.shape[1]), here),
            pl.BlockSpec((TILE, model), here),
            pl.BlockSpec(weights.shape, fixed),
            pl.BlockSpec((side.shape[0], 1) + side.shape[2:], lambda i: (0, 0, 0, 0)),
        ],
        out_specs=[
            pl.BlockSpec((TILE, model), other),
            pl.BlockSpec((TILE, model), own),
            pl.BlockSpec((8, model), fixed),
        ],
        out_shape=[
            jax.ShapeDtypeStruct((count // 2, model), BF16),
            jax.ShapeDtypeStruct((count // 2, model), BF16),
            jax.ShapeDtypeStruct((8, model), F32),
        ],
        name="d_normed_rows",
        **roomy(),
    )(d_mix, normed, weights, side)


def mix_grads_kernel(normed_ref, mix_ref, out_ref):
    out_ref[...] = mm(normed_ref[...], mix_ref[...], TN).astype(BF16)


def mix_grads(normed, d_mix, shards):
    count, model = normed.shape
    depth, width = model // shards, d_mix.shape[1]
    return pl.pallas_call(
        mix_grads_kernel,
        grid=(shards,),
        in_specs=[
            pl.BlockSpec((count, depth), lambda f: (0, f)),
            pl.BlockSpec(d_mix.shape, lambda f: (0, 0)),
        ],
        out_specs=pl.BlockSpec((depth, width), lambda f: (f, 0)),
        out_shape=jax.ShapeDtypeStruct((model, width), BF16),
        name="mix_grads",
        **roomy(),
    )(normed, d_mix)


def out_grads_kernel(d_own_ref, d_other_ref, heads_ref, out_ref):
    half = d_own_ref.shape[0]
    out_ref[...] = (
        mm(d_own_ref[...], heads_ref[:half, :], TN) + mm(d_other_ref[...], heads_ref[half:, :], TN)
    ).astype(BF16)


def out_grads(d_own, d_other, heads_out, shards):
    count, model = d_own.shape
    depth, width = model // shards, heads_out.shape[1]
    column = pl.BlockSpec((count, depth), lambda f: (0, f))
    return pl.pallas_call(
        out_grads_kernel,
        grid=(shards,),
        in_specs=[column, column, pl.BlockSpec(heads_out.shape, lambda f: (0, 0))],
        out_specs=pl.BlockSpec((depth, width), lambda f: (f, 0)),
        out_shape=jax.ShapeDtypeStruct((model, width), BF16),
        name="out_grads",
        **roomy(),
    )(d_own, d_other, heads_out)


def place_kernel(turns_ref, *refs):
    parts, out_ref = refs[:-1], refs[-1]
    size = turns_ref.shape[0]
    rows = parts[0].shape[0]
    for p in range(size):
        at = pl.multiple_of(turns_ref[p] * rows, rows)
        if len(parts) == size:
            part = parts[p][...]
        elif p == 0:
            part = parts[0][...]
        else:
            part = parts[p][...] + parts[2 * size - 1 - p][...]
        out_ref[pl.ds(at, rows), :] = part


def place(turns, parts):
    size = turns.shape[0]
    rows, model = parts[0].shape
    whole = lambda i, turns: (0, 0)
    return pl.pallas_call(
        place_kernel,
        grid_spec=pltpu.PrefetchScalarGridSpec(
            num_scalar_prefetch=1,
            grid=(1,),
            in_specs=[pl.BlockSpec((rows, model), whole)] * len(parts),
            out_specs=pl.BlockSpec((size * rows, model), whole),
        ),
        out_shape=jax.ShapeDtypeStruct((size * rows, model), BF16),
        name="place",
        **roomy(),
    )(turns, *parts)


def finish_kernel(cuts, turned, core_ref, own_ref, other_ref, *refs):
    first = core_ref[0] == 0
    own, other = own_ref[...].astype(F32), other_ref[...].astype(F32)
    low, high = jnp.where(first, own, other), jnp.where(first, other, own)
    for (begin, size), ref in zip(cuts, refs):
        ref[:, :size] = low[:, begin : begin + size]
        ref[:, size:] = high[:, begin : begin + size]
    if turned is None:
        return
    begin, size = turned
    refs[-1][:size, :] = jnp.transpose(low[:, begin : begin + size])
    refs[-1][size:, :] = jnp.transpose(high[:, begin : begin + size])


def finish(core, own, other, cuts, turned):
    depth, width = own.shape
    row = lambda size: pl.BlockSpec((128, size), lambda i, core: (i, 0))
    shapes = [(depth, 2 * size) for _, size in cuts]
    specs = [row(2 * size) for _, size in cuts]
    if turned is not None:
        shapes.append((2 * turned[1], depth))
        specs.append(pl.BlockSpec((2 * turned[1], 128), lambda i, core: (0, i)))
    return pl.pallas_call(
        functools.partial(finish_kernel, cuts, turned),
        grid_spec=pltpu.PrefetchScalarGridSpec(
            num_scalar_prefetch=1,
            grid=(depth // 128,),
            in_specs=[row(width), row(width)],
            out_specs=specs,
        ),
        out_shape=[jax.ShapeDtypeStruct(shape, F32) for shape in shapes],
        name="finish",
        **roomy(),
    )(core, own, other)


def after(value, *others):
    return lax.optimization_barrier((value,) + others)[0]


def is_square(axis):
    return lax.axis_size(axis) == 4


def across(value, flip):
    return lax.ppermute(value, "fsdp", [(i, i ^ flip) for i in range(4)])


def swapped(value):
    return lax.ppermute(value, "context", [(0, 1), (1, 0)])


def gathered_rows(own, beside, later):
    if not is_square("fsdp"):
        return lax.all_gather(own, "fsdp", axis=0, tiled=True), beside, later(beside)
    rows = own.shape[0]
    half = rows // 2
    along_x = across(own, 1)
    along_y = across(own, 2)
    along_x, along_y, beside = lax.optimization_barrier((along_x, along_y, beside))
    low = across(along_x[:half], 2)
    high = across(along_y[half:], 1)
    low, high, extra = lax.optimization_barrier((low, high, later(beside)))
    shard = lax.axis_index("fsdp")
    whole = jnp.zeros((4 * rows,) + own.shape[1:], own.dtype)
    for place, part in ((0, own), (1, along_x), (2, along_y)):
        whole = lax.dynamic_update_slice_in_dim(whole, part, (shard ^ place) * rows, 0)
    whole = lax.dynamic_update_slice_in_dim(whole, low, (shard ^ 3) * rows, 0)
    return lax.dynamic_update_slice_in_dim(whole, high, (shard ^ 3) * rows + half, 0), beside, extra


def scattered(blocks):
    return lax.psum_scatter(blocks, "fsdp", scatter_dimension=0, tiled=True)


def line_sum(value, beside=(), axis="tensor"):
    size = lax.axis_size(axis)
    rows = value.shape[0] // size
    parts = [
        lax.ppermute(
            value[p * rows : (p + 1) * rows], axis, [(i, (i - p) % size) for i in range(size)]
        )
        for p in range(1, size)
    ]
    if beside:
        parts, beside = lax.optimization_barrier((parts, tuple(beside)))
    total = value[:rows].astype(F32)
    for part in parts:
        total = total + part.astype(F32)
    return (total, *beside) if beside else total


def line_sum_hops(value, beside=None, axis="tensor"):
    size = lax.axis_size(axis)
    rows = value.shape[0] // size
    block = lambda p: value[p * rows : (p + 1) * rows].astype(F32)
    right = left = None
    for step in range(1, size):
        send_r, send_l = block(step), block(size - step)
        if right is not None:
            send_r = send_r + right.astype(F32)
            send_l = send_l + left.astype(F32)
        right = lax.ppermute(send_r.astype(BF16), axis, [(i, i + 1) for i in range(step)])
        left = lax.ppermute(
            send_l.astype(BF16), axis, [(i, i - 1) for i in range(size - step, size)]
        )
        if beside:
            right, left = beside(step, (right, left))
    return block(0) + right.astype(F32) + left.astype(F32)


def line_gather(own, axis="tensor"):
    size = lax.axis_size(axis)
    rights, lefts = [own], [own]
    for step in range(1, size):
        rights.append(
            lax.ppermute(rights[-1], axis, [(i, i + 1) for i in range(step - 1, size - 1)])
        )
        lefts.append(lax.ppermute(lefts[-1], axis, [(i, i - 1) for i in range(1, size - step + 1)]))
    return [own] + [rights[k] + lefts[size - k] for k in range(1, size)]


def line_hop(right, left, step, axis="tensor"):
    size = lax.axis_size(axis)
    return (
        lax.ppermute(right, axis, [(i, i + 1) for i in range(step - 1, size - 1)]),
        lax.ppermute(left, axis, [(i, i - 1) for i in range(1, size - step + 1)]),
    )


def flat(hops):
    return [hops[0][0]] + [hop[0] for hop in hops[1:]] + [hop[1] for hop in hops[1:]]


def core_sum(other_rows, own_rows):
    return (own_rows.astype(F32) + swapped(other_rows).astype(F32)).astype(BF16)


def dot(a, b, dims=NN):
    return lax.dot_general(a, b, (dims, ((), ())), preferred_element_type=F32)


def norm_parts(values, epsilon):
    return lax.rsqrt(jnp.mean(values * values, -1, keepdims=True) + epsilon)


def norm_back(d_scaled, values, scale, gain):
    raised = d_scaled * gain
    return scale * raised - values * (
        scale * scale * scale * jnp.mean(raised * values, -1, keepdims=True)
    )


def on_device(
    inputs, lengths, norm_attn, w_query, w_key, w_value, w_decay, w_strength, decay_log,
    decay_bias, conv_query, conv_key, conv_value, w_outgate, norm_head, w_out, norm_mlp, w_gate,
    w_up, w_down, cotangent,
):
    shard, core, layer = (lax.axis_index(name) for name in ("fsdp", "context", "tensor"))
    shards, layers = lax.axis_size("fsdp"), lax.axis_size("tensor")
    seg, model = inputs.shape[1:]
    rows = seg // layers
    depth = norm_attn.shape[0]
    all_heads, taps_count, key_part = conv_query.shape
    val_part = conv_value.shape[2]
    heads = all_heads // 2
    key_dim, val_dim = key_part * shards, val_part * shards
    wide, tall = heads * key_dim, heads * val_dim
    width = 2 * wide + tall
    units = w_gate.shape[1] // 2

    def mine(array, dim):
        size = array.shape[dim] // 2
        first = lax.slice_in_dim(array, 0, size, axis=dim)
        second = lax.slice_in_dim(array, size, 2 * size, axis=dim)
        return jnp.where(core == 0, first, second)

    core_id = core.reshape(1).astype(jnp.int32)
    own_mix = pack_mix(core_id, heads, w_query, w_key, w_value, w_decay, w_strength)

    pieces = (
        norm_attn, norm_mlp, norm_head,
        mine(conv_query, 0).reshape(-1), mine(conv_key, 0).reshape(-1),
        mine(conv_value, 0).reshape(-1),
    )
    small = after(jnp.concatenate(pieces), own_mix)
    if is_square("fsdp"):
        stack = jnp.stack([small, across(small, 1), across(small, 2), across(small, 3)])
        stack = jnp.stack([lax.dynamic_index_in_dim(stack, shard ^ i, 0, False) for i in range(4)])
    else:
        stack = lax.all_gather(small, "fsdp")
    cuts = [0]
    for piece in pieces:
        cuts.append(cuts[-1] + piece.shape[0])
    gain_attn = stack[:, cuts[0] : cuts[1]].reshape(1, model).astype(F32)
    gain_mlp = stack[:, cuts[1] : cuts[2]].reshape(1, model).astype(F32)
    gain_head = stack[:, cuts[2] : cuts[3]].reshape(1, val_dim).astype(F32)

    def taps_of(at, part):
        array = stack[:, cuts[at] : cuts[at + 1]].reshape(shards, heads, taps_count, part)
        return jnp.transpose(array, (2, 1, 0, 3)).reshape(taps_count, -1)

    taps = jnp.concatenate([taps_of(3, key_part), taps_of(4, key_part), taps_of(5, val_part)], 1)
    taps = jnp.pad(taps.astype(F32), ((0, 8 - taps_count), (0, 0)))
    params = jnp.pad(
        jnp.stack([mine(decay_log, 0), mine(decay_bias, 0)]).astype(F32),
        ((0, 6), (0, 128 - heads)),
    )

    turns = ((layer - jnp.arange(layers, dtype=jnp.int32)) % layers).astype(jnp.int32)
    scalars = jnp.concatenate([(core * seg).reshape(1), lengths[:1], turns]).astype(jnp.int32)
    per_core, per_block = seg // CHUNK, rows // CHUNK
    ids = jnp.arange(2 * per_core, dtype=jnp.int32)
    within = ids % per_core
    order = (
        jnp.where(ids // per_core == core, 0, per_core)
        + ((layer - within // per_block) % layers) * per_block
        + within % per_block
    ).astype(jnp.int32)
    live_own = (
        core * seg + layer * rows + jnp.arange(rows, dtype=jnp.int32) < lengths[0]
    ).astype(F32)[:, None]
    tokens_own = lax.dynamic_slice_in_dim(inputs[0], layer * rows, rows, 0).astype(F32)
    d_out_own = lax.dynamic_slice_in_dim(cotangent[0], layer * rows, rows, 0).astype(F32)
    normed_own, d_branch_own = arrange(scalars, inputs[0], cotangent[0], gain_attn, layers)
    own_side, own_feed = pack_rest(core_id, w_outgate, w_out, w_gate, w_up, w_down)
    full_mix, (_, own_side, own_feed), (normed, d_branch_other) = gathered_rows(
        own_mix,
        (normed_own, own_side, own_feed),
        lambda held: (
            jnp.concatenate([held[0], swapped(held[0])], 0),
            swapped(after(d_branch_own, held[0])),
        ),
    )
    side = lax.all_gather(own_side, "fsdp", axis=0, tiled=True)
    d_branch = (d_branch_own, d_branch_other)

    projected = dot(normed, full_mix)
    feed = lax.all_gather(after(own_feed, projected), "fsdp", axis=0, tiled=True)
    side = side.reshape(shards, 2, depth, tall)
    feed = feed.reshape(shards, 3, depth, units)
    mixed, states, inverses, news, active, sigma = mixer_forward(
        order, projected, taps, params, heads, key_dim, val_dim
    )
    gates, heads_out, attn_other, attn_own = head_outputs(normed, mixed, side, gain_head, heads)
    attn = line_sum_hops(core_sum(attn_other, attn_own))
    middle = tokens_own + live_own * attn
    mlp_scale = norm_parts(middle, 1e-6)
    hidden_own = (middle * mlp_scale * gain_mlp).astype(BF16)
    hidden_mine = jnp.concatenate(line_gather(hidden_own), 0)
    hidden = (hidden_mine, swapped(hidden_mine))

    stack_own, d_hidden_mine, branch_mine = feed_forward(turns, hidden[0], d_branch[0], feed)
    stack_other, d_hidden_other, branch_other = feed_forward(turns, hidden[1], d_branch[1], feed)
    d_hidden_core = core_sum(d_hidden_other, d_hidden_mine)
    d_hidden = lax.psum_scatter(d_hidden_core, "tensor", scatter_dimension=0, tiled=True)
    held = lax.optimization_barrier((stack_own, stack_other, branch_other, d_hidden_core))
    grad_feed = feed_grads(hidden, d_branch, held[:2], shards)
    branch_core = core_sum(held[2], branch_mine)
    d_hidden, grad_feed, branch_core = lax.optimization_barrier((d_hidden, grad_feed, branch_core))
    sum_feed = scattered(grad_feed)
    d_hidden = d_hidden.astype(F32)

    grad_mlp = jnp.sum(d_hidden * middle * mlp_scale, 0)
    d_middle = d_out_own + norm_back(d_hidden, middle, mlp_scale, gain_mlp)
    d_attn_mine = jnp.concatenate(line_gather((live_own * d_middle).astype(BF16)), 0)
    branch_core, d_attn_mine = lax.optimization_barrier((branch_core, d_attn_mine))
    d_attn = (d_attn_mine, swapped(d_attn_mine))


    d_mix, d_taps, d_params, d_gain = mixer_backward(
        order, projected, active, sigma, taps, params, states, inverses, news, mixed, gates,
        *d_attn, side, gain_head, heads, key_dim, val_dim,
    )
    branch, d_mix = line_sum(branch_core, (d_mix,))
    out_own = (middle + live_own * branch).astype(BF16)
    out_own, sum_feed, d_mix = lax.optimization_barrier((out_own, sum_feed, d_mix))
    side_at = width + 128

    hops = [(out_own, out_own)]
    hops.append(line_hop(*hops[-1], 1))
    d_normed_other, d_normed_mine, weighted = d_normed_rows(d_mix, normed, full_mix, side)
    hops[1], d_normed_other, d_normed_mine = lax.optimization_barrier(
        (hops[1], d_normed_other, d_normed_mine)
    )
    hops.append(line_hop(*hops[-1], 2))
    grad_out = out_grads(*d_attn, heads_out, shards)
    d_normed_other, grad_out = lax.optimization_barrier((swapped(d_normed_other), grad_out))
    sum_out = scattered(grad_out)
    d_normed_core = (d_normed_mine.astype(F32) + d_normed_other.astype(F32)).astype(BF16)

    small_sum = {"value": jnp.concatenate([weighted[0] / gain_attn[0], grad_mlp, d_gain[0]])}
    axes = ("context", "tensor", "fsdp")
    pairs = [
        (axis, 1 << k) for axis in axes for k in range((lax.axis_size(axis) - 1).bit_length())
    ]
    taps_line = jnp.concatenate([d_taps[:taps_count].reshape(-1), d_params[:2].reshape(-1)])

    def advance(hop):
        if not pairs:
            return hop
        axis, flip = pairs.pop(0)
        value = small_sum["value"]
        if axis == "fsdp" and flip == 1:
            value = jnp.concatenate([value, taps_line])
        value = after(value, d_normed_core)
        other = lax.ppermute(value, axis, [(i, i ^ flip) for i in range(lax.axis_size(axis))])
        hop, other = lax.optimization_barrier((hop, other))
        small_sum["value"] = value + other
        return hop

    work = {}

    def with_rest(step, hop):
        if step == 1:
            grad_mix = mix_grads(normed, after(d_mix, d_normed_core), shards)
            hop, hops[:], grad_mix = lax.optimization_barrier((hop, hops, grad_mix))
            work["mix"] = scattered(grad_mix)
        else:
            while len(hops) < (layers if step == layers - 1 else step + 2):
                hops.append(line_hop(*hops[-1], len(hops)))
        if step == 2:
            done = finish(
                core_id, sum_feed, swapped(sum_feed), ((0, units), (units, units)),
                (2 * units, units),
            )
            hop, work["feed"], hops[:] = lax.optimization_barrier((hop, done, hops))
        if step == 3:
            hop, work["output"] = lax.optimization_barrier((hop, place(turns, flat(hops))))
        return advance(hop)

    d_normed = line_sum_hops(d_normed_core, with_rest)
    output = work["output"] if "output" in work else place(turns, flat(hops))
    d_tokens = norm_back(d_normed, tokens_own, norm_parts(tokens_own, 1e-6), gain_attn)
    grad_own = (d_middle + d_tokens).astype(BF16)
    back = [(grad_own, grad_own)]
    for step in range(1, layers):
        hop = line_hop(*back[-1], step)
        if step == 1:
            out_done = finish(core_id, sum_out, swapped(sum_out), (), (0, tall))
            hop, (g_out,) = lax.optimization_barrier((hop, out_done))
        back.append(advance(hop))
    while pairs:
        advance(())
    vector = small_sum["value"]
    g_attn = lax.dynamic_slice_in_dim(vector, shard * depth, depth, 0)
    g_mlp = lax.dynamic_slice_in_dim(vector, model + shard * depth, depth, 0)
    g_head = lax.dynamic_slice_in_dim(vector, 2 * model + shard * val_part, val_part, 0)
    mine_taps = vector[2 * model + val_dim :]
    local = jnp.stack([mine_taps, swapped(mine_taps)])
    table = jnp.where(core == 0, local, local[::-1])
    tap_table = table[:, : taps_count * width].reshape(2, taps_count, width)
    param_table = table[:, taps_count * width :].reshape(2, 2, 128)
    d_log, d_bias = param_table[:, 0, :heads].reshape(-1), param_table[:, 1, :heads].reshape(-1)

    def tap_grad(begin, size):
        array = tap_table[:, :, begin : begin + heads * size].reshape(2, taps_count, heads, size)
        part = lax.dynamic_slice_in_dim(array, shard * (size // shards), size // shards, 3)
        return jnp.transpose(part, (0, 2, 1, 3)).reshape(all_heads, taps_count, size // shards)

    d_conv_q, d_conv_k, d_conv_v = (
        tap_grad(0, key_dim), tap_grad(wide, key_dim), tap_grad(2 * wide, val_dim)
    )

    g_gate, g_up, g_down = work["feed"]
    input_grad = place(turns, flat(back))[None]
    low_mix, input_grad = lax.optimization_barrier((work["mix"], input_grad))
    other_mix = swapped(low_mix)
    g_query, g_key, g_value, g_outgate = finish(
        core_id, low_mix, other_mix,
        ((0, wide), (wide, wide), (2 * wide, tall), (side_at, tall)), None,
    )

    def narrow(begin):
        own, other = low_mix[:, begin : begin + heads], other_mix[:, begin : begin + heads]
        return jnp.where(
            core == 0, jnp.concatenate([own, other], 1), jnp.concatenate([other, own], 1)
        ).astype(F32)

    return (
        output[None],
        input_grad,
        g_attn,
        g_query,
        g_key,
        g_value,
        narrow(width),
        narrow(width + heads),
        d_log,
        d_bias,
        d_conv_q,
        d_conv_k,
        d_conv_v,
        g_outgate,
        g_head,
        g_out,
        g_mlp,
        g_gate,
        g_up,
        g_down,
    )


def solution(mesh):
    placed = (
        P("fsdp", "context", None),
        P("fsdp"),
        P("fsdp"),
        P("fsdp", "tensor"),
        P("fsdp", "tensor"),
        P("fsdp", "tensor"),
        P("fsdp", "tensor"),
        P("fsdp", "tensor"),
        P("tensor"),
        P("tensor"),
        P("tensor", None, "fsdp"),
        P("tensor", None, "fsdp"),
        P("tensor", None, "fsdp"),
        P("fsdp", "tensor"),
        P("fsdp"),
        P("tensor", "fsdp"),
        P("fsdp"),
        P("fsdp", "tensor"),
        P("fsdp", "tensor"),
        P("tensor", "fsdp"),
        P("fsdp", "context", None),
    )
    return jax.shard_map(
        on_device,
        mesh=mesh,
        in_specs=placed,
        out_specs=(placed[0], placed[0]) + placed[2:20],
        check_vma=False,
    )
```

```python
import functools
import jax
import jax.numpy as jnp
from jax import lax
from jax.experimental import pallas as pl
from jax.experimental.pallas import tpu as pltpu
from jax.sharding import PartitionSpec as P

F32 = jnp.float32
BF16 = jnp.bfloat16
CHUNK = 128
exact = lax.Precision.HIGHEST
NN = ((1,), (0,))
NT = ((1,), (1,))
TN = ((0,), (0,))


def mm(a, b, dims=NN):
    return lax.dot_general(
        a.astype(BF16), b.astype(BF16), (dims, ((), ())), preferred_element_type=F32
    )


def mm_exact(a, b, dims=NN):
    return lax.dot_general(a, b, (dims, ((), ())), precision=exact, preferred_element_type=F32)


def small_cost():
    return pl.CostEstimate(flops=1, bytes_accessed=1, transcendentals=0)


def grid_ids(size):
    rows = lax.broadcasted_iota(jnp.int32, (size, size), 0)
    cols = lax.broadcasted_iota(jnp.int32, (size, size), 1)
    return rows, cols


def softplus(v):
    return jnp.maximum(v, 0.0) + jnp.log1p(jnp.exp(-jnp.abs(v)))


def rates_of(rates, params, heads, triangle):
    lanes = lax.broadcasted_iota(jnp.int32, rates.shape, 1)
    shifted = rates + params[1:2, :]
    scale = jnp.exp(params[0:1, :])
    logdecay = jnp.where(lanes < heads, -scale * softplus(shifted), 0.0)
    running = mm_exact(triangle, logdecay)
    last = running[CHUNK - 1 : CHUNK, :]
    return (
        jax.nn.sigmoid(rates),
        shifted,
        scale,
        logdecay,
        running,
        jnp.transpose(running),
        jnp.exp(running),
        jnp.exp(last - running),
        jnp.exp(last),
    )


def convolved(window, taps, rows):
    total = taps[0:1, :] * window[5 : 5 + rows, :]
    for j in range(1, 4):
        total = total + taps[j : j + 1, :] * window[5 + j : 5 + j + rows, :]
    return total


PER = 2
FORWARD_PER = 4


def inverses_of(systems, rows, cols):
    eye = (rows == cols).astype(F32)
    near = [jnp.where(rows // 8 == cols // 8, s, 0.0).astype(BF16) for s in systems]
    second = [mm(n, n) for n in near]
    low = [s.astype(BF16) for s in second]
    third = [mm(s, n) for s, n in zip(low, near)]
    fourth = [mm(s, s) for s in low]
    partial = [eye - n.astype(F32) + s - t for n, s, t in zip(near, second, third)]
    result = [p + mm(p, f) for p, f in zip(partial, fourth)]
    size = 8
    while size < CHUNK:
        step = min(4, CHUNK // size)
        inside = (rows // (step * size) == cols // (step * size)) & (rows // size > cols // size)
        off = [jnp.where(inside, s, 0.0).astype(BF16) for s in systems]
        low = [r.astype(BF16) for r in result]
        reach = [mm(o, r).astype(BF16) for o, r in zip(off, low)]
        twice = [mm(r, r) for r in reach]
        once = [r - mm(x, y) for r, x, y in zip(result, low, reach)]
        result = [o + mm(o, t) for o, t in zip(once, twice)]
        size *= step
    high = [s.astype(BF16) for s in systems]
    rest = [s - h.astype(F32) for s, h in zip(systems, high)]
    low = [r.astype(BF16) for r in result]
    tail = [r - x.astype(F32) for r, x in zip(result, low)]
    left = [
        eye - (r + mm(h, x) + mm(e, x) + mm(h, t))
        for r, h, x, e, t in zip(result, high, low, rest, tail)
    ]
    return [r + mm(x, d) for r, x, d in zip(result, low, left)]


def forward_kernel(heads, key_dim, val_dim, order_ref, *refs):
    pre_refs, refs = refs[:FORWARD_PER], refs[FORWARD_PER:]
    (
        taps_ref, params_ref, mixed_ref, states_ref, inverse_ref, new_ref, active_ref, sigma_ref,
        state, window,
    ) = refs
    step = pl.program_id(0)
    wide = heads * key_dim
    width = window.shape[1]
    span = FORWARD_PER * CHUNK

    @pl.when(step == 0)
    def _():
        state[...] = jnp.zeros_like(state)
        window[0:8, :] = jnp.zeros((8, width), F32)

    for c in range(FORWARD_PER):
        window[8 + c * CHUNK : 8 + (c + 1) * CHUNK, :] = (
            pre_refs[c][:, :width].astype(BF16).astype(F32)
        )
    summed = convolved(window, taps_ref, span)
    window[0:8, :] = window[span : span + 8, :]
    sigma = jax.nn.sigmoid(summed)
    active = summed * sigma
    active_ref[...] = active
    sigma_ref[...] = sigma
    rows, cols = grid_ids(CHUNK)
    causal = rows >= cols
    strict = rows > cols
    triangle = causal.astype(F32)
    rates = [rates_of(pre_refs[c][:, width:], params_ref, heads, triangle) for c in range(FORWARD_PER)]
    chains = [(c, h) for c in range(FORWARD_PER) for h in range(heads)]

    def piece(at, c, h, size):
        return active[c * CHUNK : (c + 1) * CHUNK, at + h * size : at + (h + 1) * size]

    def unit(values, factor):
        return values * (lax.rsqrt(jnp.sum(values * values, -1, keepdims=True) + 1e-6) * factor)

    query = [unit(piece(0, c, h, key_dim), key_dim ** -0.5) for c, h in chains]
    keys = [unit(piece(wide, c, h, key_dim), 1.0) for c, h in chains]
    values = [piece(2 * wide, c, h, val_dim) for c, h in chains]
    beta = [rates[c][0][:, heads + h : heads + h + 1] for c, h in chains]
    decay = [rates[c][6][:, h : h + 1] for c, h in chains]
    ratios = [
        jnp.where(
            causal,
            jnp.exp(jnp.where(causal, rates[c][4][:, h : h + 1] - rates[c][5][h : h + 1, :], 0.0)),
            0.0,
        )
        for c, h in chains
    ]
    dots = [mm(jnp.concatenate([k, q], 0), k, NT) for k, q in zip(keys, query)]
    systems = [
        jnp.where(strict, b * d[:CHUNK] * r, 0.0) for b, d, r in zip(beta, dots, ratios)
    ]
    scores = [(d[CHUNK:] * r).astype(BF16) for d, r in zip(dots, ratios)]
    inverse = [x.astype(BF16) for x in inverses_of(systems, rows, cols)]
    solved = [
        mm(x, jnp.concatenate([(b * e) * k, b * v], 1))
        for x, b, e, k, v in zip(inverse, beta, decay, keys, values)
    ]
    for i, (c, h) in enumerate(chains):
        inverse_ref[(c * heads + h) * CHUNK : (c * heads + h + 1) * CHUNK, :] = inverse[i]
    for c in range(FORWARD_PER):
        place = pl.multiple_of(order_ref[step * FORWARD_PER + c] * CHUNK, CHUNK)
        for h in range(heads):
            i = c * heads + h
            begin = state[h * key_dim : (h + 1) * key_dim, :]
            begin_low = begin.astype(BF16)
            states_ref[(c * heads + h) * key_dim : (c * heads + h + 1) * key_dim, :] = begin_low
            through = mm(
                jnp.concatenate([solved[i][:, :key_dim], query[i] * decay[i]], 0), begin_low
            )
            new = (solved[i][:, key_dim:] - through[:CHUNK]).astype(BF16)
            mixed_ref[pl.ds(place, CHUNK), h * val_dim : (h + 1) * val_dim] = through[
                CHUNK:
            ] + mm(scores[i], new)
            state[h * key_dim : (h + 1) * key_dim, :] = rates[c][8][:, h : h + 1] * begin + mm(
                keys[i] * rates[c][7][:, h : h + 1], new, TN
            )
            new_ref[c * CHUNK : (c + 1) * CHUNK, h * val_dim : (h + 1) * val_dim] = new


def backward_kernel(heads, key_dim, val_dim, order_ref, *refs):
    pre_refs, refs = refs[:PER], refs[PER:]
    active_ref, sigma_ref, taps_ref, params_ref, states_ref, inverse_ref, new_ref = refs[:7]
    mixed_refs, refs = refs[7 : 7 + PER], refs[7 + PER :]
    gates_refs, refs = refs[:PER], refs[PER:]
    own_refs, refs = refs[:PER], refs[PER:]
    other_refs, refs = refs[:PER], refs[PER:]
    (side_ref, gain_ref, d_pre_ref, d_taps_ref, d_params_ref, d_gain_ref, d_state, after) = (
        refs
    )
    step = pl.program_id(0)
    steps = pl.num_programs(0)
    wide = heads * key_dim
    width = after.shape[1]
    span = PER * CHUNK
    first = (steps - 1 - step) * PER

    @pl.when(step == 0)
    def _():
        d_state[...] = jnp.zeros_like(d_state)
        after[span : span + 8, :] = jnp.zeros((8, width), F32)
        d_taps_ref[...] = jnp.zeros_like(d_taps_ref)
        d_params_ref[...] = jnp.zeros_like(d_params_ref)
        d_gain_ref[...] = jnp.zeros_like(d_gain_ref)

    active = active_ref[...]
    sigma = sigma_ref[...]
    slope = sigma + active * (1.0 - sigma)
    rows, cols = grid_ids(CHUNK)
    causal = rows >= cols
    strict = rows > cols
    triangle = causal.astype(F32)
    rates = [rates_of(pre_refs[c][:, width:], params_ref, heads, triangle) for c in range(PER)]
    chains = [(c, h) for c in range(PER) for h in range(heads)]
    places = [pl.multiple_of(order_ref[first + c] * CHUNK, CHUNK) for c in range(PER)]
    d_attn = jnp.concatenate(
        [
            jnp.where(order_ref[first + c] < steps * PER // 2, own_refs[c][...], other_refs[c][...])
            for c in range(PER)
        ],
        0,
    )
    depth = side_ref.shape[2]
    d_heads = mm(d_attn[:, :depth], side_ref[0, 0])
    for f in range(1, side_ref.shape[0]):
        d_heads = d_heads + mm(d_attn[:, f * depth : (f + 1) * depth], side_ref[f, 0])
    gain = gain_ref[...]

    def piece(array, at, c, h, size):
        return array[c * CHUNK : (c + 1) * CHUNK, at + h * size : at + (h + 1) * size]

    def scale_of(values):
        return lax.rsqrt(jnp.sum(values * values, -1, keepdims=True) + 1e-6)

    q_act = [piece(active, 0, c, h, key_dim) for c, h in chains]
    k_act = [piece(active, wide, c, h, key_dim) for c, h in chains]
    values = [piece(active, 2 * wide, c, h, val_dim) for c, h in chains]
    q_scale = [scale_of(x) for x in q_act]
    k_scale = [scale_of(x) for x in k_act]
    q_unit = [x * s for x, s in zip(q_act, q_scale)]
    keys = [x * s for x, s in zip(k_act, k_scale)]
    query = [x * key_dim ** -0.5 for x in q_unit]
    keys_low = [x.astype(BF16) for x in keys]
    query_low = [x.astype(BF16) for x in query]
    beta = [rates[c][0][:, heads + h : heads + h + 1] for c, h in chains]
    decay = [rates[c][6][:, h : h + 1] for c, h in chains]
    remain = [rates[c][7][:, h : h + 1] for c, h in chains]
    whole = [rates[c][8][:, h : h + 1] for c, h in chains]
    lead = [b * e for b, e in zip(beta, decay)]
    ratios = [
        jnp.where(
            causal,
            jnp.exp(jnp.where(causal, rates[c][4][:, h : h + 1] - rates[c][5][h : h + 1, :], 0.0)),
            0.0,
        )
        for c, h in chains
    ]
    d_mixed = []
    for c, h in chains:
        at = slice(h * val_dim, (h + 1) * val_dim)
        mixed = mixed_refs[c][:, at]
        gates = gates_refs[c][:, at]
        d_out = piece(d_heads, 0, c, h, val_dim)
        m_scale = lax.rsqrt(jnp.mean(mixed * mixed, -1, keepdims=True) + 1e-5)
        unit = mixed * m_scale
        g_sigma = jax.nn.sigmoid(gates)
        gated = gates * g_sigma
        weighted = d_out * unit
        d_pre_ref[
            pl.ds(places[c], CHUNK), width + 128 + h * val_dim : width + 128 + (h + 1) * val_dim
        ] = (weighted * gain * (g_sigma * (1.0 + gates * (1.0 - g_sigma)))).astype(BF16)
        d_gain_ref[0:1, :] += jnp.sum(weighted * gated, 0, keepdims=True)
        d_unit = d_out * gated * gain
        d_mixed.append(
            (m_scale * (d_unit - unit * jnp.mean(d_unit * unit, -1, keepdims=True))).astype(BF16)
        )
    dots = [mm(jnp.concatenate([k, q], 0), k, NT) for k, q in zip(keys_low, query_low)]
    weights = [jnp.where(strict, d[:CHUNK] * r, 0.0) for d, r in zip(dots, ratios)]
    scores = [d[CHUNK:] * r for d, r in zip(dots, ratios)]
    begin = [
        states_ref[(c * heads + h) * key_dim : (c * heads + h + 1) * key_dim, :] for c, h in chains
    ]
    inverse = [
        inverse_ref[(c * heads + h) * CHUNK : (c * heads + h + 1) * CHUNK, :] for c, h in chains
    ]
    new = [
        new_ref[c * CHUNK : (c + 1) * CHUNK, h * val_dim : (h + 1) * val_dim] for c, h in chains
    ]
    straight = [mm(s, d, TN) for s, d in zip(scores, d_mixed)]
    kept = [(k * r).astype(BF16) for k, r in zip(keys, remain)]
    both = [mm(x, jnp.concatenate([s.astype(BF16), k], 1), TN) for x, s, k in zip(inverse, straight, kept)]
    fixed = [mm(q * e, d, TN) for q, e, d in zip(query, decay, d_mixed)]
    pull = [(l * k).astype(BF16) for l, k in zip(lead, keys)]
    d_end = [None] * len(chains)
    solved = [None] * len(chains)
    for c in reversed(range(PER)):
        for h in range(heads):
            i = c * heads + h
            at = slice(h * key_dim, (h + 1) * key_dim)
            d_end[i] = d_state[at, :]
            solved[i] = both[i][:, :val_dim] + mm(both[i][:, val_dim:], d_end[i])
            d_state[at, :] = whole[i] * d_end[i] + fixed[i] - mm(pull[i], solved[i], TN)
    end_low = [d.astype(BF16) for d in d_end]
    outer = [
        mm(jnp.concatenate([d, s.astype(BF16)], 0), jnp.concatenate([b, n], 0), NT)
        for d, s, b, n in zip(d_mixed, solved, begin, new)
    ]
    d_kept = [mm(n, d, NT) for n, d in zip(new, end_low)]
    d_scores = [jnp.where(causal, o[:CHUNK, key_dim:], 0.0) for o in outer]
    d_system = [jnp.where(strict, -o[CHUNK:, key_dim:], 0.0) for o in outer]
    d_dots = [
        jnp.concatenate([(d * r).astype(BF16), (e * (b * r)).astype(BF16)], 0)
        for d, e, b, r in zip(d_scores, d_system, beta, ratios)
    ]
    near = [mm(d, low) for d, low in zip(d_dots, keys_low)]
    far = [
        mm(d, jnp.concatenate([q, k], 0), TN) for d, q, k in zip(d_dots, query_low, keys_low)
    ]
    lanes = lax.broadcasted_iota(jnp.int32, (CHUNK, 128), 1)
    row_ids = lax.broadcasted_iota(jnp.int32, (CHUNK, 1), 0)
    d_running = [jnp.zeros((CHUNK, 128), F32) for _ in range(PER)]
    d_strengths = [jnp.zeros((CHUNK, 128), F32) for _ in range(PER)]
    columns = [[] for _ in range(PER)]
    for i, (c, h) in enumerate(chains):
        d_query_state = outer[i][:CHUNK, :key_dim]
        d_keys_state = outer[i][CHUNK:, :key_dim]
        d_query = decay[i] * d_query_state + near[i][:CHUNK]
        d_keys = near[i][CHUNK:] + far[i] - lead[i] * d_keys_state + remain[i] * d_kept[i]
        along = decay[i] * jnp.sum(keys[i] * d_keys_state, -1, keepdims=True)
        weighed = d_system[i] * weights[i]
        d_beta = (
            jnp.sum(solved[i] * values[i], -1, keepdims=True)
            - along
            + jnp.sum(weighed, -1, keepdims=True)
        )
        joint = weighed * beta[i] + d_scores[i] * scores[i]
        left = remain[i] * jnp.sum(keys[i] * d_kept[i], -1, keepdims=True)
        total = jnp.sum(left, 0, keepdims=True) + whole[i] * jnp.sum(
            jnp.sum(d_end[i] * begin[i].astype(F32), -1, keepdims=True), 0, keepdims=True
        )
        d_run = (
            jnp.sum(joint, -1, keepdims=True)
            + decay[i] * jnp.sum(query[i] * d_query_state, -1, keepdims=True)
            - beta[i] * along
            - left
            + jnp.where(row_ids == CHUNK - 1, total, 0.0)
        )
        d_running[c] = jnp.where(lanes == h, d_run, d_running[c])
        columns[c].append(jnp.sum(joint, 0, keepdims=True))
        d_strengths[c] = jnp.where(lanes == heads + h, d_beta, d_strengths[c])
        d_q = d_query * key_dim ** -0.5
        d_q = q_scale[i] * (d_q - q_unit[i] * jnp.sum(q_unit[i] * d_q, -1, keepdims=True))
        d_k = k_scale[i] * (d_keys - keys[i] * jnp.sum(keys[i] * d_keys, -1, keepdims=True))
        here = slice(c * CHUNK, (c + 1) * CHUNK)
        after[here, h * key_dim : (h + 1) * key_dim] = d_q * piece(slope, 0, c, h, key_dim)
        after[here, wide + h * key_dim : wide + (h + 1) * key_dim] = d_k * piece(
            slope, wide, c, h, key_dim
        )
        after[here, 2 * wide + h * val_dim : 2 * wide + (h + 1) * val_dim] = (
            beta[i] * solved[i]
        ) * piece(slope, 2 * wide, c, h, val_dim)
    upper = (rows <= cols).astype(F32)
    for c in range(PER):
        strengths, shifted, scale, logdecay = rates[c][:4]
        turned = jnp.transpose(
            jnp.concatenate(columns[c] + [jnp.zeros((CHUNK - heads, CHUNK), F32)], 0)
        )
        d_logdecay = mm_exact(upper, d_running[c] - turned)
        d_shifted = jnp.where(lanes < heads, d_logdecay * (-scale) * jax.nn.sigmoid(shifted), 0.0)
        d_params_ref[0:1, :] += jnp.sum(d_logdecay * logdecay, 0, keepdims=True)
        d_params_ref[1:2, :] += jnp.sum(d_shifted, 0, keepdims=True)
        d_pre_ref[pl.ds(places[c], CHUNK), width : width + 128] = (
            d_shifted + d_strengths[c] * strengths * (1.0 - strengths)
        ).astype(BF16)
    total = None
    pre = jnp.concatenate([ref[:, :width].astype(BF16).astype(F32) for ref in pre_refs], 0)
    for j in range(4):
        shifted = after[3 - j : 3 - j + span, :]
        term = taps_ref[j : j + 1, :] * shifted
        total = term if total is None else total + term
        d_taps_ref[j : j + 1, :] += jnp.sum(pre * shifted, 0, keepdims=True)
    for c in range(PER):
        d_pre_ref[pl.ds(places[c], CHUNK), :width] = total[c * CHUNK : (c + 1) * CHUNK].astype(BF16)
    after[span : span + 8, :] = after[0:8, :]


def mixer_forward(order, pre, taps, params, heads, key_dim, val_dim):
    chunks = pre.shape[0] // CHUNK
    width = taps.shape[1]
    here = lambda c: lambda n, order: (order[n * FORWARD_PER + c], 0)
    plain = lambda n, order: (n, 0)
    fixed = lambda n, order: (0, 0)
    return pl.pallas_call(
        functools.partial(forward_kernel, heads, key_dim, val_dim),
        grid_spec=pltpu.PrefetchScalarGridSpec(
            num_scalar_prefetch=1,
            grid=(chunks // FORWARD_PER,),
            in_specs=[pl.BlockSpec((CHUNK, pre.shape[1]), here(c)) for c in range(FORWARD_PER)]
            + [pl.BlockSpec(taps.shape, fixed), pl.BlockSpec(params.shape, fixed)],
            out_specs=[
                pl.BlockSpec((pre.shape[0], heads * val_dim), fixed),
                pl.BlockSpec((FORWARD_PER * heads * key_dim, val_dim), plain),
                pl.BlockSpec((FORWARD_PER * heads * CHUNK, CHUNK), plain),
                pl.BlockSpec((FORWARD_PER * CHUNK, heads * val_dim), plain),
                pl.BlockSpec((FORWARD_PER * CHUNK, width), plain),
                pl.BlockSpec((FORWARD_PER * CHUNK, width), plain),
            ],
            scratch_shapes=[
                pltpu.VMEM((heads * key_dim, val_dim), F32),
                pltpu.VMEM((FORWARD_PER * CHUNK + 8, width), F32),
            ],
        ),
        out_shape=[
            jax.ShapeDtypeStruct((pre.shape[0], heads * val_dim), F32),
            jax.ShapeDtypeStruct((chunks * heads * key_dim, val_dim), BF16),
            jax.ShapeDtypeStruct((chunks * heads * CHUNK, CHUNK), BF16),
            jax.ShapeDtypeStruct((pre.shape[0], heads * val_dim), BF16),
            jax.ShapeDtypeStruct((pre.shape[0], width), F32),
            jax.ShapeDtypeStruct((pre.shape[0], width), F32),
        ],
        compiler_params=pltpu.CompilerParams(vmem_limit_bytes=62 * 2**20),
        cost_estimate=small_cost(),
        name="mixer_forward",
    )(order, *[pre] * FORWARD_PER, taps, params)


def mixer_backward(
    order, pre, active, sigma, taps, params, states, inverses, news, mixed, gates, d_own, d_other,
    side, gain, heads, key_dim, val_dim,
):
    chunks = pre.shape[0] // CHUNK
    width = taps.shape[1]
    out_width = heads * val_dim
    steps = chunks // PER
    half = chunks // 2
    at = lambda n, c, order: order[(steps - 1 - n) * PER + c]
    here = lambda c: lambda n, order: (at(n, c, order), 0)
    first = lambda c: lambda n, order: (jnp.minimum(at(n, c, order), half - 1), 0)
    second = lambda c: lambda n, order: (jnp.maximum(at(n, c, order) - half, 0), 0)
    plain = lambda n, order: (steps - 1 - n, 0)
    fixed = lambda n, order: (0, 0)
    each = lambda shape, place: [pl.BlockSpec(shape, place(c)) for c in range(PER)]
    return pl.pallas_call(
        functools.partial(backward_kernel, heads, key_dim, val_dim),
        grid_spec=pltpu.PrefetchScalarGridSpec(
            num_scalar_prefetch=1,
            grid=(steps,),
            in_specs=each((CHUNK, pre.shape[1]), here)
            + [
                pl.BlockSpec((PER * CHUNK, width), plain),
                pl.BlockSpec((PER * CHUNK, width), plain),
                pl.BlockSpec(taps.shape, fixed),
                pl.BlockSpec(params.shape, fixed),
                pl.BlockSpec((PER * heads * key_dim, val_dim), plain),
                pl.BlockSpec((PER * heads * CHUNK, CHUNK), plain),
                pl.BlockSpec((PER * CHUNK, out_width), plain),
            ]
            + each((CHUNK, out_width), here)
            + each((CHUNK, out_width), here)
            + each((CHUNK, d_own.shape[1]), first)
            + each((CHUNK, d_own.shape[1]), second)
            + [
                pl.BlockSpec(
                    (side.shape[0], 1) + side.shape[2:], lambda n, order: (0, 1, 0, 0)
                ),
                pl.BlockSpec((1, val_dim), fixed),
            ],
            out_specs=[
                pl.BlockSpec((pre.shape[0], pre.shape[1] + out_width), fixed),
                pl.BlockSpec((8, width), fixed),
                pl.BlockSpec((8, 128), fixed),
                pl.BlockSpec((8, val_dim), fixed),
            ],
            scratch_shapes=[
                pltpu.VMEM((heads * key_dim, val_dim), F32),
                pltpu.VMEM((PER * CHUNK + 8, width), F32),
            ],
        ),
        out_shape=[
            jax.ShapeDtypeStruct((pre.shape[0], pre.shape[1] + out_width), BF16),
            jax.ShapeDtypeStruct((8, width), F32),
            jax.ShapeDtypeStruct((8, 128), F32),
            jax.ShapeDtypeStruct((8, val_dim), F32),
        ],
        compiler_params=pltpu.CompilerParams(vmem_limit_bytes=56 * 2**20),
        cost_estimate=small_cost(),
        name="mixer_backward",
    )(
        order, *[pre] * PER, active, sigma, taps, params, states, inverses, news, *[mixed] * PER,
        *[gates] * PER, *[d_own] * PER, *[d_other] * PER, side, gain,
    )


def roomy():
    return dict(
        compiler_params=pltpu.CompilerParams(vmem_limit_bytes=56 * 2**20),
        cost_estimate=small_cost(),
    )


def pack_mix_kernel(heads, core_ref, q_ref, k_ref, v_ref, decay_ref, strength_ref, out_ref):
    first = core_ref[0] == 0
    wide, tall = q_ref.shape[1], v_ref.shape[1]
    out_ref[:, :wide] = q_ref[...]
    out_ref[:, wide : 2 * wide] = k_ref[...]
    out_ref[:, 2 * wide : 2 * wide + tall] = v_ref[...]

    rates = jnp.transpose(
        jnp.concatenate([decay_ref[...].astype(F32), strength_ref[...].astype(F32)], 0)
    )
    pick = lambda at: jnp.where(
        first, rates[:, at : at + heads], rates[:, at + heads : at + 2 * heads]
    )
    rows = out_ref.shape[0]
    out_ref[:, 2 * wide + tall :] = jnp.concatenate(
        [pick(0), pick(2 * heads), jnp.zeros((rows, 128 - 2 * heads), F32)], 1
    ).astype(BF16)


def pack_mix(core, heads, w_query, w_key, w_value, w_decay, w_strength):
    depth = w_query.shape[0]
    wide, tall = w_query.shape[1] // 2, w_value.shape[1] // 2
    here = lambda i, core: (0, core[0])
    fixed = lambda i, core: (0, 0)
    return pl.pallas_call(
        functools.partial(pack_mix_kernel, heads),
        grid_spec=pltpu.PrefetchScalarGridSpec(
            num_scalar_prefetch=1,
            grid=(1,),
            in_specs=[
                pl.BlockSpec((depth, wide), here),
                pl.BlockSpec((depth, wide), here),
                pl.BlockSpec((depth, tall), here),
                pl.BlockSpec(w_decay.shape[::-1], fixed),
                pl.BlockSpec(w_strength.shape[::-1], fixed),
            ],
            out_specs=pl.BlockSpec((depth, 2 * wide + tall + 128), fixed),
        ),
        out_shape=jax.ShapeDtypeStruct((depth, 2 * wide + tall + 128), BF16),
        name="pack_mix",
        **roomy(),
    )(core, w_query, w_key, w_value, w_decay.T, w_strength.T)


def pack_rest_kernel(core_ref, outgate_ref, out_ref, gate_ref, up_ref, down_ref, side_ref, wide_ref):
    first = core_ref[0] == 0
    depth = outgate_ref.shape[0]
    units = gate_ref.shape[1] // 2
    side_ref[:depth, :] = outgate_ref[...]
    side_ref[depth:, :] = jnp.transpose(out_ref[...].astype(F32)).astype(BF16)
    for at, ref in ((0, gate_ref), (1, up_ref)):
        values = ref[...]
        wide_ref[at * depth : (at + 1) * depth, :] = jnp.where(
            first, values[:, :units], values[:, units:]
        )
    wide_ref[2 * depth :, :] = jnp.transpose(down_ref[...].astype(F32)).astype(BF16)


def pack_rest(core, w_outgate, w_out, w_gate, w_up, w_down):
    depth = w_outgate.shape[0]
    tall, units = w_outgate.shape[1] // 2, w_gate.shape[1] // 2
    fixed = lambda i, core: (0, 0)
    return pl.pallas_call(
        pack_rest_kernel,
        grid_spec=pltpu.PrefetchScalarGridSpec(
            num_scalar_prefetch=1,
            grid=(1,),
            in_specs=[
                pl.BlockSpec((depth, tall), lambda i, core: (0, core[0])),
                pl.BlockSpec((tall, depth), lambda i, core: (core[0], 0)),
                pl.BlockSpec(w_gate.shape, fixed),
                pl.BlockSpec(w_up.shape, fixed),
                pl.BlockSpec((units, depth), lambda i, core: (core[0], 0)),
            ],
            out_specs=[
                pl.BlockSpec((2 * depth, tall), fixed),
                pl.BlockSpec((3 * depth, units), fixed),
            ],
        ),
        out_shape=[
            jax.ShapeDtypeStruct((2 * depth, tall), BF16),
            jax.ShapeDtypeStruct((3 * depth, units), BF16),
        ],
        name="pack_rest",
        **roomy(),
    )(core, w_outgate, w_out, w_gate, w_up, w_down)


def arrange_kernel(scalars_ref, tokens_ref, cotangent_ref, gain_ref, normed_ref, branch_ref):
    step = pl.program_id(0)
    rows = tokens_ref.shape[0]
    tokens = tokens_ref[...].astype(F32)
    scale = lax.rsqrt(jnp.mean(tokens * tokens, -1, keepdims=True) + 1e-6)
    normed_ref[...] = (tokens * scale * gain_ref[...]).astype(BF16)
    place = scalars_ref[0] + scalars_ref[2 + step] * rows + lax.broadcasted_iota(
        jnp.int32, (rows, 1), 0
    )
    branch_ref[...] = jnp.where(place < scalars_ref[1], cotangent_ref[...], 0).astype(BF16)


def arrange(scalars, tokens, cotangent, gain, layers):
    rows, model = tokens.shape[0] // layers, tokens.shape[1]
    there = pl.BlockSpec((rows, model), lambda p, scalars: (scalars[2 + p], 0))
    plain = pl.BlockSpec((rows, model), lambda p, scalars: (p, 0))
    return pl.pallas_call(
        arrange_kernel,
        grid_spec=pltpu.PrefetchScalarGridSpec(
            num_scalar_prefetch=1,
            grid=(layers,),
            in_specs=[there, there, pl.BlockSpec((1, model), lambda p, scalars: (0, 0))],
            out_specs=[plain, plain],
        ),
        out_shape=[jax.ShapeDtypeStruct(tokens.shape, BF16)] * 2,
        name="arrange",
        **roomy(),
    )(scalars, tokens, cotangent, gain)


TILE = 256


def heads_kernel(
    heads, normed_ref, mixed_ref, side_ref, gain_ref, gates_ref, heads_ref, other_ref, own_ref
):
    step = pl.program_id(0)
    half = pl.num_programs(0) // 2
    shards, _, depth, tall = side_ref.shape
    val_dim = tall // heads
    gates = mm(normed_ref[:, :depth], side_ref[0, 0])
    for f in range(1, shards):
        gates = gates + mm(normed_ref[:, f * depth : (f + 1) * depth], side_ref[f, 0])
    gates_ref[...] = gates
    for h in range(heads):
        at = slice(h * val_dim, (h + 1) * val_dim)
        mixed = mixed_ref[:, at]
        gate = gates[:, at]
        scale = lax.rsqrt(jnp.mean(mixed * mixed, -1, keepdims=True) + 1e-5)
        heads_ref[:, at] = (
            mixed * scale * gain_ref[...] * (gate * jax.nn.sigmoid(gate))
        ).astype(BF16)
    low = heads_ref[...]

    def write(ref):
        for f in range(shards):
            ref[:, f * depth : (f + 1) * depth] = mm(low, side_ref[f, 1], NT).astype(BF16)

    @pl.when(step < half)
    def _():
        write(other_ref)

    @pl.when(step >= half)
    def _():
        write(own_ref)


def turned_specs(tiles):
    half = tiles // 2
    here = lambda i: (jnp.where(i < half, i + half, i - half), 0)
    other = lambda i: (jnp.minimum(i, half - 1), 0)
    own = lambda i: (jnp.maximum(i - half, 0), 0)
    return here, other, own


def head_outputs(normed, mixed, side, gain, heads):
    count, model = normed.shape
    tall = mixed.shape[1]
    here, other, own = turned_specs(count // TILE)
    return pl.pallas_call(
        functools.partial(heads_kernel, heads),
        grid=(count // TILE,),
        in_specs=[
            pl.BlockSpec((TILE, model), here),
            pl.BlockSpec((TILE, tall), here),
            pl.BlockSpec(side.shape, lambda i: (0, 0, 0, 0)),
            pl.BlockSpec(gain.shape, lambda i: (0, 0)),
        ],
        out_specs=[
            pl.BlockSpec((TILE, tall), here),
            pl.BlockSpec((TILE, tall), here),
            pl.BlockSpec((TILE, model), other),
            pl.BlockSpec((TILE, model), own),
        ],
        out_shape=[
            jax.ShapeDtypeStruct((count, tall), F32),
            jax.ShapeDtypeStruct((count, tall), BF16),
            jax.ShapeDtypeStruct((count // 2, model), BF16),
            jax.ShapeDtypeStruct((count // 2, model), BF16),
        ],
        name="head_outputs",
        **roomy(),
    )(normed, mixed, side, gain)


def feed_kernel(turns_ref, hidden_ref, branch_ref, wide_ref, stack_ref, d_hidden_ref, branch_out_ref):
    shards, _, depth, units = wide_ref.shape
    step = pl.program_id(0)
    rows = d_hidden_ref.shape[0] // turns_ref.shape[0]
    blocks = hidden_ref.shape[0] // rows

    def forward(ref, at):
        total = mm(ref[:, :depth], wide_ref[0, at])
        for f in range(1, shards):
            total = total + mm(ref[:, f * depth : (f + 1) * depth], wide_ref[f, at])
        return total

    gate = forward(hidden_ref, 0)
    up = forward(hidden_ref, 1)
    d_act = forward(branch_ref, 2)
    sigma = jax.nn.sigmoid(gate)
    silu = gate * sigma
    act = (silu * up).astype(BF16)
    d_gate = (d_act * up * (sigma + silu * (1.0 - sigma))).astype(BF16)
    d_up = (d_act * silu).astype(BF16)
    stack_ref[0] = d_gate
    stack_ref[1] = d_up
    stack_ref[2] = act
    for f in range(shards):
        at = slice(f * depth, (f + 1) * depth)
        d_hidden = (mm(d_gate, wide_ref[f, 0], NT) + mm(d_up, wide_ref[f, 1], NT)).astype(BF16)
        for k in range(blocks):
            place = pl.multiple_of(turns_ref[step * blocks + k] * rows, rows)
            d_hidden_ref[pl.ds(place, rows), at] = d_hidden[k * rows : (k + 1) * rows]
        branch_out_ref[:, at] = mm(act, wide_ref[f, 2], NT).astype(BF16)


def feed_forward(turns, hidden, branch, wide):
    count, model = hidden.shape
    units = wide.shape[3]
    tile = max(TILE, count // turns.shape[0])
    row = pl.BlockSpec((tile, model), lambda i, turns: (i, 0))
    return pl.pallas_call(
        feed_kernel,
        grid_spec=pltpu.PrefetchScalarGridSpec(
            num_scalar_prefetch=1,
            grid=(count // tile,),
            in_specs=[row, row, pl.BlockSpec(wide.shape, lambda i, turns: (0, 0, 0, 0))],
            out_specs=[
                pl.BlockSpec((3, tile, units), lambda i, turns: (0, i, 0)),
                pl.BlockSpec((count, model), lambda i, turns: (0, 0)),
                row,
            ],
        ),
        out_shape=[
            jax.ShapeDtypeStruct((3, count, units), BF16),
            jax.ShapeDtypeStruct((count, model), BF16),
            jax.ShapeDtypeStruct((count, model), BF16),
        ],
        name="feed_forward",
        **roomy(),
    )(turns, hidden, branch, wide)


def feed_grads_kernel(h_own, h_other, b_own, b_other, s_own, s_other, out_ref):
    units = s_own.shape[2]
    for at, own, other in ((0, h_own, h_other), (1, h_own, h_other), (2, b_own, b_other)):
        out_ref[:, at * units : (at + 1) * units] = (
            mm(own[...], s_own[at], TN) + mm(other[...], s_other[at], TN)
        ).astype(BF16)
    rest = out_ref.shape[1] - 3 * units
    if rest:
        out_ref[:, 3 * units :] = jnp.zeros((out_ref.shape[0], rest), BF16)


def feed_grads(hidden, branch, stacks, shards):
    count, model = hidden[0].shape
    units = stacks[0].shape[2]
    depth = model // shards
    width = -(-3 * units // 128) * 128
    part = pl.BlockSpec((count, depth), lambda f: (0, f))
    use_s = pl.BlockSpec((3, count, units), lambda f: (0, 0, 0))
    return pl.pallas_call(
        feed_grads_kernel,
        grid=(shards,),
        in_specs=[part, part, part, part, use_s, use_s],
        out_specs=pl.BlockSpec((depth, width), lambda f: (f, 0)),
        out_shape=jax.ShapeDtypeStruct((model, width), BF16),
        name="feed_grads",
        **roomy(),
    )(*hidden, *branch, *stacks)


def d_normed_kernel(side_at, mix_ref, normed_ref, weights_ref, side_ref, other_ref, own_ref, sum_ref):
    step = pl.program_id(0)
    half = pl.num_programs(0) // 2
    shards, _, depth, _ = side_ref.shape

    @pl.when(step == 0)
    def _():
        sum_ref[...] = jnp.zeros_like(sum_ref)

    def write(ref):
        for f in range(shards):
            at = slice(f * depth, (f + 1) * depth)
            part = mm(mix_ref[:, :side_at], weights_ref[at, :], NT) + mm(
                mix_ref[:, side_at:], side_ref[f, 0], NT
            )
            ref[:, at] = part.astype(BF16)
            sum_ref[0:1, at] += jnp.sum(part * normed_ref[:, at].astype(F32), 0, keepdims=True)

    @pl.when(step < half)
    def _():
        write(other_ref)

    @pl.when(step >= half)
    def _():
        write(own_ref)


def d_normed_rows(d_mix, normed, weights, side):
    count, model = normed.shape
    here, other, own = turned_specs(count // TILE)
    fixed = lambda i: (0, 0)
    return pl.pallas_call(
        functools.partial(d_normed_kernel, weights.shape[1]),
        grid=(count // TILE,),
        in_specs=[
            pl.BlockSpec((TILE, d_mix.shape[1]), here),
            pl.BlockSpec((TILE, model), here),
            pl.BlockSpec(weights.shape, fixed),
            pl.BlockSpec((side.shape[0], 1) + side.shape[2:], lambda i: (0, 0, 0, 0)),
        ],
        out_specs=[
            pl.BlockSpec((TILE, model), other),
            pl.BlockSpec((TILE, model), own),
            pl.BlockSpec((8, model), fixed),
        ],
        out_shape=[
            jax.ShapeDtypeStruct((count // 2, model), BF16),
            jax.ShapeDtypeStruct((count // 2, model), BF16),
            jax.ShapeDtypeStruct((8, model), F32),
        ],
        name="d_normed_rows",
        **roomy(),
    )(d_mix, normed, weights, side)


def mix_grads_kernel(normed_ref, mix_ref, out_ref):
    out_ref[...] = mm(normed_ref[...], mix_ref[...], TN).astype(BF16)


def mix_grads(normed, d_mix, shards):
    count, model = normed.shape
    depth, width = model // shards, d_mix.shape[1]
    return pl.pallas_call(
        mix_grads_kernel,
        grid=(shards,),
        in_specs=[
            pl.BlockSpec((count, depth), lambda f: (0, f)),
            pl.BlockSpec(d_mix.shape, lambda f: (0, 0)),
        ],
        out_specs=pl.BlockSpec((depth, width), lambda f: (f, 0)),
        out_shape=jax.ShapeDtypeStruct((model, width), BF16),
        name="mix_grads",
        **roomy(),
    )(normed, d_mix)


def out_grads_kernel(d_own_ref, d_other_ref, heads_ref, out_ref):
    half = d_own_ref.shape[0]
    out_ref[...] = (
        mm(d_own_ref[...], heads_ref[:half, :], TN) + mm(d_other_ref[...], heads_ref[half:, :], TN)
    ).astype(BF16)


def out_grads(d_own, d_other, heads_out, shards):
    count, model = d_own.shape
    depth, width = model // shards, heads_out.shape[1]
    column = pl.BlockSpec((count, depth), lambda f: (0, f))
    return pl.pallas_call(
        out_grads_kernel,
        grid=(shards,),
        in_specs=[column, column, pl.BlockSpec(heads_out.shape, lambda f: (0, 0))],
        out_specs=pl.BlockSpec((depth, width), lambda f: (f, 0)),
        out_shape=jax.ShapeDtypeStruct((model, width), BF16),
        name="out_grads",
        **roomy(),
    )(d_own, d_other, heads_out)


def place_kernel(turns_ref, *refs):
    parts, out_ref = refs[:-1], refs[-1]
    size = turns_ref.shape[0]
    rows = parts[0].shape[0]
    for p in range(size):
        at = pl.multiple_of(turns_ref[p] * rows, rows)
        if len(parts) == size:
            part = parts[p][...]
        elif p == 0:
            part = parts[0][...]
        else:
            part = parts[p][...] + parts[2 * size - 1 - p][...]
        out_ref[pl.ds(at, rows), :] = part


def place(turns, parts):
    size = turns.shape[0]
    rows, model = parts[0].shape
    whole = lambda i, turns: (0, 0)
    return pl.pallas_call(
        place_kernel,
        grid_spec=pltpu.PrefetchScalarGridSpec(
            num_scalar_prefetch=1,
            grid=(1,),
            in_specs=[pl.BlockSpec((rows, model), whole)] * len(parts),
            out_specs=pl.BlockSpec((size * rows, model), whole),
        ),
        out_shape=jax.ShapeDtypeStruct((size * rows, model), BF16),
        name="place",
        **roomy(),
    )(turns, *parts)


def finish_kernel(cuts, turned, core_ref, own_ref, other_ref, *refs):
    first = core_ref[0] == 0
    own, other = own_ref[...].astype(F32), other_ref[...].astype(F32)
    low, high = jnp.where(first, own, other), jnp.where(first, other, own)
    for (begin, size), ref in zip(cuts, refs):
        ref[:, :size] = low[:, begin : begin + size]
        ref[:, size:] = high[:, begin : begin + size]
    if turned is None:
        return
    begin, size = turned
    refs[-1][:size, :] = jnp.transpose(low[:, begin : begin + size])
    refs[-1][size:, :] = jnp.transpose(high[:, begin : begin + size])


def finish(core, own, other, cuts, turned):
    depth, width = own.shape
    row = lambda size: pl.BlockSpec((128, size), lambda i, core: (i, 0))
    shapes = [(depth, 2 * size) for _, size in cuts]
    specs = [row(2 * size) for _, size in cuts]
    if turned is not None:
        shapes.append((2 * turned[1], depth))
        specs.append(pl.BlockSpec((2 * turned[1], 128), lambda i, core: (0, i)))
    return pl.pallas_call(
        functools.partial(finish_kernel, cuts, turned),
        grid_spec=pltpu.PrefetchScalarGridSpec(
            num_scalar_prefetch=1,
            grid=(depth // 128,),
            in_specs=[row(width), row(width)],
            out_specs=specs,
        ),
        out_shape=[jax.ShapeDtypeStruct(shape, F32) for shape in shapes],
        name="finish",
        **roomy(),
    )(core, own, other)


def after(value, *others):
    return lax.optimization_barrier((value,) + others)[0]


def is_square(axis):
    return lax.axis_size(axis) == 4


def across(value, flip):
    return lax.ppermute(value, "fsdp", [(i, i ^ flip) for i in range(4)])


def swapped(value):
    return lax.ppermute(value, "context", [(0, 1), (1, 0)])


def gathered_rows(own, beside, later):
    if not is_square("fsdp"):
        return lax.all_gather(own, "fsdp", axis=0, tiled=True), beside, later(beside)
    rows = own.shape[0]
    half = rows // 2
    along_x = across(own, 1)
    along_y = across(own, 2)
    along_x, along_y, beside = lax.optimization_barrier((along_x, along_y, beside))
    low = across(along_x[:half], 2)
    high = across(along_y[half:], 1)
    low, high, extra = lax.optimization_barrier((low, high, later(beside)))
    shard = lax.axis_index("fsdp")
    whole = jnp.zeros((4 * rows,) + own.shape[1:], own.dtype)
    for place, part in ((0, own), (1, along_x), (2, along_y)):
        whole = lax.dynamic_update_slice_in_dim(whole, part, (shard ^ place) * rows, 0)
    whole = lax.dynamic_update_slice_in_dim(whole, low, (shard ^ 3) * rows, 0)
    return lax.dynamic_update_slice_in_dim(whole, high, (shard ^ 3) * rows + half, 0), beside, extra


def scattered(blocks):
    return lax.psum_scatter(blocks, "fsdp", scatter_dimension=0, tiled=True)


def line_sum(value, beside=(), axis="tensor"):
    size = lax.axis_size(axis)
    rows = value.shape[0] // size
    parts = [
        lax.ppermute(
            value[p * rows : (p + 1) * rows], axis, [(i, (i - p) % size) for i in range(size)]
        )
        for p in range(1, size)
    ]
    if beside:
        parts, beside = lax.optimization_barrier((parts, tuple(beside)))
    total = value[:rows].astype(F32)
    for part in parts:
        total = total + part.astype(F32)
    return (total, *beside) if beside else total


def line_sum_hops(value, beside=None, axis="tensor"):
    size = lax.axis_size(axis)
    rows = value.shape[0] // size
    block = lambda p: value[p * rows : (p + 1) * rows].astype(F32)
    right = left = None
    for step in range(1, size):
        send_r, send_l = block(step), block(size - step)
        if right is not None:
            send_r = send_r + right.astype(F32)
            send_l = send_l + left.astype(F32)
        right = lax.ppermute(send_r.astype(BF16), axis, [(i, i + 1) for i in range(step)])
        left = lax.ppermute(
            send_l.astype(BF16), axis, [(i, i - 1) for i in range(size - step, size)]
        )
        if beside:
            right, left = beside(step, (right, left))
    return block(0) + right.astype(F32) + left.astype(F32)


def line_gather(own, axis="tensor"):
    size = lax.axis_size(axis)
    rights, lefts = [own], [own]
    for step in range(1, size):
        rights.append(
            lax.ppermute(rights[-1], axis, [(i, i + 1) for i in range(step - 1, size - 1)])
        )
        lefts.append(lax.ppermute(lefts[-1], axis, [(i, i - 1) for i in range(1, size - step + 1)]))
    return [own] + [rights[k] + lefts[size - k] for k in range(1, size)]


def line_hop(right, left, step, axis="tensor"):
    size = lax.axis_size(axis)
    return (
        lax.ppermute(right, axis, [(i, i + 1) for i in range(step - 1, size - 1)]),
        lax.ppermute(left, axis, [(i, i - 1) for i in range(1, size - step + 1)]),
    )


def flat(hops):
    return [hops[0][0]] + [hop[0] for hop in hops[1:]] + [hop[1] for hop in hops[1:]]


def core_sum(other_rows, own_rows):
    return (own_rows.astype(F32) + swapped(other_rows).astype(F32)).astype(BF16)


def dot(a, b, dims=NN):
    return lax.dot_general(a, b, (dims, ((), ())), preferred_element_type=F32)


def norm_parts(values, epsilon):
    return lax.rsqrt(jnp.mean(values * values, -1, keepdims=True) + epsilon)


def norm_back(d_scaled, values, scale, gain):
    raised = d_scaled * gain
    return scale * raised - values * (
        scale * scale * scale * jnp.mean(raised * values, -1, keepdims=True)
    )


def on_device(
    inputs, lengths, norm_attn, w_query, w_key, w_value, w_decay, w_strength, decay_log,
    decay_bias, conv_query, conv_key, conv_value, w_outgate, norm_head, w_out, norm_mlp, w_gate,
    w_up, w_down, cotangent,
):
    shard, core, layer = (lax.axis_index(name) for name in ("fsdp", "context", "tensor"))
    shards, layers = lax.axis_size("fsdp"), lax.axis_size("tensor")
    seg, model = inputs.shape[1:]
    rows = seg // layers
    depth = norm_attn.shape[0]
    all_heads, taps_count, key_part = conv_query.shape
    val_part = conv_value.shape[2]
    heads = all_heads // 2
    key_dim, val_dim = key_part * shards, val_part * shards
    wide, tall = heads * key_dim, heads * val_dim
    width = 2 * wide + tall
    units = w_gate.shape[1] // 2

    def mine(array, dim):
        size = array.shape[dim] // 2
        first = lax.slice_in_dim(array, 0, size, axis=dim)
        second = lax.slice_in_dim(array, size, 2 * size, axis=dim)
        return jnp.where(core == 0, first, second)

    core_id = core.reshape(1).astype(jnp.int32)
    own_mix = pack_mix(core_id, heads, w_query, w_key, w_value, w_decay, w_strength)

    pieces = (
        norm_attn, norm_mlp, norm_head,
        mine(conv_query, 0).reshape(-1), mine(conv_key, 0).reshape(-1),
        mine(conv_value, 0).reshape(-1),
    )
    small = after(jnp.concatenate(pieces), own_mix)
    if is_square("fsdp"):
        stack = jnp.stack([small, across(small, 1), across(small, 2), across(small, 3)])
        stack = jnp.stack([lax.dynamic_index_in_dim(stack, shard ^ i, 0, False) for i in range(4)])
    else:
        stack = lax.all_gather(small, "fsdp")
    cuts = [0]
    for piece in pieces:
        cuts.append(cuts[-1] + piece.shape[0])
    gain_attn = stack[:, cuts[0] : cuts[1]].reshape(1, model).astype(F32)
    gain_mlp = stack[:, cuts[1] : cuts[2]].reshape(1, model).astype(F32)
    gain_head = stack[:, cuts[2] : cuts[3]].reshape(1, val_dim).astype(F32)

    def taps_of(at, part):
        array = stack[:, cuts[at] : cuts[at + 1]].reshape(shards, heads, taps_count, part)
        return jnp.transpose(array, (2, 1, 0, 3)).reshape(taps_count, -1)

    taps = jnp.concatenate([taps_of(3, key_part), taps_of(4, key_part), taps_of(5, val_part)], 1)
    taps = jnp.pad(taps.astype(F32), ((0, 8 - taps_count), (0, 0)))
    params = jnp.pad(
        jnp.stack([mine(decay_log, 0), mine(decay_bias, 0)]).astype(F32),
        ((0, 6), (0, 128 - heads)),
    )

    turns = ((layer - jnp.arange(layers, dtype=jnp.int32)) % layers).astype(jnp.int32)
    scalars = jnp.concatenate([(core * seg).reshape(1), lengths[:1], turns]).astype(jnp.int32)
    per_core, per_block = seg // CHUNK, rows // CHUNK
    ids = jnp.arange(2 * per_core, dtype=jnp.int32)
    within = ids % per_core
    order = (
        jnp.where(ids // per_core == core, 0, per_core)
        + ((layer - within // per_block) % layers) * per_block
        + within % per_block
    ).astype(jnp.int32)
    live_own = (
        core * seg + layer * rows + jnp.arange(rows, dtype=jnp.int32) < lengths[0]
    ).astype(F32)[:, None]
    tokens_own = lax.dynamic_slice_in_dim(inputs[0], layer * rows, rows, 0).astype(F32)
    d_out_own = lax.dynamic_slice_in_dim(cotangent[0], layer * rows, rows, 0).astype(F32)
    normed_own, d_branch_own = arrange(scalars, inputs[0], cotangent[0], gain_attn, layers)
    own_side, own_feed = pack_rest(core_id, w_outgate, w_out, w_gate, w_up, w_down)
    full_mix, (_, own_side, own_feed), (normed, d_branch_other) = gathered_rows(
        own_mix,
        (normed_own, own_side, own_feed),
        lambda held: (
            jnp.concatenate([held[0], swapped(held[0])], 0),
            swapped(after(d_branch_own, held[0])),
        ),
    )
    side = lax.all_gather(own_side, "fsdp", axis=0, tiled=True)
    d_branch = (d_branch_own, d_branch_other)

    projected = dot(normed, full_mix)
    feed = lax.all_gather(after(own_feed, projected), "fsdp", axis=0, tiled=True)
    side = side.reshape(shards, 2, depth, tall)
    feed = feed.reshape(shards, 3, depth, units)
    mixed, states, inverses, news, active, sigma = mixer_forward(
        order, projected, taps, params, heads, key_dim, val_dim
    )
    gates, heads_out, attn_other, attn_own = head_outputs(normed, mixed, side, gain_head, heads)
    attn = line_sum_hops(core_sum(attn_other, attn_own))
    middle = tokens_own + live_own * attn
    mlp_scale = norm_parts(middle, 1e-6)
    hidden_own = (middle * mlp_scale * gain_mlp).astype(BF16)
    hidden_mine = jnp.concatenate(line_gather(hidden_own), 0)
    hidden = (hidden_mine, swapped(hidden_mine))

    stack_own, d_hidden_mine, branch_mine = feed_forward(turns, hidden[0], d_branch[0], feed)
    stack_other, d_hidden_other, branch_other = feed_forward(turns, hidden[1], d_branch[1], feed)
    d_hidden_core = core_sum(d_hidden_other, d_hidden_mine)
    d_hidden = lax.psum_scatter(d_hidden_core, "tensor", scatter_dimension=0, tiled=True)
    held = lax.optimization_barrier((stack_own, stack_other, branch_other, d_hidden_core))
    grad_feed = feed_grads(hidden, d_branch, held[:2], shards)
    branch_core = core_sum(held[2], branch_mine)
    d_hidden, grad_feed, branch_core = lax.optimization_barrier((d_hidden, grad_feed, branch_core))
    sum_feed = scattered(grad_feed)
    d_hidden = d_hidden.astype(F32)

    grad_mlp = jnp.sum(d_hidden * middle * mlp_scale, 0)
    d_middle = d_out_own + norm_back(d_hidden, middle, mlp_scale, gain_mlp)
    d_attn_mine = jnp.concatenate(line_gather((live_own * d_middle).astype(BF16)), 0)
    branch_core, d_attn_mine = lax.optimization_barrier((branch_core, d_attn_mine))
    d_attn = (d_attn_mine, swapped(d_attn_mine))


    d_mix, d_taps, d_params, d_gain = mixer_backward(
        order, projected, active, sigma, taps, params, states, inverses, news, mixed, gates,
        *d_attn, side, gain_head, heads, key_dim, val_dim,
    )
    branch, d_mix = line_sum(branch_core, (d_mix,))
    out_own = (middle + live_own * branch).astype(BF16)
    out_own, sum_feed, d_mix = lax.optimization_barrier((out_own, sum_feed, d_mix))
    side_at = width + 128

    hops = [(out_own, out_own)]
    hops.append(line_hop(*hops[-1], 1))
    d_normed_other, d_normed_mine, weighted = d_normed_rows(d_mix, normed, full_mix, side)
    hops[1], d_normed_other, d_normed_mine = lax.optimization_barrier(
        (hops[1], d_normed_other, d_normed_mine)
    )
    hops.append(line_hop(*hops[-1], 2))
    grad_out = out_grads(*d_attn, heads_out, shards)
    d_normed_other, grad_out = lax.optimization_barrier((swapped(d_normed_other), grad_out))
    sum_out = scattered(grad_out)
    d_normed_core = (d_normed_mine.astype(F32) + d_normed_other.astype(F32)).astype(BF16)

    small_sum = {"value": jnp.concatenate([weighted[0] / gain_attn[0], grad_mlp, d_gain[0]])}
    axes = ("context", "tensor", "fsdp")
    pairs = [
        (axis, 1 << k) for axis in axes for k in range((lax.axis_size(axis) - 1).bit_length())
    ]
    taps_line = jnp.concatenate([d_taps[:taps_count].reshape(-1), d_params[:2].reshape(-1)])

    def advance(hop):
        if not pairs:
            return hop
        axis, flip = pairs.pop(0)
        value = small_sum["value"]
        if axis == "fsdp" and flip == 1:
            value = jnp.concatenate([value, taps_line])
        value = after(value, d_normed_core)
        other = lax.ppermute(value, axis, [(i, i ^ flip) for i in range(lax.axis_size(axis))])
        hop, other = lax.optimization_barrier((hop, other))
        small_sum["value"] = value + other
        return hop

    work = {}

    def with_rest(step, hop):
        if step == 1:
            grad_mix = mix_grads(normed, after(d_mix, d_normed_core), shards)
            hop, hops[:], grad_mix = lax.optimization_barrier((hop, hops, grad_mix))
            work["mix"] = scattered(grad_mix)
        else:
            while len(hops) < (layers if step == layers - 1 else step + 2):
                hops.append(line_hop(*hops[-1], len(hops)))
        if step == 2:
            done = finish(
                core_id, sum_feed, swapped(sum_feed), ((0, units), (units, units)),
                (2 * units, units),
            )
            hop, work["feed"], hops[:] = lax.optimization_barrier((hop, done, hops))
        if step == 3:
            hop, work["output"] = lax.optimization_barrier((hop, place(turns, flat(hops))))
        return advance(hop)

    d_normed = line_sum_hops(d_normed_core, with_rest)
    output = work["output"] if "output" in work else place(turns, flat(hops))
    d_tokens = norm_back(d_normed, tokens_own, norm_parts(tokens_own, 1e-6), gain_attn)
    grad_own = (d_middle + d_tokens).astype(BF16)
    back = [(grad_own, grad_own)]
    for step in range(1, layers):
        hop = line_hop(*back[-1], step)
        if step == 1:
            out_done = finish(core_id, sum_out, swapped(sum_out), (), (0, tall))
            hop, (g_out,) = lax.optimization_barrier((hop, out_done))
        back.append(advance(hop))
    while pairs:
        advance(())
    vector = small_sum["value"]
    g_attn = lax.dynamic_slice_in_dim(vector, shard * depth, depth, 0)
    g_mlp = lax.dynamic_slice_in_dim(vector, model + shard * depth, depth, 0)
    g_head = lax.dynamic_slice_in_dim(vector, 2 * model + shard * val_part, val_part, 0)
    mine_taps = vector[2 * model + val_dim :]
    local = jnp.stack([mine_taps, swapped(mine_taps)])
    table = jnp.where(core == 0, local, local[::-1])
    tap_table = table[:, : taps_count * width].reshape(2, taps_count, width)
    param_table = table[:, taps_count * width :].reshape(2, 2, 128)
    d_log, d_bias = param_table[:, 0, :heads].reshape(-1), param_table[:, 1, :heads].reshape(-1)

    def tap_grad(begin, size):
        array = tap_table[:, :, begin : begin + heads * size].reshape(2, taps_count, heads, size)
        part = lax.dynamic_slice_in_dim(array, shard * (size // shards), size // shards, 3)
        return jnp.transpose(part, (0, 2, 1, 3)).reshape(all_heads, taps_count, size // shards)

    d_conv_q, d_conv_k, d_conv_v = (
        tap_grad(0, key_dim), tap_grad(wide, key_dim), tap_grad(2 * wide, val_dim)
    )

    g_gate, g_up, g_down = work["feed"]
    input_grad = place(turns, flat(back))[None]
    low_mix, input_grad = lax.optimization_barrier((work["mix"], input_grad))
    other_mix = swapped(low_mix)
    g_query, g_key, g_value, g_outgate = finish(
        core_id, low_mix, other_mix,
        ((0, wide), (wide, wide), (2 * wide, tall), (side_at, tall)), None,
    )

    def narrow(begin):
        own, other = low_mix[:, begin : begin + heads], other_mix[:, begin : begin + heads]
        return jnp.where(
            core == 0, jnp.concatenate([own, other], 1), jnp.concatenate([other, own], 1)
        ).astype(F32)

    return (
        output[None],
        input_grad,
        g_attn,
        g_query,
        g_key,
        g_value,
        narrow(width),
        narrow(width + heads),
        d_log,
        d_bias,
        d_conv_q,
        d_conv_k,
        d_conv_v,
        g_outgate,
        g_head,
        g_out,
        g_mlp,
        g_gate,
        g_up,
        g_down,
    )


def solution(mesh):
    placed = (
        P("fsdp", "context", None),
        P("fsdp"),
        P("fsdp"),
        P("fsdp", "tensor"),
        P("fsdp", "tensor"),
        P("fsdp", "tensor"),
        P("fsdp", "tensor"),
        P("fsdp", "tensor"),
        P("tensor"),
        P("tensor"),
        P("tensor", None, "fsdp"),
        P("tensor", None, "fsdp"),
        P("tensor", None, "fsdp"),
        P("fsdp", "tensor"),
        P("fsdp"),
        P("tensor", "fsdp"),
        P("fsdp"),
        P("fsdp", "tensor"),
        P("fsdp", "tensor"),
        P("tensor", "fsdp"),
        P("fsdp", "context", None),
    )
    return jax.shard_map(
        on_device,
        mesh=mesh,
        in_specs=placed,
        out_specs=(placed[0], placed[0]) + placed[2:20],
        check_vma=False,
    )
```
